32 devices in a mesh: dp: 8 (over y, x, core), mp: 4 (over z).
Axes of the slice: x: 2, y: 2, z: 4, core: 2. Of those that a mesh axis runs over, the one named last changes fastest.
Arguments:
- tokens: bfloat16 [2, 8, 1536, 1024], P(None, 'dp', 'mp'), may hold values from -6 to 6
- views: int32 [2, 8], P(None, 'dp'), may hold values from 1 to 3
- norm_gains: float32 [1, 2, 1024], replicated, may hold values from 0.25 to 1.75
- norm_biases: float32 [1, 2, 1024], replicated, may hold values from -1.8 to 1.8
- w_proj: bfloat16 [1, 3, 1024, 1024], P(None, None, 'dp', 'mp'), may hold values from -0.1875 to 0.1875
- w_out: bfloat16 [1, 1024, 1024], P(None, 'dp', 'mp'), may hold values from -3 to 3
- w_up: bfloat16 [1, 1024, 4096], P(None, 'dp', 'mp'), may hold values from -0.1875 to 0.1875
- w_down: bfloat16 [1, 1024, 4096], P(None, 'dp', 'mp'), may hold values from -0.09375 to 0.09375
- cotangent: bfloat16 [2, 8, 1536, 1024], P(None, 'dp', 'mp'), may hold values from -6 to 6
Outputs:
- output: bfloat16 [2, 8, 1536, 1024], P(None, 'dp', 'mp')
- grad_tokens: bfloat16 [2, 8, 1536, 1024], P(None, 'dp', 'mp')
- grad_proj: float32 [1, 3, 1024, 1024], P(None, None, 'dp', 'mp')
- grad_out: float32 [1, 1024, 1024], P(None, 'dp', 'mp')
- grad_up: float32 [1, 1024, 4096], P(None, 'dp', 'mp')
- grad_down: float32 [1, 1024, 4096], P(None, 'dp', 'mp')
- grad_gains: float32 [1, 2, 1024], P(None, None, ('dp', 'mp'))
- grad_biases: float32 [1, 1024], P(None, ('dp', 'mp'))
- grad_biases_second: float32 [1, 1024], P(None, ('dp', 'mp'))
The draws below stay inside these ranges and needn't reach their ends.
Inputs may be any that keep to these rules, and one draw needn't show every extreme that they name: Number of views of each scene; its live tokens are the first 768 + views * 256.
All inputs are finite; a program needn't handle non-finite values.
Results may differ from the reference program's by a relative error of at most 0.02.
Values may be sent and summed in bfloat16 or wider, within the bound.
No kernel may reach another device: no remote copies, remote signals or barrier semaphores. Data moves between devices by JAX's collectives and lax.ppermute only.
A program may use at most 192 MiB of HBM per device.

```python
import jax
import jax.numpy as jnp
from jax import lax

D = 1024
HEADS = 16
HDIM = 64
FF = 4096
VIEW_TOK = 256
TRI = 768
MAX_VIEWS = 3
LAYERS = 1
MICRO = 2
QBLOCK = 512
SEQ = 1536
SCENES = 8


def touch_ends(drawn, rng, least, top_value):
    dims = drawn.shape
    spot = [jax.random.randint(jax.random.fold_in(rng, axis), (), 0, dims[axis]) for axis in range(len(dims))]
    drawn = drawn.at[tuple(spot)].set(least)
    longest = dims.index(max(dims))
    spot[longest] = (spot[longest] + 1) % dims[longest]
    return drawn.at[tuple(spot)].set(top_value)


def block_scale(own_key, dims, split, least, top_value):
    factor_of, own = 1.0, jax.random.fold_in(own_key, 6)
    for position, shards_of in split:
        heights = jnp.exp(jax.random.uniform(jax.random.fold_in(own, position), (shards_of,), jnp.float32, least / len(split), top_value / len(split)))
        factor_of = factor_of * jnp.repeat(heights, dims[position] // shards_of).reshape([-1 if axis == position else 1 for axis in range(len(dims))])
    return factor_of


def bell_draw(rng, extent, width, most, pieces=(), held_as=jnp.bfloat16):
    values = jax.random.normal(rng, extent, jnp.float32) * width
    if len(pieces) > 0:
        values = block_scale(rng, extent, pieces, -0.22, 0.18) * values
    return jnp.clip(values, min=-most, max=most).astype(held_as)


def setup_inputs(seed: int = 0) -> dict:
    splits = jax.random.split(jax.random.key(seed), 10)
    tokens = bell_draw(splits[0], (MICRO, SCENES, SEQ, D), 1.0, 6.0, ((1, 8), (2, 4)))
    views = touch_ends(jax.random.randint(splits[1], (MICRO, SCENES), 1, MAX_VIEWS + 1), jax.random.fold_in(splits[1], 1), 1, MAX_VIEWS).astype(jnp.int32)
    norm_gains = jnp.clip(1.0 + 0.15 * jax.random.normal(splits[2], (LAYERS, 2, D), jnp.float32), 0.25, 1.75)
    norm_biases = bell_draw(splits[3], (LAYERS, 2, D), 0.3, 1.8, (), jnp.float32)
    w_proj = bell_draw(splits[4], (LAYERS, 3, D, D), D ** -0.5, 0.1875, ((2, 8), (3, 4)))
    w_out = bell_draw(splits[5], (LAYERS, D, D), (max(D // 256, 1)) ** -0.5, 3.0, ((1, 8), (2, 4)))
    w_up = bell_draw(splits[6], (LAYERS, D, FF), D ** -0.5, 0.1875, ((1, 8), (2, 4)))
    w_down = bell_draw(splits[7], (LAYERS, D, FF), FF ** -0.5, 0.09375, ((1, 8), (2, 4)))
    cotangent = bell_draw(splits[8], (MICRO, SCENES, SEQ, D), 1.0, 6.0, ((1, 8), (2, 4)))
    return dict(tokens=tokens, views=views, norm_gains=norm_gains, norm_biases=norm_biases, w_proj=w_proj, w_out=w_out, w_up=w_up, w_down=w_down, cotangent=cotangent)


@jax.custom_vjp
def low(v):
    return lax.optimization_barrier(v.astype(jnp.bfloat16)).astype(jnp.float32)

@jax.custom_vjp
def low_back(v):
    return v

def low_keep(v):
    return (low(v), None)

def low_pass(kept, grad):
    return (grad,)

def back_keep(v):
    return (v, None)

def back_low(kept, grad):
    return (low(grad),)
low.defvjp(low_keep, low_pass)
low_back.defvjp(back_keep, back_low)
EPSILON = 1e-05
MASKED = -1000000000.0
HIGHEST = lax.Precision.HIGHEST

def normalize(state, gain, bias):
    centre = lax.optimization_barrier(jnp.mean(state, axis=-1, keepdims=True))
    centred = state - centre
    spread = lax.optimization_barrier(jnp.mean(centred * centred, axis=-1, keepdims=True))
    return centred * lax.rsqrt(spread + EPSILON) * gain + bias

def attend(queries, keys, values, live):
    scale = HDIM ** (-0.5)

    def block(query_part):
        scores = jnp.einsum('qhd,khd->hqk', query_part, keys, precision=HIGHEST) * scale
        scores = low_back(scores)
        scores = jnp.where(live[None, None, :], scores, MASKED)
        probs = low(jax.nn.softmax(scores, axis=-1))
        return jnp.einsum('hqk,khd->qhd', probs, values, precision=HIGHEST)
    blocks = queries.reshape(SEQ // QBLOCK, QBLOCK, HEADS, HDIM)
    mixed = lax.map(jax.checkpoint(block), blocks)
    return mixed.reshape(SEQ, D)

def layer(state, live, gains, biases, w_proj, w_out, w_up, w_down):
    normed = low(normalize(state, gains[0], biases[0]))
    projected = low(low_back(jnp.einsum('sd,ide->ise', normed, w_proj, precision=HIGHEST)))
    heads = projected.reshape(3, SEQ, HEADS, HDIM)
    mixed = low(low_back(attend(heads[0], heads[1], heads[2], live)))
    branch = low_back(jnp.dot(mixed, w_out.T, precision=HIGHEST))
    middle = state + branch
    normed = low(normalize(middle, gains[1], biases[1]))
    hidden_pre = low_back(jnp.dot(normed, w_up, precision=HIGHEST))
    activation = low(jax.nn.gelu(hidden_pre, approximate=False))
    branch = low_back(jnp.dot(activation, w_down.T, precision=HIGHEST))
    return middle + branch

def reference(tokens, views, norm_gains, norm_biases, w_proj, w_out, w_up, w_down, cotangent):
    weights = tuple((t.astype(jnp.float32) for t in (norm_gains, norm_biases, w_proj, w_out, w_up, w_down)))
    inputs = tokens.reshape(MICRO * SCENES, SEQ, D).astype(jnp.float32)
    pullbacks = cotangent.reshape(MICRO * SCENES, SEQ, D).astype(jnp.float32)
    counts = views.reshape(MICRO * SCENES).astype(jnp.int32)
    positions = jnp.arange(SEQ, dtype=jnp.int32)

    def scene(totals, item):
        start_state, pullback, count = item
        live = positions < TRI + count * VIEW_TOK

        def forward(state, gains, biases, proj, outs, ups, downs):
            for index in range(LAYERS):
                state = layer(state, live, gains[index], biases[index], proj[index], outs[index], ups[index], downs[index])
            return state
        result, pull = jax.vjp(forward, start_state, *weights)
        grads = pull(pullback)
        totals = tuple((total + grad for total, grad in zip(totals, grads[1:])))
        return (totals, (result.astype(jnp.bfloat16), grads[0].astype(jnp.bfloat16)))
    zeros = tuple((jnp.zeros(w.shape, jnp.float32) for w in weights))
    totals, (results, grad_inputs) = lax.scan(scene, zeros, (inputs, pullbacks, counts))
    return (results.reshape(tokens.shape), grad_inputs.reshape(tokens.shape), totals[2], totals[3], totals[4], totals[5], totals[0], totals[1][:, 0], totals[1][:, 1])
```

```python
import functools

import jax
import jax.numpy as jnp
from jax import lax
from jax.experimental import pallas as pl
from jax.experimental.pallas import tpu as pltpu
from jax.sharding import PartitionSpec as P

HDIM = 64
VIEW_TOK = 256
TRI = 768
EPSILON = 1e-05
MASKED = -1000000000.0
F32 = jnp.float32
BF16 = jnp.bfloat16
MIB = 1024 * 1024


def params(mib, *semantics):
    return pltpu.CompilerParams(
        vmem_limit_bytes=mib * MIB,
        dimension_semantics=semantics if semantics else None,
    )


def swap(value, bit, size):
    return lax.ppermute(value, "dp", [(i, i ^ bit) for i in range(size)])


def ring(value, step, size):
    return lax.ppermute(value, "mp", [(i, (i + step) % size) for i in range(size)])


def gather_pieces(shard, order, nd, nm):
    column, current = [shard], shard
    for _ in range(nm - 1):
        current = ring(current, 1, nm)
        column.append(current)
    pieces = {0: jnp.stack(column)}
    for bit in order:
        for j in list(pieces):
            pieces[j | bit] = swap(pieces[j], bit, nd)
    return [pieces[j] for j in range(nd)]


def scatter_pieces(pieces, order, nd, nm):
    pieces = dict(enumerate(pieces))
    for bit in order:
        for j in list(pieces):
            if j & bit:
                came = swap(pieces.pop(j), bit, nd)
                kept = pieces[j ^ bit]
                pieces[j ^ bit] = (kept.astype(F32) + came.astype(F32)).astype(BF16)
    own = pieces[0]
    current = own[nm - 1]
    for k in range(nm - 2, -1, -1):
        came = ring(current, -1, nm)
        total = own[k].astype(F32) + came.astype(F32)
        current = total.astype(BF16) if k else total
    return current


def assemble_kernel(nd, nm, place_ref, *refs):
    pieces, out_ref, sems = refs[:nd], refs[nd], refs[nd + 1]
    rows, cols = pieces[0].shape[-2:]
    copies = []
    for j in range(nd):
        row = place_ref[0] ^ j
        for k in range(nm):
            col = lax.rem(place_ref[1] + nm - k, nm)
            dst = out_ref.at[
                :,
                pl.ds(pl.multiple_of(row * rows, rows), rows),
                pl.ds(pl.multiple_of(col * cols, cols), cols),
            ]
            copies.append(pltpu.make_async_copy(pieces[j].at[k], dst, sems.at[j * nm + k]))
    for copy in copies:
        copy.start()
    for copy in copies:
        copy.wait()


def assemble(pieces, place, nd, nm):
    _, lead, rows, cols = pieces[0].shape
    return pl.pallas_call(
        functools.partial(assemble_kernel, nd, nm),
        out_shape=jax.ShapeDtypeStruct((lead, nd * rows, nm * cols), BF16),
        in_specs=[pl.BlockSpec(memory_space=pltpu.SMEM)]
        + [pl.BlockSpec(memory_space=pl.ANY)] * nd,
        out_specs=pl.BlockSpec(memory_space=pltpu.VMEM),
        compiler_params=params(32),
        scratch_shapes=[pltpu.SemaphoreType.DMA((nd * nm,))],
        name="assemble",
    )(place, *pieces)


def split_kernel(nd, nm, place_ref, in_ref, *refs):
    pieces, sems = refs[:nd], refs[nd]
    rows, cols = pieces[0].shape[-2:]
    copies = []
    for j in range(nd):
        row = place_ref[0] ^ j
        for k in range(nm):
            col = lax.rem(place_ref[1] + nm - k, nm)
            src = in_ref.at[
                :,
                pl.ds(pl.multiple_of(row * rows, rows), rows),
                pl.ds(pl.multiple_of(col * cols, cols), cols),
            ]
            copies.append(pltpu.make_async_copy(src, pieces[j].at[k], sems.at[j * nm + k]))
    for copy in copies:
        copy.start()
    for copy in copies:
        copy.wait()


def split(full, place, nd, nm):
    lead, rows, cols = full.shape
    piece = jax.ShapeDtypeStruct((nm, lead, rows // nd, cols // nm), BF16)
    return pl.pallas_call(
        functools.partial(split_kernel, nd, nm),
        out_shape=[piece] * nd,
        in_specs=[pl.BlockSpec(memory_space=pltpu.SMEM), pl.BlockSpec(memory_space=pltpu.VMEM)],
        compiler_params=params(32),
        out_specs=[pl.BlockSpec(memory_space=pl.ANY)] * nd,
        scratch_shapes=[pltpu.SemaphoreType.DMA((nd * nm,))],
        name="split",
    )(place, full)


def dot_nt(a, b):
    return lax.dot_general(a, b, (((1,), (1,)), ((), ())), preferred_element_type=F32)


def dot_nn(a, b):
    return lax.dot_general(a, b, (((1,), (0,)), ((), ())), preferred_element_type=F32)


def dot_tn(a, b):
    return lax.dot_general(a, b, (((0,), (0,)), ((), ())), preferred_element_type=F32)


def attend_kernel(q_ref, k_ref, v_ref, bias_ref, out_ref, lse_ref):
    rows = q_ref.shape[1]
    low = lax.broadcasted_iota(jnp.int32, (1, 2 * HDIM), 1) < HDIM
    query = q_ref[0] * jnp.asarray(HDIM ** (-0.5), BF16)
    keys, values = k_ref[0], v_ref[0]
    bias = bias_ref[...]
    mixed = None
    for head in range(2):
        mine = low if head == 0 else jnp.logical_not(low)
        scores = dot_nt(jnp.where(mine, query, jnp.zeros_like(query)), keys)
        scores = jnp.where(bias < 0.0, MASKED, scores)
        top = jnp.max(scores, axis=1, keepdims=True)
        expo = jnp.exp(scores - top)
        total = jnp.sum(expo, axis=1, keepdims=True)
        part = dot_nn(expo.astype(BF16), values) / total
        mixed = part if head == 0 else jnp.where(low, mixed, part)
        lse = top + jnp.log(total)
        lse_ref[0, head : head + 1, :] = jnp.transpose(jnp.broadcast_to(lse, (rows, 128)))[0:1, :]
    out_ref[...] = mixed.astype(BF16)


def attend(qkv, keys_values, bias, block=256):
    _, rows, width = qkv.shape
    keys = keys_values.shape[1]
    pairs = width // (2 * HDIM)
    return pl.pallas_call(
        attend_kernel,
        grid=(pairs, rows // block),
        in_specs=[
            pl.BlockSpec((1, block, 2 * HDIM), lambda h, i: (0, i, h)),
            pl.BlockSpec((1, keys, 2 * HDIM), lambda h, i: (0, 0, h)),
            pl.BlockSpec((1, keys, 2 * HDIM), lambda h, i: (1, 0, h)),
            pl.BlockSpec((1, keys), lambda h, i: (0, 0)),
        ],
        out_specs=[
            pl.BlockSpec((block, 2 * HDIM), lambda h, i: (i, h)),
            pl.BlockSpec((1, 2, block), lambda h, i: (h, 0, i)),
        ],
        out_shape=[
            jax.ShapeDtypeStruct((rows, width), BF16),
            jax.ShapeDtypeStruct((pairs, 2, rows), F32),
        ],
        compiler_params=params(48),
        cost_estimate=pl.CostEstimate(
            flops=16 * rows * keys * width, bytes_accessed=8 * keys * width, transcendentals=0
        ),
        name="attend",
    )(qkv, keys_values, keys_values, bias)


def attend_back_kernel(
    q_ref, k_ref, v_ref, bias_ref, lse_ref, mixed_ref, grad_ref, dq_ref, dkv_ref, dk_acc, dv_acc
):
    step = pl.program_id(1)
    low = lax.broadcasted_iota(jnp.int32, (1, 2 * HDIM), 1) < HDIM
    scale = jnp.asarray(HDIM ** (-0.5), BF16)
    query = q_ref[0] * scale
    grad = grad_ref[...]
    keys, values = k_ref[0], v_ref[0]
    bias = bias_ref[...]
    product = mixed_ref[...].astype(F32) * grad.astype(F32)
    grad_query = None
    new_key, new_value = None, None
    for head in range(2):
        mine = low if head == 0 else jnp.logical_not(low)
        q_mine = jnp.where(mine, query, jnp.zeros_like(query))
        g_mine = jnp.where(mine, grad, jnp.zeros_like(grad))
        delta = jnp.sum(jnp.where(mine, product, 0.0), axis=1, keepdims=True)
        delta = jnp.transpose(jnp.broadcast_to(delta, (delta.shape[0], 128)))[0:1, :]
        scores = dot_nt(keys, q_mine)
        scores = jnp.where(bias < 0.0, MASKED, scores)
        probs = jnp.exp(scores - lse_ref[0, head : head + 1, :])
        upstream = dot_nt(values, g_mine)
        grad_scores = (probs * (upstream - delta)).astype(BF16)
        value_part = dot_nn(probs.astype(BF16), g_mine)
        key_part = dot_nn(grad_scores, q_mine)
        query_part = dot_tn(grad_scores, keys)
        if head == 0:
            new_key, new_value, grad_query = key_part, value_part, query_part
        else:
            new_key, new_value = new_key + key_part, new_value + value_part
            grad_query = jnp.where(low, grad_query, query_part)
    dq_ref[...] = (grad_query * HDIM ** (-0.5)).astype(BF16)

    @pl.when(step == 0)
    def _():
        dk_acc[...] = new_key
        dv_acc[...] = new_value

    @pl.when(step > 0)
    def _():
        dk_acc[...] += new_key
        dv_acc[...] += new_value

    @pl.when(step == pl.num_programs(1) - 1)
    def _():
        dkv_ref[0] = dk_acc[...].astype(BF16)
        dkv_ref[1] = dv_acc[...].astype(BF16)


def attend_back(qkv, keys_values, bias, lse, mixed, grad_mixed, block=256):
    _, rows, width = qkv.shape
    keys = keys_values.shape[1]
    pairs = width // (2 * HDIM)
    return pl.pallas_call(
        attend_back_kernel,
        grid=(pairs, rows // block),
        in_specs=[
            pl.BlockSpec((1, block, 2 * HDIM), lambda h, i: (0, i, h)),
            pl.BlockSpec((1, keys, 2 * HDIM), lambda h, i: (0, 0, h)),
            pl.BlockSpec((1, keys, 2 * HDIM), lambda h, i: (1, 0, h)),
            pl.BlockSpec((keys, 1), lambda h, i: (0, 0)),
            pl.BlockSpec((1, 2, block), lambda h, i: (h, 0, i)),
            pl.BlockSpec((block, 2 * HDIM), lambda h, i: (i, h)),
            pl.BlockSpec((block, 2 * HDIM), lambda h, i: (i, h)),
        ],
        out_specs=[
            pl.BlockSpec((block, 2 * HDIM), lambda h, i: (i, h)),
            pl.BlockSpec((2, keys, 2 * HDIM), lambda h, i: (0, 0, h)),
        ],
        out_shape=[
            jax.ShapeDtypeStruct((rows, width), BF16),
            jax.ShapeDtypeStruct((2, keys, width), BF16),
        ],
        scratch_shapes=[pltpu.VMEM((keys, 2 * HDIM), F32), pltpu.VMEM((keys, 2 * HDIM), F32)],
        compiler_params=params(48),
        cost_estimate=pl.CostEstimate(
            flops=40 * rows * keys * width, bytes_accessed=16 * keys * width, transcendentals=0
        ),
        name="attend_back",
    )(qkv, keys_values, keys_values, bias, lse, mixed, grad_mixed)


def normalize(state, gain, bias):
    centre = jnp.mean(state, axis=-1, keepdims=True)
    centred = state - centre
    spread = jnp.mean(centred * centred, axis=-1, keepdims=True)
    inverse = lax.rsqrt(spread + EPSILON)
    scaled = centred * inverse
    return (scaled * gain + bias, scaled, inverse)


def normalize_back(grad, scaled, inverse, gain):
    weighted = grad * gain
    first = jnp.mean(weighted, axis=-1, keepdims=True)
    second = jnp.mean(weighted * scaled, axis=-1, keepdims=True)
    return (
        inverse * (weighted - first - scaled * second),
        jnp.sum(grad * scaled, axis=0),
        jnp.sum(grad, axis=0),
    )


def gelu_exact(values):
    return jax.nn.gelu(values, approximate=False)


def shards(nd, nm, tokens, views, norm_gains, norm_biases, w_proj, w_out, w_up, w_down, cotangent):
    micro, _, chunk, width = tokens.shape
    ranks = nm // micro
    half = max(ranks // 2, 1)
    rows = micro * chunk
    dp, mp = lax.axis_index("dp"), lax.axis_index("mp")
    core = dp & 1
    place = jnp.stack([dp, mp]).astype(jnp.int32)
    gains, biases = norm_gains[0], norm_biases[0]
    orders = [[1 << b for b in range(1, nd.bit_length() - 1)]]
    orders.append(orders[0][::-1])
    orders = [order + [1] for order in orders]
    group = mp // half
    step_here = group // 2
    rank = core + 2 * (mp % half)

    def routes(k):
        pairs = []
        for d in range(nd):
            for z in range(nm):
                m = (k + z) % micro
                r = z // micro
                to_d = (d & ~1) | (r & 1)
                to_z = (2 * m + (d & 1)) * half + r // 2
                pairs.append((d * nm + z, to_d * nm + to_z))
        return pairs

    def bring(value):
        came = [
            lax.ppermute(
                lax.dynamic_index_in_dim(value, (k + mp) % micro, 0, keepdims=False),
                ("dp", "mp"),
                routes(k),
            )
            for k in range(micro)
        ]
        came = jnp.stack(came)
        slots = [
            lax.dynamic_index_in_dim(came, (step_here - s) % micro, 0, keepdims=False)
            for s in range(micro)
        ]
        return jnp.concatenate(slots, axis=0)

    def send_back(value):
        slots = value.reshape((micro, chunk) + value.shape[1:])
        back = jnp.stack(
            [
                lax.ppermute(
                    lax.dynamic_index_in_dim(slots, (step_here - k) % micro, 0, keepdims=False),
                    ("dp", "mp"),
                    [(b, a) for a, b in routes(k)],
                )
                for k in range(micro)
            ]
        )
        return jnp.stack(
            [
                lax.dynamic_index_in_dim(back, (m - mp) % micro, 0, keepdims=False)
                for m in range(micro)
            ]
        )

    state = bring(tokens[:, 0]).astype(F32)
    count = lax.ppermute(
        lax.dynamic_index_in_dim(views[:, 0], mp % micro, 0, keepdims=True), ("dp", "mp"), routes(0)
    )[0]

    gather = functools.partial(gather_pieces, nd=nd, nm=nm)
    wq_out = gather(jnp.stack([w_proj[0, 0], w_out[0]]), orders[0])
    wk_v = gather(w_proj[0, 1:], orders[1])
    up_pieces = gather(w_up, orders[0])
    down_pieces = gather(w_down, orders[1])
    full_a = assemble(wq_out, place, nd, nm)
    full_b = assemble(wk_v, place, nd, nm)
    wq, wo = full_a[0], full_a[1]
    upw = assemble(up_pieces, place, nd, nm)[0]
    dnw = assemble(down_pieces, place, nd, nm)[0]
    grad_state = bring(cotangent[:, 0])

    normed, scaled_one, inverse_one = normalize(state, gains[0], biases[0])
    normed = normed.astype(BF16)
    query = jnp.dot(normed, wq, preferred_element_type=F32).astype(BF16)
    kv = jnp.einsum("sd,ide->ise", normed, full_b, preferred_element_type=F32).astype(BF16)
    qkv = query[None]
    pieces = {0: kv}
    bits = [1 << b for b in range(ranks.bit_length() - 1)]

    def swap_rank(value, bit):
        if bit == 1:
            return swap(value, 1, nd)
        return lax.ppermute(value, "mp", [(i, i ^ (bit >> 1)) for i in range(nm)])

    for bit in bits:
        for j in list(pieces):
            pieces[j | bit] = swap_rank(pieces[j], bit)
    all_kv = jnp.concatenate([pieces[j] for j in range(ranks)], axis=1)
    position = jnp.concatenate(
        [(rank ^ j) * rows + jnp.arange(rows, dtype=jnp.int32) for j in range(ranks)]
    )
    bias = jnp.where(position < TRI + count * VIEW_TOK, 0.0, -1.0).astype(F32)
    mixed, lse = attend(qkv, all_kv, bias[None, :])
    middle = state + dot_nt(mixed, wo)

    normed_two, scaled_two, inverse_two = normalize(middle, gains[1], biases[1])
    normed_two = normed_two.astype(BF16)
    hidden_pre = jnp.dot(normed_two, upw, preferred_element_type=F32)
    activation, pull = jax.vjp(gelu_exact, hidden_pre)
    activation = activation.astype(BF16)
    result = middle + dot_nt(activation, dnw)
    output = send_back(result.astype(BF16))

    give = functools.partial(scatter_pieces, nd=nd, nm=nm)
    back_orders = [[1] + order[:-1][::-1] for order in orders]
    grad_down = dot_tn(grad_state, activation).astype(BF16)
    g_down = give(split(grad_down[None], place, nd, nm), back_orders[1])
    grad_hidden = pull(jnp.dot(grad_state, dnw, preferred_element_type=F32))[0].astype(BF16)
    grad_up = dot_tn(normed_two, grad_hidden).astype(BF16)
    g_up = give(split(grad_up[None], place, nd, nm), back_orders[0])
    grad_normed_two = dot_nt(grad_hidden, upw)
    grad_norm_two, gain_two, bias_two = normalize_back(
        grad_normed_two, scaled_two, inverse_two, gains[1]
    )
    grad_middle = grad_state.astype(F32) + grad_norm_two
    grad_attn = grad_middle.astype(BF16)

    grad_out = dot_tn(grad_attn, mixed).astype(BF16)
    grad_mixed = jnp.dot(grad_attn, wo, preferred_element_type=F32).astype(BF16)
    grad_query, grad_kv = attend_back(qkv, all_kv, bias[:, None], lse, mixed, grad_mixed)
    parts = {j: grad_kv[:, j * rows : (j + 1) * rows] for j in range(ranks)}
    for bit in bits[::-1]:
        for j in list(parts):
            if j & bit:
                came = swap_rank(parts.pop(j), bit)
                parts[j ^ bit] = (parts[j ^ bit].astype(F32) + came.astype(F32)).astype(BF16)
    grad_kv = parts[0]
    grad_q_w = dot_tn(normed, grad_query).astype(BF16)
    grad_kv_w = jnp.einsum("sd,ise->ide", normed, grad_kv, preferred_element_type=F32).astype(BF16)
    g_qo = give(split(jnp.stack([grad_q_w, grad_out]), place, nd, nm), back_orders[0])
    g_kv = give(split(grad_kv_w, place, nd, nm), back_orders[1])
    grad_normed = (
        dot_nt(grad_query, wq) + dot_nt(grad_kv[0], full_b[0]) + dot_nt(grad_kv[1], full_b[1])
    )
    grad_norm_one, gain_one, bias_one = normalize_back(
        grad_normed, scaled_one, inverse_one, gains[0]
    )
    grad_tokens = send_back((grad_middle + grad_norm_one).astype(BF16))

    def everywhere(value):
        bit = 1
        while bit < nd:
            value = value + swap(value, bit, nd)
            bit *= 2
        bit = 1
        while bit < nm:
            value = value + lax.ppermute(value, "mp", [(i, i ^ bit) for i in range(nm)])
            bit *= 2
        share = width // (nd * nm)
        return lax.dynamic_slice_in_dim(value, (dp * nm + mp) * share, share, 1)

    second = everywhere(jnp.stack([gain_two, bias_two]))
    first = everywhere(jnp.stack([gain_one, bias_one]))
    return (
        output[:, None],
        grad_tokens[:, None],
        jnp.concatenate([g_qo[:1], g_kv])[None],
        g_qo[1][None],
        g_up,
        g_down,
        jnp.stack([first[0], second[0]])[None],
        first[1][None],
        second[1][None],
    )


def solution(mesh):
    placed = (
        P(None, "dp", "mp", None),
        P(None, "dp"),
        P(),
        P(),
        P(None, None, "dp", "mp"),
        P(None, "dp", "mp"),
        P(None, "dp", "mp"),
        P(None, "dp", "mp"),
        P(None, "dp", "mp", None),
    )
    return jax.shard_map(
        functools.partial(shards, mesh.shape["dp"], mesh.shape["mp"]),
        mesh=mesh,
        in_specs=placed,
        out_specs=(
            P(None, "dp", "mp", None),
            P(None, "dp", "mp", None),
            P(None, None, "dp", "mp"),
            P(None, "dp", "mp"),
            P(None, "dp", "mp"),
            P(None, "dp", "mp"),
            P(None, None, ("dp", "mp")),
            P(None, ("dp", "mp")),
            P(None, ("dp", "mp")),
        ),
        check_vma=False,
    )
```

```python
import functools

import jax
import jax.numpy as jnp
from jax import lax
from jax.experimental import pallas as pl
from jax.experimental.pallas import tpu as pltpu
from jax.sharding import PartitionSpec as P

HDIM = 64
PAIR = 2 * HDIM
VIEW_TOK = 256
TRI = 768
EPSILON = 1e-05
MASKED = -1000000000.0
F32 = jnp.float32
BF16 = jnp.bfloat16
MIB = 1024 * 1024
ANY = pl.BlockSpec(memory_space=pl.ANY)
WHOLE = pl.BlockSpec(memory_space=pltpu.VMEM)
SHAPE = jax.ShapeDtypeStruct


def params(mib=56):
    return pltpu.CompilerParams(vmem_limit_bytes=mib * MIB)


def cost(flops, nbytes):
    return pl.CostEstimate(flops=int(flops), bytes_accessed=int(nbytes), transcendentals=0)


def dot_nt(a, b):
    return lax.dot_general(a, b, (((1,), (1,)), ((), ())), preferred_element_type=F32)


def dot_nn(a, b):
    return lax.dot_general(a, b, (((1,), (0,)), ((), ())), preferred_element_type=F32)


def dot_tn(a, b):
    return lax.dot_general(a, b, (((0,), (0,)), ((), ())), preferred_element_type=F32)


def row_block(rows):
    return 256 if rows % 256 == 0 else 128


def swap(value, bit, nd):
    return lax.ppermute(value, "dp", [(i, i ^ bit) for i in range(nd)])


def ring(value, step, nm):
    return lax.ppermute(value, "mp", [(i, (i + step) % nm) for i in range(nm)])


class Flow:
    def __init__(self, nd, nm):
        self.nd, self.nm = nd, nm
        self.bits = [1 << b for b in range(1, nd.bit_length() - 1)]
        self.queue = {bit: [] for bit in self.bits}
        self.order, self.pieces, self.flying, self.kept = {}, {}, {}, {}

    def add(self, name, value, order):
        self.order[name] = list(order)
        self.pieces[name] = [(0, value)]
        self.next(name)

    def next(self, name):
        if self.order[name]:
            self.queue[self.order[name][0]].append(name)

    def launch(self, chip=1):
        for bit, tasks in self.queue.items():
            for _ in range(chip):
                if tasks:
                    name = tasks.pop(0)
                    values = [value for _, value in self.pieces[name]]
                    value = values[0][None] if len(values) == 1 else jnp.stack(values)
                    self.flying["chip", name] = swap(value, bit, self.nd)

    def fly(self, name, value):
        self.flying["kept", name] = value

    def land(self, *extra):
        names, flying, kept = list(self.pieces), list(self.flying), list(self.kept)
        values = lax.optimization_barrier(
            (
                [self.pieces[name] for name in names],
                [self.flying[key] for key in flying],
                [self.kept[key] for key in kept],
                extra,
            )
        )
        for name, pieces in zip(names, values[0]):
            self.pieces[name] = [(j, v) for (j, _), (_, v) in zip(self.pieces[name], pieces)]
        self.kept = dict(zip(kept, values[2]))
        self.flying = {}
        for (kind, name), value in zip(flying, values[1]):
            if kind == "kept":
                self.kept[name] = value
                continue
            bit = self.order[name].pop(0)
            held = self.pieces[name]
            self.pieces[name] = held + [(j | bit, value[n]) for n, (j, _) in enumerate(held)]
            self.next(name)
        extra = values[3]
        return extra[0] if len(extra) == 1 else extra

    def whole(self, name):
        return name in self.pieces and not self.order[name]

    def take_half(self, name):
        pieces = dict(self.pieces.pop(name))
        return jnp.stack([pieces[2 * i] for i in range(self.nd // 2)])


def pack_kernel(index_ref, in_ref, out_ref):
    nd = index_ref.shape[0] - 1
    wide = in_ref.shape[2] // nd
    for p in range(nd):
        there = pl.ds(pl.multiple_of(index_ref[p] * wide, wide), wide)
        out_ref[:, p * wide : (p + 1) * wide] = in_ref[index_ref[nd], :, there]


def pack_features(value, index, which):
    micro, rows, width = value.shape
    nd = index.shape[0]
    if width // nd % 128:
        chunk = lax.dynamic_index_in_dim(value, which, 0, keepdims=False)
        return jnp.take(chunk.reshape(rows, nd, -1), index, axis=1).reshape(rows, width)
    return pl.pallas_call(
        pack_kernel,
        in_specs=[pl.BlockSpec(memory_space=pltpu.SMEM), WHOLE],
        out_specs=WHOLE,
        out_shape=SHAPE((rows, width), value.dtype),
        compiler_params=params(),
        cost_estimate=cost(0, 6 * rows * width),
        name="pack_features",
    )(jnp.append(index, which.astype(jnp.int32)), value)


def unpack_kernel(index_ref, *refs):
    ins, out_ref = refs[:-1], refs[-1]
    nd = index_ref.shape[0] - len(ins)
    wide = out_ref.shape[2] // nd
    for k, in_ref in enumerate(ins):
        for p in range(nd):
            there = pl.ds(pl.multiple_of(index_ref[p] * wide, wide), wide)
            out_ref[index_ref[nd + k], :, there] = in_ref[:, p * wide : (p + 1) * wide]


def unpack_features(chunks, index, places):
    rows, width = chunks[0].shape
    micro, nd = len(chunks), index.shape[0]
    places = [place.astype(jnp.int32) for place in places]
    if width // nd % 128:
        back = jnp.argsort(index)
        stacked = jnp.stack(chunks).reshape(micro, rows, nd, -1)
        stacked = jnp.take(stacked, back, axis=2).reshape(micro, rows, width)
        return jnp.take(stacked, jnp.argsort(jnp.stack(places)), axis=0)
    return pl.pallas_call(
        unpack_kernel,
        in_specs=[pl.BlockSpec(memory_space=pltpu.SMEM)] + [WHOLE] * micro,
        out_specs=WHOLE,
        out_shape=SHAPE((micro, rows, width), chunks[0].dtype),
        compiler_params=params(),
        cost_estimate=cost(0, 4 * micro * rows * width),
        name="unpack_features",
    )(jnp.concatenate([index, jnp.stack(places)]), *chunks)


def standardize(state):
    centre = jnp.mean(state, axis=-1, keepdims=True)
    centred = state - centre
    spread = jnp.mean(centred * centred, axis=-1, keepdims=True)
    inverse = lax.rsqrt(spread + EPSILON)
    return centred * inverse, inverse


def norm_back(grad, state, gain):
    scaled, inverse = standardize(state)
    weighted = grad * gain
    first = jnp.mean(weighted, axis=-1, keepdims=True)
    second = jnp.mean(weighted * scaled, axis=-1, keepdims=True)
    sums = jnp.concatenate(
        [jnp.sum(grad * scaled, axis=0, keepdims=True), jnp.sum(grad, axis=0, keepdims=True)], 0
    )
    return inverse * (weighted - first - scaled * second), sums


def first_norm_kernel(micro, *refs):
    chunks = refs[:micro]
    gain_ref, bias_ref, x_ref, out_ref, flip_ref = refs[micro:]
    rows = chunks[0].shape[0]
    for k, ref in enumerate(chunks):
        here = slice(k * rows, (k + 1) * rows)
        x_ref[here] = ref[...]
        scaled, _ = standardize(ref[...].astype(F32))
        normed = (scaled * gain_ref[...] + bias_ref[...]).astype(BF16)
        out_ref[here] = normed
        flip_ref[:, here] = normed.T


def first_norm(chunks, gain, bias):
    rows, width = chunks[0].shape
    rows = rows * len(chunks)
    return pl.pallas_call(
        functools.partial(first_norm_kernel, len(chunks)),
        in_specs=[WHOLE] * (len(chunks) + 2),
        out_specs=[WHOLE] * 3,
        out_shape=[SHAPE((rows, width), BF16)] * 2 + [SHAPE((width, rows), BF16)],
        compiler_params=params(),
        cost_estimate=cost(0, 10 * rows * width),
        name="first_norm",
    )(*chunks, gain, bias)


def flip_kernel(*refs):
    chunks, out_ref, flip_ref = refs[:-2], refs[-2], refs[-1]
    rows = chunks[0].shape[0]
    for k, ref in enumerate(chunks):
        here = slice(k * rows, (k + 1) * rows)
        out_ref[here] = ref[...]
        flip_ref[:, here] = ref[...].T


def flip(chunks):
    rows, width = chunks[0].shape
    rows = rows * len(chunks)
    return pl.pallas_call(
        flip_kernel,
        in_specs=[WHOLE] * len(chunks),
        out_specs=[WHOLE] * 2,
        out_shape=[SHAPE((rows, width), BF16), SHAPE((width, rows), BF16)],
        compiler_params=params(),
        cost_estimate=cost(0, 6 * rows * width),
        name="flip",
    )(*chunks)


def proj_kernel(in_ref, own_ref, other_ref, out_ref):
    value = in_ref[...]
    half = value.shape[1] // 2
    wide = own_ref.shape[-1]
    for k in range(own_ref.shape[1]):
        first = own_ref[:, k, 0].reshape(half, wide)
        second = other_ref[:, k, 0].reshape(half, wide)
        total = dot_nn(value[:, :half], first) + dot_nn(value[:, half:], second)
        out_ref[0, :, k * wide : (k + 1) * wide] = total.astype(BF16)


def project(value, own, other, start, count):
    rows, width = value.shape
    chips, nm, _, deep, wide = own.shape
    spec = pl.BlockSpec((chips, nm, 1, deep, wide), lambda i: (0, 0, start + i, 0, 0))
    return pl.pallas_call(
        proj_kernel,
        grid=(count,),
        in_specs=[pl.BlockSpec((rows, width), lambda i: (0, 0)), spec, spec],
        out_specs=pl.BlockSpec((1, rows, nm * wide), lambda i: (i, 0, 0)),
        out_shape=SHAPE((count, rows, nm * wide), BF16),
        compiler_params=params(),
        cost_estimate=cost(2 * count * rows * width * nm * wide, 2 * count * rows * width),
        name="project",
    )(value, own, other)


def attend_kernel(parts, q_ref, *refs):
    k_refs, v_refs = refs[:parts], refs[parts : 2 * parts]
    bias_ref, out_ref, lse_ref = refs[2 * parts :]
    rows = q_ref.shape[1]
    low = lax.broadcasted_iota(jnp.int32, (1, PAIR), 1) < HDIM
    query = q_ref[0] * jnp.asarray(HDIM ** (-0.5), BF16)
    mixed = None
    for head in range(2):
        mine = low if head == 0 else jnp.logical_not(low)
        q_mine = jnp.where(mine, query, jnp.zeros_like(query))
        scores = [
            jnp.where(bias_ref[p : p + 1, :] < 0.0, MASKED, dot_nt(q_mine, k_refs[p][0]))
            for p in range(parts)
        ]
        top = functools.reduce(
            jnp.maximum, [jnp.max(part, axis=1, keepdims=True) for part in scores]
        )
        total, part = 0.0, 0.0
        for p in range(parts):
            expo = jnp.exp(scores[p] - top)
            total = total + jnp.sum(expo, axis=1, keepdims=True)
            part = part + dot_nn(expo.astype(BF16), v_refs[p][0])
        part = part / total
        mixed = part if head == 0 else jnp.where(low, mixed, part)
        lse = top + jnp.log(total)
        lse_ref[0, head : head + 1, :] = jnp.transpose(jnp.broadcast_to(lse, (rows, 128)))[0:1, :]
    out_ref[...] = mixed.astype(BF16)


def attend(query, kvs, bias, start, count):
    _, rows, width = query.shape
    parts = len(kvs)
    block = row_block(rows)
    keys = rows * parts
    key_spec = pl.BlockSpec((1, rows, PAIR), lambda h, i: (0, 0, start + h))
    value_spec = pl.BlockSpec((1, rows, PAIR), lambda h, i: (1, 0, start + h))
    return pl.pallas_call(
        functools.partial(attend_kernel, parts),
        grid=(count, rows // block),
        in_specs=[pl.BlockSpec((1, block, PAIR), lambda h, i: (0, i, start + h))]
        + [key_spec] * parts
        + [value_spec] * parts
        + [pl.BlockSpec((parts, rows), lambda h, i: (0, 0))],
        out_specs=[
            pl.BlockSpec((block, PAIR), lambda h, i: (i, h)),
            pl.BlockSpec((1, 2, block), lambda h, i: (h, 0, i)),
        ],
        out_shape=[SHAPE((rows, count * PAIR), BF16), SHAPE((count, 2, rows), F32)],
        compiler_params=params(),
        cost_estimate=cost(16 * rows * keys * count * PAIR, 8 * keys * count * PAIR),
        name="attend",
    )(query, *kvs, *kvs, bias)


def attend_back_kernel(parts, q_ref, *refs):
    k_refs, v_refs = refs[:parts], refs[parts : 2 * parts]
    bias_ref, lse_ref, mixed_ref, grad_ref, dq_ref = refs[2 * parts : 2 * parts + 5]
    dkv_refs = refs[2 * parts + 5 : 3 * parts + 5]
    dk_acc, dv_acc = refs[3 * parts + 5 :]
    step = pl.program_id(1)
    low = lax.broadcasted_iota(jnp.int32, (1, PAIR), 1) < HDIM
    query = q_ref[0] * jnp.asarray(HDIM ** (-0.5), BF16)
    grad = grad_ref[0]
    product = mixed_ref[...].astype(F32) * grad.astype(F32)

    @pl.when(step == 0)
    def _():
        dk_acc[...] = jnp.zeros_like(dk_acc)
        dv_acc[...] = jnp.zeros_like(dv_acc)

    grad_query = None
    for head in range(2):
        mine = low if head == 0 else jnp.logical_not(low)
        q_mine = jnp.where(mine, query, jnp.zeros_like(query))
        g_mine = jnp.where(mine, grad, jnp.zeros_like(grad))
        delta = jnp.sum(jnp.where(mine, product, 0.0), axis=1, keepdims=True)
        delta = jnp.transpose(jnp.broadcast_to(delta, (delta.shape[0], 128)))[0:1, :]
        query_part = 0.0
        for p in range(parts):
            keys, values = k_refs[p][0], v_refs[p][0]
            scores = jnp.where(bias_ref[p] < 0.0, MASKED, dot_nt(keys, q_mine))
            probs = jnp.exp(scores - lse_ref[0, head : head + 1, :])
            upstream = dot_nt(values, g_mine)
            grad_scores = (probs * (upstream - delta)).astype(BF16)
            dv_acc[p] += dot_nn(probs.astype(BF16), g_mine)
            dk_acc[p] += dot_nn(grad_scores, q_mine)
            query_part = query_part + dot_tn(grad_scores, keys)
        grad_query = query_part if head == 0 else jnp.where(low, grad_query, query_part)
    dq_ref[...] = (grad_query * HDIM ** (-0.5)).astype(BF16)

    @pl.when(step == pl.num_programs(1) - 1)
    def _():
        for p in range(parts):
            dkv_refs[p][0] = dk_acc[p].astype(BF16)
            dkv_refs[p][1] = dv_acc[p].astype(BF16)


def attend_back(query, kvs, bias, lse, mixed, grad, start, count):
    _, rows, width = query.shape
    parts = len(kvs)
    block = row_block(rows)
    keys = rows * parts
    key_spec = pl.BlockSpec((1, rows, PAIR), lambda h, i: (0, 0, start + h))
    value_spec = pl.BlockSpec((1, rows, PAIR), lambda h, i: (1, 0, start + h))
    return pl.pallas_call(
        functools.partial(attend_back_kernel, parts),
        grid=(count, rows // block),
        in_specs=[pl.BlockSpec((1, block, PAIR), lambda h, i: (0, i, start + h))]
        + [key_spec] * parts
        + [value_spec] * parts
        + [
            pl.BlockSpec((parts, rows, 1), lambda h, i: (0, 0, 0)),
            pl.BlockSpec((1, 2, block), lambda h, i: (h, 0, i)),
            pl.BlockSpec((block, PAIR), lambda h, i: (i, h)),
            pl.BlockSpec((1, block, PAIR), lambda h, i: (0, i, start + h)),
        ],
        out_specs=[pl.BlockSpec((block, PAIR), lambda h, i: (i, h))]
        + [pl.BlockSpec((2, rows, PAIR), lambda h, i: (0, 0, h))] * parts,
        out_shape=[SHAPE((rows, count * PAIR), BF16)]
        + [SHAPE((2, rows, count * PAIR), BF16)] * parts,
        scratch_shapes=[pltpu.VMEM((parts, rows, PAIR), F32)] * 2,
        compiler_params=params(),
        cost_estimate=cost(40 * rows * keys * count * PAIR, 16 * keys * count * PAIR),
        name="attend_back",
    )(query, *kvs, *kvs, bias, lse, mixed, grad)


def middle_kernel(nm, x_ref, *refs):
    mixed_refs = refs[:nm]
    own_ref, other_ref, gain_ref, bias_ref, mid_ref, out_ref, flip_ref = refs[nm:]
    half = x_ref.shape[1] // 2
    wide = own_ref.shape[-1]
    sides = []
    for ref in (own_ref, other_ref):
        total = 0.0
        for k in range(nm):
            total = total + dot_nt(mixed_refs[k][...], ref[:, k, 0].reshape(half, wide))
        sides.append(total)
    middle = x_ref[...].astype(F32) + jnp.concatenate(sides, axis=1)
    mid_ref[...] = middle
    scaled, _ = standardize(middle)
    normed = (scaled * gain_ref[...] + bias_ref[...]).astype(BF16)
    out_ref[...] = normed
    flip_ref[...] = normed.T


def middle_norm(x, mixed, own, other, which, gain, bias):
    rows, width = x.shape
    chips, nm, _, deep, wide = own.shape
    block = row_block(rows)
    vector = pl.BlockSpec((1, width), lambda i: (0, 0))
    spec = pl.BlockSpec((chips, nm, 1, deep, wide), lambda i: (0, 0, which, 0, 0))
    line = pl.BlockSpec((block, width), lambda i: (i, 0))
    return pl.pallas_call(
        functools.partial(middle_kernel, nm),
        grid=(rows // block,),
        in_specs=[line]
        + [pl.BlockSpec((block, wide), lambda i: (i, 0))] * nm
        + [spec, spec, vector, vector],
        out_specs=[line, line, pl.BlockSpec((width, block), lambda i: (0, i))],
        out_shape=[
            SHAPE((rows, width), F32),
            SHAPE((rows, width), BF16),
            SHAPE((width, rows), BF16),
        ],
        compiler_params=params(),
        cost_estimate=cost(2 * rows * width * nm * wide, 14 * x.size),
        name="middle_norm",
    )(x, *mixed, own, other, gain, bias)


def load_weights(sizes, refs, held, sems):
    step = pl.program_id(0)
    nm = sum(sizes)
    copies, k, refs = {}, 0, list(refs)
    for size in sizes:
        sides = [refs.pop(0) for _ in range(4)]
        for i in range(size):
            for n, ref in enumerate(sides):
                w, side = n // 2, n % 2
                copies[w, 2 * k + side] = pltpu.make_async_copy(
                    ref.at[:, i], held.at[w, 2 * k + side], sems.at[w, 2 * k + side]
                )
            k += 1

    @pl.when(step == 0)
    def _():
        for copy in copies.values():
            copy.start()

    for k in range(nm):

        @pl.when(step == k)
        def _():
            for w in range(2):
                for side in range(2):
                    copies[w, 2 * k + side].wait()


def feed_kernel(sizes, *refs):
    nm, count = sum(sizes), 4 * len(sizes)
    in_ref, mid_ref, out_ref, act_ref, slope_ref, held, acc, sems = refs[count:]
    step = pl.program_id(0)
    load_weights(sizes, refs[:count], held, sems)
    half = in_ref.shape[1] // 2
    up = [held[0, 2 * step + side].reshape(half, -1) for side in range(2)]
    down = [held[1, 2 * step + side].reshape(half, -1) for side in range(2)]

    @pl.when(step == 0)
    def _():
        acc[...] = mid_ref[...]

    hidden = dot_nn(in_ref[:, :half], up[0]) + dot_nn(in_ref[:, half:], up[1])
    below = 0.5 + 0.5 * lax.erf(hidden * (0.5**0.5))
    density = jnp.exp(-0.5 * hidden * hidden) * 0.3989422804014327
    active = (hidden * below).astype(BF16)
    act_ref[0] = active
    slope_ref[0] = (below + hidden * density).astype(BF16)
    acc[:, :half] += dot_nt(active, down[0])
    acc[:, half:] += dot_nt(active, down[1])

    @pl.when(step == nm - 1)
    def _():
        out_ref[...] = acc[...].astype(BF16)


def feed(normed, middle, sizes, weights):
    rows, width = normed.shape
    nm = sum(sizes)
    chips, _, deep, hidden = weights[0].shape
    line = pl.BlockSpec((rows, width), lambda k: (0, 0))
    wide = pl.BlockSpec((1, rows, hidden), lambda k: (k, 0, 0))
    return pl.pallas_call(
        functools.partial(feed_kernel, sizes),
        grid=(nm,),
        in_specs=[ANY] * len(weights) + [line, line],
        out_specs=[line, wide, wide],
        out_shape=[SHAPE((rows, width), BF16)] + [SHAPE((nm, rows, hidden), BF16)] * 2,
        scratch_shapes=[
            pltpu.VMEM((2, 2 * nm, chips, deep, hidden), BF16),
            pltpu.VMEM((rows, width), F32),
            pltpu.SemaphoreType.DMA((2, 2 * nm)),
        ],
        compiler_params=params(60),
        cost_estimate=cost(4 * rows * width * nm * hidden, 4 * nm * width * hidden),
        name="feed",
    )(*weights, normed, middle)


def feed_back_kernel(sizes, *refs):
    nm, count = sum(sizes), 4 * len(sizes)
    g_ref, slope_ref, mid_ref, gain_ref = refs[count : count + 4]
    hid_ref, gmid_ref, attn_ref, flip_ref, sums_ref, held, acc, sems = refs[count + 4 :]
    step = pl.program_id(0)
    load_weights(sizes, refs[:count], held, sems)
    half = g_ref.shape[1] // 2
    up = [held[0, 2 * step + side].reshape(half, -1) for side in range(2)]
    down = [held[1, 2 * step + side].reshape(half, -1) for side in range(2)]
    active = dot_nn(g_ref[:, :half], down[0]) + dot_nn(g_ref[:, half:], down[1])
    hidden = (active * slope_ref[0].astype(F32)).astype(BF16)
    hid_ref[0] = hidden
    first, second = dot_nt(hidden, up[0]), dot_nt(hidden, up[1])

    @pl.when(step == 0)
    def _():
        acc[:, :half] = first
        acc[:, half:] = second

    @pl.when(step > 0)
    def _():
        acc[:, :half] += first
        acc[:, half:] += second

    @pl.when(step == nm - 1)
    def _():
        into, sums = norm_back(acc[...], mid_ref[...], gain_ref[...])
        result = g_ref[...].astype(F32) + into
        gmid_ref[...] = result
        attn = result.astype(BF16)
        attn_ref[...] = attn
        flip_ref[...] = attn.T
        sums_ref[...] = sums


def feed_back(grad, slope, middle, gain, sizes, weights):
    rows, width = grad.shape
    nm = sum(sizes)
    chips, _, deep, hidden = weights[0].shape
    line = pl.BlockSpec((rows, width), lambda k: (0, 0))
    wide = pl.BlockSpec((1, rows, hidden), lambda k: (k, 0, 0))
    return pl.pallas_call(
        functools.partial(feed_back_kernel, sizes),
        grid=(nm,),
        in_specs=[ANY] * len(weights)
        + [line, wide, line, pl.BlockSpec((1, width), lambda k: (0, 0))],
        out_specs=[
            wide,
            line,
            line,
            pl.BlockSpec((width, rows), lambda k: (0, 0)),
            pl.BlockSpec((2, width), lambda k: (0, 0)),
        ],
        out_shape=[
            SHAPE((nm, rows, hidden), BF16),
            SHAPE((rows, width), F32),
            SHAPE((rows, width), BF16),
            SHAPE((width, rows), BF16),
            SHAPE((2, width), F32),
        ],
        scratch_shapes=[
            pltpu.VMEM((2, 2 * nm, chips, deep, hidden), BF16),
            pltpu.VMEM((rows, width), F32),
            pltpu.SemaphoreType.DMA((2, 2 * nm)),
        ],
        compiler_params=params(60),
        cost_estimate=cost(4 * rows * width * nm * hidden, 4 * nm * width * hidden),
        name="feed_back",
    )(*weights, grad, slope, middle, gain)


def wide_grad_kernel(a_ref, b_ref, keep_ref, give_ref):
    half = a_ref.shape[0] // 2
    value = b_ref[0]
    keep_ref[0] = dot_nn(a_ref[:half], value).astype(BF16)
    give_ref[0] = dot_nn(a_ref[half:], value).astype(BF16)


def wide_grad(flipped, values, first, count, chips):
    width, rows = flipped.shape
    hidden = values.shape[2]
    block = min(512, hidden)
    piece = SHAPE((count, width // 2, hidden), BF16)
    out = pl.BlockSpec((1, width // 2, block), lambda k, i: (k, 0, i))
    keep, give = pl.pallas_call(
        wide_grad_kernel,
        grid=(count, hidden // block),
        in_specs=[
            pl.BlockSpec((width, rows), lambda k, i: (0, 0)),
            pl.BlockSpec((1, rows, block), lambda k, i: (first + k, 0, i)),
        ],
        out_specs=[out, out],
        out_shape=[piece, piece],
        compiler_params=params(),
        cost_estimate=cost(2 * count * width * rows * hidden, 4 * count * width * hidden),
        name="wide_grad",
    )(flipped, values)
    shape = (count, chips, width // 2 // chips, hidden)
    return keep.reshape(shape), give.reshape(shape)


def head_grad_kernel(count, *refs):
    n_ref, g_ref = refs[:2]
    mixeds, dqs, dkvs, cames = (refs[2 + i * count : 2 + (i + 1) * count] for i in range(4))
    sums = refs[2 + 4 * count : 2 + 5 * count]
    ka_ref, ga_ref, kb_ref, gb_ref = refs[2 + 5 * count :]
    half = n_ref.shape[0] // 2
    for n in range(count):
        total = (dkvs[n][...].astype(F32) + cames[n][...].astype(F32)).astype(BF16)
        sums[n][...] = total
        pairs = (
            (n_ref, dqs[n][...], ka_ref, ga_ref, 0),
            (g_ref, mixeds[n][...], ka_ref, ga_ref, 1),
            (n_ref, total[0], kb_ref, gb_ref, 0),
            (n_ref, total[1], kb_ref, gb_ref, 1),
        )
        for left, right, keep, give, i in pairs:
            shape = (keep.shape[1],) + keep.shape[3:]
            keep[n, :, i] = dot_nn(left[:half], right).astype(BF16).reshape(shape)
            give[n, :, i] = dot_nn(left[half:], right).astype(BF16).reshape(shape)


def head_grad(n_flip, g_flip, mixeds, dqs, dkvs, cames, chips):
    width, rows = n_flip.shape
    count, wide = len(dqs), dqs[0].shape[1]
    piece = SHAPE((count, chips, 2, width // 2 // chips, wide), BF16)
    return pl.pallas_call(
        functools.partial(head_grad_kernel, count),
        in_specs=[WHOLE] * (2 + 4 * count),
        out_specs=[WHOLE] * (count + 4),
        out_shape=[SHAPE(dkvs[0].shape, BF16)] * count + [piece] * 4,
        compiler_params=params(),
        cost_estimate=cost(8 * count * width * rows * wide, 8 * count * width * wide),
        name="head_grad",
    )(n_flip, g_flip, *mixeds, *dqs, *dkvs, *cames)


def first_back_kernel(nm, x_ref, gmid_ref, gain_ref, *refs):
    dqs, dkvs = refs[:nm], refs[nm : 2 * nm]
    qo_refs, kv_refs, out_ref, sums_ref = refs[2 * nm : 2 * nm + 2], refs[2 * nm + 2 : 2 * nm + 4], *refs[2 * nm + 4 :]
    step = pl.program_id(0)
    half = x_ref.shape[1] // 2
    wide = dqs[0].shape[1]
    sides = []
    for side in range(2):
        total = 0.0
        for k in range(nm):
            total = total + dot_nt(dqs[k][...], qo_refs[side][:, k, 0].reshape(half, wide))
            for i in range(2):
                total = total + dot_nt(dkvs[k][i], kv_refs[side][:, k, i].reshape(half, wide))
        sides.append(total)
    into, sums = norm_back(
        jnp.concatenate(sides, axis=1), x_ref[...].astype(F32), gain_ref[...]
    )
    out_ref[...] = (gmid_ref[...] + into).astype(BF16)

    @pl.when(step == 0)
    def _():
        sums_ref[...] = sums

    @pl.when(step > 0)
    def _():
        sums_ref[...] += sums


def first_back(x, gmid, gain, dqs, dkvs, qo, kv):
    rows, width = x.shape
    chips, nm, _, deep, wide = qo[0].shape
    block = row_block(rows)
    line = pl.BlockSpec((block, width), lambda i: (i, 0))
    q_spec = pl.BlockSpec((chips, nm, 1, deep, wide), lambda i: (0, 0, 0, 0, 0))
    kv_spec = pl.BlockSpec((chips, nm, 2, deep, wide), lambda i: (0, 0, 0, 0, 0))
    return pl.pallas_call(
        functools.partial(first_back_kernel, nm),
        grid=(rows // block,),
        in_specs=[line, line, pl.BlockSpec((1, width), lambda i: (0, 0))]
        + [pl.BlockSpec((block, wide), lambda i: (i, 0))] * nm
        + [pl.BlockSpec((2, block, wide), lambda i: (0, i, 0))] * nm
        + [q_spec, q_spec, kv_spec, kv_spec],
        out_specs=[line, pl.BlockSpec((2, width), lambda i: (0, 0))],
        out_shape=[SHAPE((rows, width), BF16), SHAPE((2, width), F32)],
        compiler_params=params(),
        cost_estimate=cost(6 * rows * width * nm * wide, 12 * x.size),
        name="first_back",
    )(x, gmid, gain, *dqs, *dkvs, *qo, *kv)


def add_low(a, b):
    return (a.astype(F32) + b.astype(F32)).astype(BF16)


class Scatter:
    def __init__(self, nd, nm, bits):
        self.nd, self.nm = nd, nm
        self.queue = {1: [], **{bit: [] for bit in bits}, "z": []}
        self.order, self.kept, self.waits, self.flying = {}, {}, {}, {}
        self.ends, self.came, self.done = {}, {}, {}

    def add(self, name, ks, keep, give, order):
        self.order[name] = order
        self.push(1, (name, tuple(ks), -1), list(range(0, self.nd, 2)), keep, give)

    def push(self, link, key, places, keep, give):
        self.kept[key], self.waits[key] = (places, keep), give
        self.queue[link].append(key)

    def launch(self, core=1, chip=1, z=1):
        for link, tasks in self.queue.items():
            for _ in range({1: core, "z": z}.get(link, chip)):
                if not tasks:
                    break
                key = tasks.pop(0)
                value = self.waits.pop(key)
                if link == "z":
                    self.flying[key] = ring(value, -1, self.nm)
                else:
                    self.flying[key] = swap(value, link, self.nd)

    def busy(self):
        return bool(self.flying) or any(self.queue.values())

    def land(self, *extra):
        waits, flying = list(self.waits), list(self.flying)
        values = lax.optimization_barrier(
            ([self.waits[key] for key in waits], [self.flying[key] for key in flying], extra)
        )
        self.waits = dict(zip(waits, values[0]))
        came = dict(zip(flying, values[1]))
        self.flying = {}
        for key, value in came.items():
            self.arrive(key, value)
        extra = values[2]
        return extra[0] if len(extra) == 1 else extra

    def arrive(self, key, value):
        name, ks, stage = key
        if stage == "z":
            self.came[name, ks - 1] = value
            self.advance(name, ks - 1)
            return
        order = self.order[name]
        places, keep = self.kept.pop(key)
        if stage + 1 == len(order):
            for n, k in enumerate(ks):
                self.ends[name, k] = (keep[n, 0], value[n, 0])
            for k in reversed(ks):
                self.advance(name, k)
            return
        bit = order[stage + 1]
        stays = [n for n, j in enumerate(places) if not j & bit]
        goes = [n for n, j in enumerate(places) if j & bit]

        def take(array, which):
            return jnp.stack([array[:, n] for n in which], axis=1)

        self.push(
            bit,
            (name, ks, stage + 1),
            [places[n] for n in stays],
            add_low(take(keep, stays), take(value, stays)),
            add_low(take(keep, goes), take(value, goes)),
        )

    def advance(self, name, k):
        if (name, k) not in self.ends or (k < self.nm - 1 and (name, k) not in self.came):
            return
        total = sum(part.astype(F32) for part in self.ends.pop((name, k)))
        if k < self.nm - 1:
            total = total + self.came.pop((name, k)).astype(F32)
        if k:
            key = (name, k, "z")
            self.waits[key] = total.astype(BF16)
            self.queue["z"].append(key)
        else:
            self.done[name] = total


def shards(nd, nm, tokens, views, norm_gains, norm_biases, w_proj, w_out, w_up, w_down, cotangent):
    micro, _, chunk, width = tokens.shape
    ranks = nm // micro
    half = max(ranks // 2, 1)
    rows = micro * chunk
    chips = nd // 2
    wide = w_out.shape[2]
    per_k = wide // PAIR
    hidden = w_up.shape[2]
    dp, mp = lax.axis_index("dp"), lax.axis_index("mp")
    group = mp // half
    step_here = group // 2
    rank = (dp & 1) + 2 * (mp % half)
    order_of = [2 * (p % chips) + p // chips for p in range(nd)]
    offsets = jnp.asarray(order_of, jnp.int32)
    index = dp.astype(jnp.int32) ^ offsets

    def routes(k):
        pairs = []
        for d in range(nd):
            for z in range(nm):
                m = (k + z) % micro
                r = z // micro
                to_d = (d & ~1) | (r & 1)
                to_z = (2 * m + (d & 1)) * half + r // 2
                pairs.append((d * nm + z, to_d * nm + to_z))
        return pairs

    there = ((dp & ~1) | ((mp // micro) & 1)).astype(jnp.int32) ^ offsets

    def pack(value):
        return [pack_features(value, there, (k + mp) % micro) for k in range(micro)]

    def send(packed, k):
        return lax.ppermute(packed[k], ("dp", "mp"), routes(k))

    def send_chunk(chunks, k):
        return lax.ppermute(chunks[k], ("dp", "mp"), [(b, a) for a, b in routes(k)])

    def unpack(came):
        return unpack_features(came, there, [(k + mp) % micro for k in range(micro)])

    def by_place(vector):
        return jnp.take(vector.reshape(-1, nd, width // nd), index, axis=1).reshape(-1, width)

    gains, biases = by_place(norm_gains[0]), by_place(norm_biases[0])

    flow = Flow(nd, nm)
    forth, back = flow.bits, flow.bits[::-1]
    groups = [[0], [1]] if nm > 1 else [[0]]
    groups += [list(range(k, min(k + 2, nm))) for k in range(2, nm, 2)]
    sizes = tuple(len(group) for group in groups)
    head = [jnp.concatenate([w_proj[0, :1], w_out, w_proj[0, 1:]])]
    up, down = [w_up[0]], [w_down[0]]
    flow.add("up0", w_up, forth)
    flow.add("down0", w_down, back)
    for step in range(nm - 1):
        head.append(ring(head[-1], 1, nm))
        flow.launch(chip=1 if step == 0 else 0)
        head = flow.land(head)
    token_parts = pack(tokens[:, 0])
    view = lax.dynamic_index_in_dim(views[:, 0], mp % micro, 0, keepdims=True)
    view = lax.ppermute(view, ("dp", "mp"), routes(0))
    flow.add("qo", jnp.stack([h[:2] for h in head]), forth)
    flow.add("kv", jnp.stack([h[2:] for h in head]), back)
    came = []
    while not (flow.whole("qo") and flow.whole("kv") and len(came) == micro):
        flow.launch(chip=2)
        if len(came) < micro:
            came.append(send(token_parts, len(came)))
        came, token_parts = flow.land(came, token_parts)
    qo_own, kv_own = flow.take_half("qo"), flow.take_half("kv")

    def turn():
        if len(up) < nm:
            up.append(ring(up[-1], 1, nm))
            down.append(ring(down[-1], 1, nm))

    def turned():
        for n, group in enumerate(groups):
            if f"up{n}" not in flow.order and group[-1] < len(up):
                flow.add(f"up{n}", jnp.stack([up[k] for k in group]), forth)
                flow.add(f"down{n}", jnp.stack([down[k] for k in group]), back)

    halves = {}

    def core_halves(most):
        for n in range(len(groups)):
            for name in (f"up{n}", f"down{n}"):
                if most and flow.whole(name):
                    halves[name] = flow.take_half(name)
                    flow.fly(name, swap(halves[name], 1, nd))
                    most -= 1

    flow.fly("kv", swap(kv_own, 1, nd))
    turn()
    x, normed, n_flip = first_norm(came, gains[:1], biases[:1])
    x, normed, n_flip, view, qo_own, kv_own, up, down = flow.land(
        x, normed, n_flip, view, qo_own, kv_own, up, down
    )
    turned()
    kv = [kv_own, flow.kept.pop("kv")]

    flow.fly("qo", swap(qo_own, 1, nd))
    turn()
    flow.launch()
    own_kv = project(normed, kv[0], kv[1], 0, 2)
    own_kv, normed, qo_own, up, down = flow.land(own_kv, normed, qo_own, up, down)
    turned()
    qo = [qo_own, flow.kept.pop("qo")]

    def swap_rank(value, bit):
        if bit == 1:
            return swap(value, 1, nd)
        return lax.ppermute(value, "mp", [(i, i ^ (bit >> 1)) for i in range(nm)])

    rank_bits = [1 << b for b in range(ranks.bit_length() - 1)]
    kvs = {0: own_kv}
    for bit in rank_bits:
        for j in list(kvs):
            kvs[j | bit] = swap_rank(kvs[j], bit)
    kvs = [kvs[j] for j in range(ranks)]
    turn()
    flow.launch(chip=1)
    query = project(normed, qo[0], qo[1], 0, 1)
    slot = jnp.stack([(step_here - t) % micro for t in range(micro)])
    within = (slot[:, None] * chunk + jnp.arange(chunk)[None]).reshape(-1)
    position = jnp.stack([(rank ^ j) * rows + within for j in range(ranks)])
    bias = jnp.where(position < TRI + view[0] * VIEW_TOK, 0.0, -1.0).astype(F32)
    grad_parts = pack(cotangent[:, 0])
    kvs, query, up, down, bias, grad_parts = flow.land(kvs, query, up, down, bias, grad_parts)
    turned()

    grad_came, mixed, lses = [], [], []
    last = [f"{name}{n}" for n in range(len(groups)) for name in ("up", "down")]
    at_once = max(nm // 2, 1)
    while len(mixed) < nm or len(grad_came) < micro or not all(
        name in halves or flow.whole(name) for name in last
    ):
        core_halves(2)
        turn()
        flow.launch(chip=1)
        if len(grad_came) < micro:
            grad_came.append(send(grad_parts, len(grad_came)))
        for k in range(len(mixed), min(len(mixed) + at_once, nm)):
            part, lse = attend(query, kvs, bias, k * per_k, per_k)
            mixed.append(part)
            lses.append(lse)
        mixed, query, halves, grad_parts, grad_came, up, down = flow.land(
            mixed, query, halves, grad_parts, grad_came, up, down
        )
        turned()
    core_halves(len(last))
    middle, normed_two, flip_two = middle_norm(x, mixed, *qo, 1, gains[1:], biases[1:])
    grad, grad_flip = flip(grad_came)
    middle, normed_two, flip_two, halves, grad, grad_flip = flow.land(
        middle, normed_two, flip_two, halves, grad, grad_flip
    )
    weights = []
    for name in last:
        weights += [halves[name], flow.kept.pop(name)]

    result, active, slope = feed(normed_two, middle, sizes, weights)
    out_chunks = result.reshape((micro, chunk, width))
    output = []

    sums = Scatter(nd, nm, flow.bits)
    pairs = [list(range(k, min(k + 2, nm))) for k in range(0, nm, 2)][::-1]

    def wide_grads(flipped, values):
        return [wide_grad(flipped, values, ks[0], len(ks), chips) for ks in pairs]

    for ks in pairs:
        sums.launch(chip=0)
        pieces = wide_grad(grad_flip, active, ks[0], len(ks), chips)
        pieces, active, grad_flip, out_chunks, grad = sums.land(
            pieces, active, grad_flip, out_chunks, grad
        )
        sums.add("down", ks, *pieces, back[::-1])
    sums.launch(core=2)
    output.append(send_chunk(out_chunks, 0))
    hid, gmid, attn, attn_flip, sums_two = feed_back(
        grad, slope, middle, gains[1:], sizes, weights
    )
    hid, gmid, attn, attn_flip, sums_two, flip_two, out_chunks, output = sums.land(
        hid, gmid, attn, attn_flip, sums_two, flip_two, out_chunks, output
    )
    sums.launch(core=0)
    pieces = wide_grads(flip_two, hid)
    pieces, attn = sums.land(pieces, attn)
    for ks, piece in zip(pairs, pieces):
        sums.add("up", ks, *piece, forth[::-1])

    sums.launch(core=2, chip=0)
    grad_mixed = project(attn, *qo, 1, 1)
    grad_mixed, query, out_chunks = sums.land(grad_mixed, query, out_chunks)
    dqs, dkvs, pending = {}, {}, []
    bias_tall = bias[:, :, None]
    closing = [[k] for k in range(min(2, nm))] + [
        list(range(k, min(k + 2, nm))) for k in range(2, nm, 2)
    ]

    def head_grads(dkv_part, dkv_came):
        if not closing or any(k not in dkv_came for k in closing[-1]):
            return None
        ks = closing.pop()
        outs = head_grad(
            n_flip,
            attn_flip,
            [mixed[k] for k in ks],
            [dqs[k] for k in ks],
            [dkv_part[k] for k in ks],
            [dkv_came[k] for k in ks],
            chips,
        )
        for n, k in enumerate(ks):
            dkvs[k] = outs[n]
        return ks, outs[len(ks) :]

    dkv_part, dkv_came = {}, {}

    def exchange(parts):
        parts = dict(enumerate(parts))
        came = None
        for bit in rank_bits[::-1]:
            if came is not None:
                parts = {j: add_low(part, came[j]) for j, part in parts.items()}
            came = {j ^ bit: swap_rank(parts.pop(j), bit) for j in list(parts) if j & bit}
        return parts[0], came[0]

    parts = None
    for k in list(reversed(range(nm))) + [-1, -2]:
        sums.launch(core=2, chip=1 if k >= 0 else 2, z=2 if k >= 0 else 3)
        if k >= 0 and len(output) < micro:
            output.append(send_chunk(out_chunks, len(output)))
        ready = head_grads(dkv_part, dkv_came)
        if parts is not None:
            dkv_part[k + 1], dkv_came[k + 1] = exchange(parts)
            parts = None
        if k >= 0:
            dqs[k], *parts = attend_back(
                query, kvs, bias_tall, lses[k], mixed[k], grad_mixed, k * per_k, per_k
            )
        live = (ready and ready[1], dqs, parts, query, dkv_part, dkv_came, dkvs, output, gmid)
        live = sums.land(*live)
        outs, dqs, parts, query, dkv_part, dkv_came, dkvs, output, gmid = live
        if ready:
            sums.add("qo", ready[0], outs[0], outs[1], forth[::-1])
            sums.add("kv", ready[0], outs[2], outs[3], back[::-1])
    sums.launch(core=2, chip=2, z=3)
    first, sums_one = first_back(
        x, gmid, gains[:1], [dqs[k] for k in range(nm)], [dkvs[k] for k in range(nm)], qo, kv
    )
    first, sums_one = sums.land(first, sums_one)
    first = first.reshape((micro, chunk, width))
    grad_tokens = [send_chunk(first, k) for k in range(micro)]
    while sums.busy():
        sums.launch(core=2, chip=2, z=3)
        sums.land()
    g_qo, g_kv, g_up, g_down = (sums.done[name] for name in ("qo", "kv", "up", "down"))

    def everywhere(value):
        count = value.shape[0]
        value = jnp.take(
            value.reshape(count, nd, width // nd), jnp.argsort(index), axis=1
        ).reshape(count, width)
        bit = 1
        while bit < nd:
            value = value + swap(value, bit, nd)
            bit *= 2
        bit = 1
        while bit < nm:
            value = value + lax.ppermute(value, "mp", [(i, i ^ bit) for i in range(nm)])
            bit *= 2
        share = width // (nd * nm)
        return lax.dynamic_slice_in_dim(value, (dp * nm + mp) * share, share, 1)

    vectors = everywhere(jnp.concatenate([sums_one, sums_two]))
    return (
        unpack(output)[:, None],
        unpack(grad_tokens)[:, None],
        jnp.concatenate([g_qo[:1], g_kv])[None],
        g_qo[1][None],
        g_up[None],
        g_down[None],
        jnp.stack([vectors[0], vectors[2]])[None],
        vectors[1][None],
        vectors[3][None],
    )


def solution(mesh):
    placed = (
        P(None, "dp", "mp", None),
        P(None, "dp"),
        P(),
        P(),
        P(None, None, "dp", "mp"),
        P(None, "dp", "mp"),
        P(None, "dp", "mp"),
        P(None, "dp", "mp"),
        P(None, "dp", "mp", None),
    )
    return jax.shard_map(
        functools.partial(shards, mesh.shape["dp"], mesh.shape["mp"]),
        mesh=mesh,
        in_specs=placed,
        out_specs=(
            P(None, "dp", "mp", None),
            P(None, "dp", "mp", None),
            P(None, None, "dp", "mp"),
            P(None, "dp", "mp"),
            P(None, "dp", "mp"),
            P(None, "dp", "mp"),
            P(None, None, ("dp", "mp")),
            P(None, ("dp", "mp")),
            P(None, ("dp", "mp")),
        ),
        check_vma=False,
    )
```

```python
import functools

import jax
import jax.numpy as jnp
from jax import lax
from jax.experimental import pallas as pl
from jax.experimental.pallas import tpu as pltpu
from jax.sharding import PartitionSpec as P

HDIM = 64
PAIR = 2 * HDIM
VIEW_TOK = 256
TRI = 768
EPSILON = 1e-05
MASKED = -1000000000.0
F32 = jnp.float32
BF16 = jnp.bfloat16
MIB = 1024 * 1024
ANY = pl.BlockSpec(memory_space=pl.ANY)
WHOLE = pl.BlockSpec(memory_space=pltpu.VMEM)
SHAPE = jax.ShapeDtypeStruct


def params(mib=56):
    return pltpu.CompilerParams(vmem_limit_bytes=mib * MIB)


def cost(flops, nbytes):
    return pl.CostEstimate(flops=int(flops), bytes_accessed=int(nbytes), transcendentals=0)


def dot_nt(a, b):
    return lax.dot_general(a, b, (((1,), (1,)), ((), ())), preferred_element_type=F32)


def dot_nn(a, b):
    return lax.dot_general(a, b, (((1,), (0,)), ((), ())), preferred_element_type=F32)


def dot_tn(a, b):
    return lax.dot_general(a, b, (((0,), (0,)), ((), ())), preferred_element_type=F32)


def row_block(rows):
    return 256 if rows % 256 == 0 else 128


def swap(value, bit, nd):
    return lax.ppermute(value, "dp", [(i, i ^ bit) for i in range(nd)])


def ring(value, step, nm):
    return lax.ppermute(value, "mp", [(i, (i + step) % nm) for i in range(nm)])


class Flow:
    def __init__(self, nd, nm):
        self.nd, self.nm = nd, nm
        self.bits = [1 << b for b in range(1, nd.bit_length() - 1)]
        self.queue = {bit: [] for bit in self.bits}
        self.order, self.pieces, self.flying, self.kept = {}, {}, {}, {}

    def add(self, name, value, order):
        self.order[name] = list(order)
        self.pieces[name] = [(0, value)]
        self.next(name)

    def next(self, name):
        if self.order[name]:
            self.queue[self.order[name][0]].append(name)

    def launch(self, chip=1):
        for bit, tasks in self.queue.items():
            for _ in range(chip):
                if tasks:
                    name = tasks.pop(0)
                    values = [value for _, value in self.pieces[name]]
                    value = values[0][None] if len(values) == 1 else jnp.stack(values)
                    self.flying["chip", name] = swap(value, bit, self.nd)

    def fly(self, name, value):
        self.flying["kept", name] = value

    def land(self, *extra):
        names, flying, kept = list(self.pieces), list(self.flying), list(self.kept)
        values = lax.optimization_barrier(
            (
                [self.pieces[name] for name in names],
                [self.flying[key] for key in flying],
                [self.kept[key] for key in kept],
                extra,
            )
        )
        for name, pieces in zip(names, values[0]):
            self.pieces[name] = [(j, v) for (j, _), (_, v) in zip(self.pieces[name], pieces)]
        self.kept = dict(zip(kept, values[2]))
        self.flying = {}
        for (kind, name), value in zip(flying, values[1]):
            if kind == "kept":
                self.kept[name] = value
                continue
            bit = self.order[name].pop(0)
            held = self.pieces[name]
            self.pieces[name] = held + [(j | bit, value[n]) for n, (j, _) in enumerate(held)]
            self.next(name)
        extra = values[3]
        return extra[0] if len(extra) == 1 else extra

    def whole(self, name):
        return name in self.pieces and not self.order[name]

    def take_half(self, name):
        pieces = dict(self.pieces.pop(name))
        return jnp.stack([pieces[2 * i] for i in range(self.nd // 2)])


def pack_kernel(index_ref, in_ref, out_ref):
    nd = index_ref.shape[0] - 1
    wide = in_ref.shape[2] // nd
    for p in range(nd):
        there = pl.ds(pl.multiple_of(index_ref[p] * wide, wide), wide)
        out_ref[:, p * wide : (p + 1) * wide] = in_ref[0, :, there]


def pack_features(value, index, which):
    micro, rows, width = value.shape
    nd = index.shape[0]
    if width // nd % 128:
        chunk = lax.dynamic_index_in_dim(value, which, 0, keepdims=False)
        return jnp.take(chunk.reshape(rows, nd, -1), index, axis=1).reshape(rows, width)
    return pl.pallas_call(
        pack_kernel,
        grid_spec=pltpu.PrefetchScalarGridSpec(
            num_scalar_prefetch=1,
            grid=(1,),
            in_specs=[pl.BlockSpec((1, rows, width), lambda i, index_ref: (index_ref[nd], 0, 0))],
            out_specs=pl.BlockSpec((rows, width), lambda i, index_ref: (0, 0)),
        ),
        out_shape=SHAPE((rows, width), value.dtype),
        compiler_params=params(),
        cost_estimate=cost(0, 6 * rows * width),
        name="pack_features",
    )(jnp.append(index, which.astype(jnp.int32)), value)


def unpack_kernel(index_ref, *refs):
    ins, out_ref = refs[:-1], refs[-1]
    nd = index_ref.shape[0] - len(ins)
    wide = out_ref.shape[2] // nd
    for k, in_ref in enumerate(ins):
        for p in range(nd):
            there = pl.ds(pl.multiple_of(index_ref[p] * wide, wide), wide)
            out_ref[index_ref[nd + k], :, there] = in_ref[:, p * wide : (p + 1) * wide]


def unpack_features(chunks, index, places):
    rows, width = chunks[0].shape
    micro, nd = len(chunks), index.shape[0]
    places = [place.astype(jnp.int32) for place in places]
    if width // nd % 128:
        back = jnp.argsort(index)
        stacked = jnp.stack(chunks).reshape(micro, rows, nd, -1)
        stacked = jnp.take(stacked, back, axis=2).reshape(micro, rows, width)
        return jnp.take(stacked, jnp.argsort(jnp.stack(places)), axis=0)
    return pl.pallas_call(
        unpack_kernel,
        in_specs=[pl.BlockSpec(memory_space=pltpu.SMEM)] + [WHOLE] * micro,
        out_specs=WHOLE,
        out_shape=SHAPE((micro, rows, width), chunks[0].dtype),
        compiler_params=params(),
        cost_estimate=cost(0, 4 * micro * rows * width),
        name="unpack_features",
    )(jnp.concatenate([index, jnp.stack(places)]), *chunks)


def standardize(state):
    centre = jnp.mean(state, axis=-1, keepdims=True)
    centred = state - centre
    spread = jnp.mean(centred * centred, axis=-1, keepdims=True)
    inverse = lax.rsqrt(spread + EPSILON)
    return centred * inverse, inverse


def norm_back(grad, state, gain):
    scaled, inverse = standardize(state)
    weighted = grad * gain
    first = jnp.mean(weighted, axis=-1, keepdims=True)
    second = jnp.mean(weighted * scaled, axis=-1, keepdims=True)
    sums = jnp.concatenate(
        [jnp.sum(grad * scaled, axis=0, keepdims=True), jnp.sum(grad, axis=0, keepdims=True)], 0
    )
    return inverse * (weighted - first - scaled * second), sums


def first_norm_kernel(micro, *refs):
    chunks = refs[:micro]
    gain_ref, bias_ref, x_ref, out_ref, flip_ref = refs[micro:]
    rows = chunks[0].shape[0]
    for k, ref in enumerate(chunks):
        here = slice(k * rows, (k + 1) * rows)
        x_ref[here] = ref[...]
        scaled, _ = standardize(ref[...].astype(F32))
        normed = (scaled * gain_ref[...] + bias_ref[...]).astype(BF16)
        out_ref[here] = normed
        flip_ref[:, here] = normed.T


def first_norm(chunks, gain, bias):
    rows, width = chunks[0].shape
    rows = rows * len(chunks)
    return pl.pallas_call(
        functools.partial(first_norm_kernel, len(chunks)),
        in_specs=[WHOLE] * (len(chunks) + 2),
        out_specs=[WHOLE] * 3,
        out_shape=[SHAPE((rows, width), BF16)] * 2 + [SHAPE((width, rows), BF16)],
        compiler_params=params(),
        cost_estimate=cost(0, 10 * rows * width),
        name="first_norm",
    )(*chunks, gain, bias)


def flip_kernel(*refs):
    chunks, out_ref, flip_ref = refs[:-2], refs[-2], refs[-1]
    rows = chunks[0].shape[0]
    for k, ref in enumerate(chunks):
        here = slice(k * rows, (k + 1) * rows)
        out_ref[here] = ref[...]
        flip_ref[:, here] = ref[...].T


def flip(chunks):
    rows, width = chunks[0].shape
    rows = rows * len(chunks)
    return pl.pallas_call(
        flip_kernel,
        in_specs=[WHOLE] * len(chunks),
        out_specs=[WHOLE] * 2,
        out_shape=[SHAPE((rows, width), BF16), SHAPE((width, rows), BF16)],
        compiler_params=params(),
        cost_estimate=cost(0, 6 * rows * width),
        name="flip",
    )(*chunks)


def proj_kernel(in_ref, own_ref, other_ref, out_ref):
    value = in_ref[...]
    half = value.shape[1] // 2
    wide = own_ref.shape[-1]
    for k in range(own_ref.shape[1]):
        first = own_ref[:, k, 0].reshape(half, wide)
        second = other_ref[:, k, 0].reshape(half, wide)
        total = dot_nn(value[:, :half], first) + dot_nn(value[:, half:], second)
        out_ref[0, :, k * wide : (k + 1) * wide] = total.astype(BF16)


def project(value, own, other, start, count):
    rows, width = value.shape
    chips, nm, _, deep, wide = own.shape
    spec = pl.BlockSpec((chips, nm, 1, deep, wide), lambda i: (0, 0, start + i, 0, 0))
    return pl.pallas_call(
        proj_kernel,
        grid=(count,),
        in_specs=[pl.BlockSpec((rows, width), lambda i: (0, 0)), spec, spec],
        out_specs=pl.BlockSpec((1, rows, nm * wide), lambda i: (i, 0, 0)),
        out_shape=SHAPE((count, rows, nm * wide), BF16),
        compiler_params=params(),
        cost_estimate=cost(2 * count * rows * width * nm * wide, 2 * count * rows * width),
        name="project",
    )(value, own, other)


def attend_kernel(parts, q_ref, *refs):
    k_refs, v_refs = refs[:parts], refs[parts : 2 * parts]
    bias_ref, out_ref, lse_ref = refs[2 * parts :]
    rows = q_ref.shape[1]
    low = lax.broadcasted_iota(jnp.int32, (1, PAIR), 1) < HDIM
    query = q_ref[0] * jnp.asarray(HDIM ** (-0.5), BF16)
    mixed = None
    for head in range(2):
        mine = low if head == 0 else jnp.logical_not(low)
        q_mine = jnp.where(mine, query, jnp.zeros_like(query))
        scores = [
            jnp.where(bias_ref[p : p + 1, :] < 0.0, MASKED, dot_nt(q_mine, k_refs[p][0]))
            for p in range(parts)
        ]
        top = functools.reduce(
            jnp.maximum, [jnp.max(part, axis=1, keepdims=True) for part in scores]
        )
        total, part = 0.0, 0.0
        for p in range(parts):
            expo = jnp.exp(scores[p] - top)
            total = total + jnp.sum(expo, axis=1, keepdims=True)
            part = part + dot_nn(expo.astype(BF16), v_refs[p][0])
        part = part / total
        mixed = part if head == 0 else jnp.where(low, mixed, part)
        lse = top + jnp.log(total)
        lse_ref[0, head : head + 1, :] = jnp.transpose(jnp.broadcast_to(lse, (rows, 128)))[0:1, :]
    out_ref[...] = mixed.astype(BF16)


def attend(query, kvs, bias, start, count):
    _, rows, width = query.shape
    parts = len(kvs)
    block = row_block(rows)
    keys = rows * parts
    key_spec = pl.BlockSpec((1, rows, PAIR), lambda h, i: (0, 0, start + h))
    value_spec = pl.BlockSpec((1, rows, PAIR), lambda h, i: (1, 0, start + h))
    return pl.pallas_call(
        functools.partial(attend_kernel, parts),
        grid=(count, rows // block),
        in_specs=[pl.BlockSpec((1, block, PAIR), lambda h, i: (0, i, start + h))]
        + [key_spec] * parts
        + [value_spec] * parts
        + [pl.BlockSpec((parts, rows), lambda h, i: (0, 0))],
        out_specs=[
            pl.BlockSpec((block, PAIR), lambda h, i: (i, h)),
            pl.BlockSpec((1, 2, block), lambda h, i: (h, 0, i)),
        ],
        out_shape=[SHAPE((rows, count * PAIR), BF16), SHAPE((count, 2, rows), F32)],
        compiler_params=params(),
        cost_estimate=cost(16 * rows * keys * count * PAIR, 8 * keys * count * PAIR),
        name="attend",
    )(query, *kvs, *kvs, bias)


def attend_back_kernel(parts, q_ref, *refs):
    k_refs, v_refs = refs[:parts], refs[parts : 2 * parts]
    bias_ref, lse_ref, mixed_ref, grad_ref, dq_ref = refs[2 * parts : 2 * parts + 5]
    dkv_refs = refs[2 * parts + 5 : 3 * parts + 5]
    dk_acc, dv_acc = refs[3 * parts + 5 :]
    step = pl.program_id(1)
    low = lax.broadcasted_iota(jnp.int32, (1, PAIR), 1) < HDIM
    query = q_ref[0] * jnp.asarray(HDIM ** (-0.5), BF16)
    grad = grad_ref[0]
    product = mixed_ref[...].astype(F32) * grad.astype(F32)

    @pl.when(step == 0)
    def _():
        dk_acc[...] = jnp.zeros_like(dk_acc)
        dv_acc[...] = jnp.zeros_like(dv_acc)

    grad_query = None
    for head in range(2):
        mine = low if head == 0 else jnp.logical_not(low)
        q_mine = jnp.where(mine, query, jnp.zeros_like(query))
        g_mine = jnp.where(mine, grad, jnp.zeros_like(grad))
        delta = jnp.sum(jnp.where(mine, product, 0.0), axis=1, keepdims=True)
        delta = jnp.transpose(jnp.broadcast_to(delta, (delta.shape[0], 128)))[0:1, :]
        query_part = 0.0
        for p in range(parts):
            keys, values = k_refs[p][0], v_refs[p][0]
            scores = jnp.where(bias_ref[p] < 0.0, MASKED, dot_nt(keys, q_mine))
            probs = jnp.exp(scores - lse_ref[0, head : head + 1, :])
            upstream = dot_nt(values, g_mine)
            grad_scores = (probs * (upstream - delta)).astype(BF16)
            dv_acc[p] += dot_nn(probs.astype(BF16), g_mine)
            dk_acc[p] += dot_nn(grad_scores, q_mine)
            query_part = query_part + dot_tn(grad_scores, keys)
        grad_query = query_part if head == 0 else jnp.where(low, grad_query, query_part)
    dq_ref[...] = (grad_query * HDIM ** (-0.5)).astype(BF16)

    @pl.when(step == pl.num_programs(1) - 1)
    def _():
        for p in range(parts):
            dkv_refs[p][0] = dk_acc[p].astype(BF16)
            dkv_refs[p][1] = dv_acc[p].astype(BF16)


def attend_back(query, kvs, bias, lse, mixed, grad, start, count):
    _, rows, width = query.shape
    parts = len(kvs)
    block = row_block(rows)
    keys = rows * parts
    key_spec = pl.BlockSpec((1, rows, PAIR), lambda h, i: (0, 0, start + h))
    value_spec = pl.BlockSpec((1, rows, PAIR), lambda h, i: (1, 0, start + h))
    return pl.pallas_call(
        functools.partial(attend_back_kernel, parts),
        grid=(count, rows // block),
        in_specs=[pl.BlockSpec((1, block, PAIR), lambda h, i: (0, i, start + h))]
        + [key_spec] * parts
        + [value_spec] * parts
        + [
            pl.BlockSpec((parts, rows, 1), lambda h, i: (0, 0, 0)),
            pl.BlockSpec((1, 2, block), lambda h, i: (h, 0, i)),
            pl.BlockSpec((block, PAIR), lambda h, i: (i, h)),
            pl.BlockSpec((1, block, PAIR), lambda h, i: (0, i, start + h)),
        ],
        out_specs=[pl.BlockSpec((block, PAIR), lambda h, i: (i, h))]
        + [pl.BlockSpec((2, rows, PAIR), lambda h, i: (0, 0, h))] * parts,
        out_shape=[SHAPE((rows, count * PAIR), BF16)]
        + [SHAPE((2, rows, count * PAIR), BF16)] * parts,
        scratch_shapes=[pltpu.VMEM((parts, rows, PAIR), F32)] * 2,
        compiler_params=params(),
        cost_estimate=cost(40 * rows * keys * count * PAIR, 16 * keys * count * PAIR),
        name="attend_back",
    )(query, *kvs, *kvs, bias, lse, mixed, grad)


def middle_kernel(nm, x_ref, *refs):
    mixed_refs = refs[:nm]
    own_ref, other_ref, gain_ref, bias_ref, mid_ref, out_ref, flip_ref = refs[nm:]
    half = x_ref.shape[1] // 2
    wide = own_ref.shape[-1]
    sides = []
    for ref in (own_ref, other_ref):
        total = 0.0
        for k in range(nm):
            total = total + dot_nt(mixed_refs[k][...], ref[:, k, 0].reshape(half, wide))
        sides.append(total)
    middle = x_ref[...].astype(F32) + jnp.concatenate(sides, axis=1)
    mid_ref[...] = middle
    scaled, _ = standardize(middle)
    normed = (scaled * gain_ref[...] + bias_ref[...]).astype(BF16)
    out_ref[...] = normed
    flip_ref[...] = normed.T


def middle_norm(x, mixed, own, other, which, gain, bias):
    rows, width = x.shape
    chips, nm, _, deep, wide = own.shape
    block = row_block(rows)
    vector = pl.BlockSpec((1, width), lambda i: (0, 0))
    spec = pl.BlockSpec((chips, nm, 1, deep, wide), lambda i: (0, 0, which, 0, 0))
    line = pl.BlockSpec((block, width), lambda i: (i, 0))
    return pl.pallas_call(
        functools.partial(middle_kernel, nm),
        grid=(rows // block,),
        in_specs=[line]
        + [pl.BlockSpec((block, wide), lambda i: (i, 0))] * nm
        + [spec, spec, vector, vector],
        out_specs=[line, line, pl.BlockSpec((width, block), lambda i: (0, i))],
        out_shape=[
            SHAPE((rows, width), F32),
            SHAPE((rows, width), BF16),
            SHAPE((width, rows), BF16),
        ],
        compiler_params=params(),
        cost_estimate=cost(2 * rows * width * nm * wide, 14 * x.size),
        name="middle_norm",
    )(x, *mixed, own, other, gain, bias)


def load_weights(sizes, refs, held, sems):
    step = pl.program_id(0)
    nm = sum(sizes)
    copies, k, refs = {}, 0, list(refs)
    for size in sizes:
        sides = [refs.pop(0) for _ in range(4)]
        for i in range(size):
            for n, ref in enumerate(sides):
                w, side = n // 2, n % 2
                copies[w, 2 * k + side] = pltpu.make_async_copy(
                    ref.at[:, i], held.at[w, 2 * k + side], sems.at[w, 2 * k + side]
                )
            k += 1

    @pl.when(step == 0)
    def _():
        for copy in copies.values():
            copy.start()

    for k in range(nm):

        @pl.when(step == k)
        def _():
            for w in range(2):
                for side in range(2):
                    copies[w, 2 * k + side].wait()


def feed_kernel(sizes, *refs):
    nm, count = sum(sizes), 4 * len(sizes)
    in_ref, mid_ref, out_ref, act_ref, slope_ref, held, acc, sems = refs[count:]
    step = pl.program_id(0)
    load_weights(sizes, refs[:count], held, sems)
    half = in_ref.shape[1] // 2
    up = [held[0, 2 * step + side].reshape(half, -1) for side in range(2)]
    down = [held[1, 2 * step + side].reshape(half, -1) for side in range(2)]

    @pl.when(step == 0)
    def _():
        acc[...] = mid_ref[...]

    hidden = dot_nn(in_ref[:, :half], up[0]) + dot_nn(in_ref[:, half:], up[1])
    below = 0.5 + 0.5 * lax.erf(hidden * (0.5**0.5))
    density = jnp.exp(-0.5 * hidden * hidden) * 0.3989422804014327
    active = (hidden * below).astype(BF16)
    act_ref[0] = active
    slope_ref[0] = (below + hidden * density).astype(BF16)
    acc[:, :half] += dot_nt(active, down[0])
    acc[:, half:] += dot_nt(active, down[1])

    @pl.when(step == nm - 1)
    def _():
        out_ref[...] = acc[...].astype(BF16)


def feed(normed, middle, sizes, weights):
    rows, width = normed.shape
    nm = sum(sizes)
    chips, _, deep, hidden = weights[0].shape
    line = pl.BlockSpec((rows, width), lambda k: (0, 0))
    wide = pl.BlockSpec((1, rows, hidden), lambda k: (k, 0, 0))
    return pl.pallas_call(
        functools.partial(feed_kernel, sizes),
        grid=(nm,),
        in_specs=[ANY] * len(weights) + [line, line],
        out_specs=[line, wide, wide],
        out_shape=[SHAPE((rows, width), BF16)] + [SHAPE((nm, rows, hidden), BF16)] * 2,
        scratch_shapes=[
            pltpu.VMEM((2, 2 * nm, chips, deep, hidden), BF16),
            pltpu.VMEM((rows, width), F32),
            pltpu.SemaphoreType.DMA((2, 2 * nm)),
        ],
        compiler_params=params(60),
        cost_estimate=cost(4 * rows * width * nm * hidden, 4 * nm * width * hidden),
        name="feed",
    )(*weights, normed, middle)


def feed_back_kernel(sizes, *refs):
    nm, count = sum(sizes), 4 * len(sizes)
    g_ref, slope_ref, mid_ref, gain_ref = refs[count : count + 4]
    hid_ref, gmid_ref, attn_ref, flip_ref, sums_ref, held, acc, sems = refs[count + 4 :]
    step = pl.program_id(0)
    load_weights(sizes, refs[:count], held, sems)
    half = g_ref.shape[1] // 2
    up = [held[0, 2 * step + side].reshape(half, -1) for side in range(2)]
    down = [held[1, 2 * step + side].reshape(half, -1) for side in range(2)]
    active = dot_nn(g_ref[:, :half], down[0]) + dot_nn(g_ref[:, half:], down[1])
    hidden = (active * slope_ref[0].astype(F32)).astype(BF16)
    hid_ref[0] = hidden
    first, second = dot_nt(hidden, up[0]), dot_nt(hidden, up[1])

    @pl.when(step == 0)
    def _():
        acc[:, :half] = first
        acc[:, half:] = second

    @pl.when(step > 0)
    def _():
        acc[:, :half] += first
        acc[:, half:] += second

    @pl.when(step == nm - 1)
    def _():
        into, sums = norm_back(acc[...], mid_ref[...], gain_ref[...])
        result = g_ref[...].astype(F32) + into
        gmid_ref[...] = result
        attn = result.astype(BF16)
        attn_ref[...] = attn
        flip_ref[...] = attn.T
        sums_ref[...] = sums


def feed_back(grad, slope, middle, gain, sizes, weights):
    rows, width = grad.shape
    nm = sum(sizes)
    chips, _, deep, hidden = weights[0].shape
    line = pl.BlockSpec((rows, width), lambda k: (0, 0))
    wide = pl.BlockSpec((1, rows, hidden), lambda k: (k, 0, 0))
    return pl.pallas_call(
        functools.partial(feed_back_kernel, sizes),
        grid=(nm,),
        in_specs=[ANY] * len(weights)
        + [line, wide, line, pl.BlockSpec((1, width), lambda k: (0, 0))],
        out_specs=[
            wide,
            line,
            line,
            pl.BlockSpec((width, rows), lambda k: (0, 0)),
            pl.BlockSpec((2, width), lambda k: (0, 0)),
        ],
        out_shape=[
            SHAPE((nm, rows, hidden), BF16),
            SHAPE((rows, width), F32),
            SHAPE((rows, width), BF16),
            SHAPE((width, rows), BF16),
            SHAPE((2, width), F32),
        ],
        scratch_shapes=[
            pltpu.VMEM((2, 2 * nm, chips, deep, hidden), BF16),
            pltpu.VMEM((rows, width), F32),
            pltpu.SemaphoreType.DMA((2, 2 * nm)),
        ],
        compiler_params=params(60),
        cost_estimate=cost(4 * rows * width * nm * hidden, 4 * nm * width * hidden),
        name="feed_back",
    )(*weights, grad, slope, middle, gain)


def wide_grad_kernel(a_ref, b_ref, keep_ref, give_ref):
    half = a_ref.shape[0] // 2
    value = b_ref[0]
    keep_ref[0] = dot_nn(a_ref[:half], value).astype(BF16)
    give_ref[0] = dot_nn(a_ref[half:], value).astype(BF16)


def wide_grad(flipped, values, first, count, chips):
    width, rows = flipped.shape
    hidden = values.shape[2]
    block = min(512, hidden)
    piece = SHAPE((count, width // 2, hidden), BF16)
    out = pl.BlockSpec((1, width // 2, block), lambda k, i: (k, 0, i))
    keep, give = pl.pallas_call(
        wide_grad_kernel,
        grid=(count, hidden // block),
        in_specs=[
            pl.BlockSpec((width, rows), lambda k, i: (0, 0)),
            pl.BlockSpec((1, rows, block), lambda k, i: (first + k, 0, i)),
        ],
        out_specs=[out, out],
        out_shape=[piece, piece],
        compiler_params=params(),
        cost_estimate=cost(2 * count * width * rows * hidden, 4 * count * width * hidden),
        name="wide_grad",
    )(flipped, values)
    shape = (count, chips, width // 2 // chips, hidden)
    return keep.reshape(shape), give.reshape(shape)


def head_grad_kernel(
    n_ref, g_ref, mixed_ref, dq_ref, dkv_ref, came_ref, sum_ref, keep_ref, give_ref
):
    half = n_ref.shape[0] // 2
    chips, _, deep, wide = keep_ref.shape
    total = (dkv_ref[...].astype(F32) + came_ref[...].astype(F32)).astype(BF16)
    sum_ref[...] = total
    pairs = ((n_ref, dq_ref[...]), (g_ref, mixed_ref[...]), (n_ref, total[0]), (n_ref, total[1]))
    for i, (left, right) in enumerate(pairs):
        for out, side in ((keep_ref, left[:half]), (give_ref, left[half:])):
            out[:, i] = dot_nn(side, right).astype(BF16).reshape(chips, deep, wide)


def head_grad(n_flip, g_flip, mixed, dq, dkv, came, chips):
    width, rows = n_flip.shape
    wide = dq.shape[1]
    piece = SHAPE((chips, 4, width // 2 // chips, wide), BF16)
    total, keep, give = pl.pallas_call(
        head_grad_kernel,
        in_specs=[WHOLE] * 6,
        out_specs=[WHOLE] * 3,
        out_shape=[SHAPE(dkv.shape, BF16), piece, piece],
        compiler_params=params(),
        cost_estimate=cost(8 * width * rows * wide, 8 * width * wide),
        name="head_grad",
    )(n_flip, g_flip, mixed, dq, dkv, came)
    return total, keep[None], give[None]


def first_back_kernel(nm, x_ref, gmid_ref, gain_ref, *refs):
    dqs, dkvs, came_ref = refs[:nm], refs[nm : 2 * nm], refs[2 * nm]
    qo_refs, kv_refs = refs[2 * nm + 1 : 2 * nm + 3], refs[2 * nm + 3 : 2 * nm + 5]
    out_ref, sums_ref = refs[2 * nm + 5 :]
    last = (dkvs[0][...].astype(F32) + came_ref[...].astype(F32)).astype(BF16)
    step = pl.program_id(0)
    half = x_ref.shape[1] // 2
    wide = dqs[0].shape[1]
    sides = []
    for side in range(2):
        total = 0.0
        for k in range(nm):
            total = total + dot_nt(dqs[k][...], qo_refs[side][:, k, 0].reshape(half, wide))
            for i in range(2):
                dkv = dkvs[k][i] if k else last[i]
                total = total + dot_nt(dkv, kv_refs[side][:, k, i].reshape(half, wide))
        sides.append(total)
    into, sums = norm_back(
        jnp.concatenate(sides, axis=1), x_ref[...].astype(F32), gain_ref[...]
    )
    out_ref[...] = (gmid_ref[...] + into).astype(BF16)

    @pl.when(step == 0)
    def _():
        sums_ref[...] = sums

    @pl.when(step > 0)
    def _():
        sums_ref[...] += sums


def first_back(x, gmid, gain, dqs, dkvs, came, qo, kv):
    rows, width = x.shape
    chips, nm, _, deep, wide = qo[0].shape
    block = row_block(rows)
    line = pl.BlockSpec((block, width), lambda i: (i, 0))
    q_spec = pl.BlockSpec((chips, nm, 1, deep, wide), lambda i: (0, 0, 0, 0, 0))
    kv_spec = pl.BlockSpec((chips, nm, 2, deep, wide), lambda i: (0, 0, 0, 0, 0))
    return pl.pallas_call(
        functools.partial(first_back_kernel, nm),
        grid=(rows // block,),
        in_specs=[line, line, pl.BlockSpec((1, width), lambda i: (0, 0))]
        + [pl.BlockSpec((block, wide), lambda i: (i, 0))] * nm
        + [pl.BlockSpec((2, block, wide), lambda i: (0, i, 0))] * (nm + 1)
        + [q_spec, q_spec, kv_spec, kv_spec],
        out_specs=[line, pl.BlockSpec((2, width), lambda i: (0, 0))],
        out_shape=[SHAPE((rows, width), BF16), SHAPE((2, width), F32)],
        compiler_params=params(),
        cost_estimate=cost(6 * rows * width * nm * wide, 12 * x.size),
        name="first_back",
    )(x, gmid, gain, *dqs, *dkvs, came, *qo, *kv)


def add_low(a, b):
    return (a.astype(F32) + b.astype(F32)).astype(BF16)


class Scatter:
    def __init__(self, nd, nm, bits):
        self.nd, self.nm = nd, nm
        self.queue = {1: [], **{bit: [] for bit in bits}, "direct": [], "z": []}
        self.order, self.kept, self.waits, self.flying = {}, {}, {}, {}
        self.ends, self.came, self.done, self.rings = {}, {}, {}, {}

    def add(self, name, ks, keep, give, order, rings=True):
        self.order[name, tuple(ks)], self.rings[name] = order, rings
        self.push(1, (name, tuple(ks), -1), list(range(0, self.nd, 2)), keep, give)

    def push(self, link, key, places, keep, give):
        self.kept[key], self.waits[key] = (places, keep), give
        self.queue[link].append(key)

    def launch(self, core=1, chip=1, direct=1, z=1):
        for link, tasks in self.queue.items():
            for _ in range({1: core, "direct": direct, "z": z}.get(link, chip)):
                if not tasks:
                    break
                key = tasks.pop(0)
                value = self.waits.pop(key)
                if link == "z" and isinstance(value, list):
                    value = [ring(part, -n - 1, self.nm) for n, part in enumerate(value)]
                elif link == "z":
                    value = ring(value, -1, self.nm)
                elif link == "direct":
                    value = [swap(part, 2 * n + 2, self.nd) for n, part in enumerate(value)]
                else:
                    value = swap(value, link, self.nd)
                self.flying[key] = value

    def busy(self):
        return bool(self.flying) or any(self.queue.values())

    def land(self, *extra):
        waits, flying = list(self.waits), list(self.flying)
        values = lax.optimization_barrier(
            ([self.waits[key] for key in waits], [self.flying[key] for key in flying], extra)
        )
        self.waits = dict(zip(waits, values[0]))
        came = dict(zip(flying, values[1]))
        self.flying = {}
        for key, value in came.items():
            self.arrive(key, value)
        extra = values[2]
        return extra[0] if len(extra) == 1 else extra

    def arrive(self, key, value):
        name, ks, stage = key
        if stage == "z" and not self.rings[name]:
            parts = [*self.ends.pop((name, 0)), *value]
            self.done[name] = sum(part.astype(F32) for part in parts)
            return
        if stage == "z":
            self.came[name, ks - 1] = value
            self.advance(name, ks - 1)
            return
        order = self.order[name, ks]
        places, keep = self.kept.pop(key)
        if order is None and stage == -1:
            parts = [add_low(keep[:, n], value[:, n]) for n in range(1, len(places))]
            own = (keep[:, 0], value[:, 0])
            self.push("direct", (name, ks, 0), own, None, parts)
            return
        if order is None:
            for n, k in enumerate(ks):
                self.ends[name, k] = tuple(part[n] for part in [*places, *value])
                self.advance(name, k)
            return
        if stage + 1 == len(order):
            for n, k in enumerate(ks):
                self.ends[name, k] = (keep[n, 0], value[n, 0])
            for k in reversed(ks):
                self.advance(name, k)
            return
        bit = order[stage + 1]
        stays = [n for n, j in enumerate(places) if not j & bit]
        goes = [n for n, j in enumerate(places) if j & bit]

        def take(array, which):
            return jnp.stack([array[:, n] for n in which], axis=1)

        self.push(
            bit,
            (name, ks, stage + 1),
            [places[n] for n in stays],
            add_low(take(keep, stays), take(value, stays)),
            add_low(take(keep, goes), take(value, goes)),
        )

    def advance(self, name, k):
        if not self.rings[name]:
            if all((name, k) in self.ends for k in range(self.nm)):
                key = (name, 0, "z")
                self.waits[key] = [
                    sum(part.astype(F32) for part in self.ends.pop((name, k))).astype(BF16)
                    for k in range(1, self.nm)
                ]
                self.queue["z"].append(key)
            return
        if (name, k) not in self.ends or (k < self.nm - 1 and (name, k) not in self.came):
            return
        total = sum(part.astype(F32) for part in self.ends.pop((name, k)))
        if k < self.nm - 1:
            total = total + self.came.pop((name, k)).astype(F32)
        if k:
            key = (name, k, "z")
            self.waits[key] = total.astype(BF16)
            self.queue["z"].append(key)
        else:
            self.done[name] = total


def shards(nd, nm, tokens, views, norm_gains, norm_biases, w_proj, w_out, w_up, w_down, cotangent):
    micro, _, chunk, width = tokens.shape
    ranks = nm // micro
    half = max(ranks // 2, 1)
    rows = micro * chunk
    chips = nd // 2
    wide = w_out.shape[2]
    per_k = wide // PAIR
    hidden = w_up.shape[2]
    dp, mp = lax.axis_index("dp"), lax.axis_index("mp")
    group = mp // half
    step_here = group // 2
    rank = (dp & 1) + 2 * (mp % half)
    order_of = [2 * (p % chips) + p // chips for p in range(nd)]
    offsets = jnp.asarray(order_of, jnp.int32)
    index = dp.astype(jnp.int32) ^ offsets

    def routes(k):
        pairs = []
        for d in range(nd):
            for z in range(nm):
                m = (k + z) % micro
                r = z // micro
                to_d = (d & ~1) | (r & 1)
                to_z = (2 * m + (d & 1)) * half + r // 2
                pairs.append((d * nm + z, to_d * nm + to_z))
        return pairs

    there = ((dp & ~1) | ((mp // micro) & 1)).astype(jnp.int32) ^ offsets

    def pack(value, k):
        return pack_features(value, there, (k + mp) % micro)

    def send(packed, k):
        return lax.ppermute(packed[k], ("dp", "mp"), routes(k))

    def send_chunk(chunks, k):
        return lax.ppermute(chunks[k], ("dp", "mp"), [(b, a) for a, b in routes(k)])

    def unpack(came):
        return unpack_features(came, there, [(k + mp) % micro for k in range(micro)])

    def by_place(vector):
        return jnp.take(vector.reshape(-1, nd, width // nd), index, axis=1).reshape(-1, width)

    flow = Flow(nd, nm)
    forth, back = flow.bits, flow.bits[::-1]
    groups = [[0], [1]] if nm > 1 else [[0]]
    groups += [list(range(k, min(k + 2, nm))) for k in range(2, nm, 2)]
    sizes = tuple(len(group) for group in groups)
    head = [jnp.concatenate([w_proj[0, :1], w_out, w_proj[0, 1:]])]
    feeds = [jnp.concatenate([w_up, w_down])]
    flow.add("up0", w_up, forth)
    flow.add("down0", w_down, back)
    for step in range(nm - 1):
        head.append(ring(head[-1], 1, nm))
        if step == 0:
            flow.launch()
            head, tokens, views, index, there = flow.land(head, tokens, views, index, there)
        elif step == 1:
            token_parts = [pack(tokens[:, 0], k) for k in range(micro)]
            head, token_parts, index = flow.land(head, token_parts, index)
        else:
            view = lax.dynamic_index_in_dim(views[:, 0], mp % micro, 0, keepdims=True)
            gains, biases = by_place(norm_gains[0]), by_place(norm_biases[0])
            head, view, gains, biases = flow.land(head, view, gains, biases)
    flow.add("qo", jnp.stack([h[:2] for h in head]), forth)
    flow.add("kv", jnp.stack([h[2:] for h in head]), back)
    flow.fly("view", lax.ppermute(view, ("dp", "mp"), routes(0)))
    came = []
    while not (flow.whole("qo") and flow.whole("kv") and len(came) == micro):
        flow.launch(chip=2)
        if len(came) < micro:
            came.append(send(token_parts, len(came)))
        if len(came) == 1:
            grad_parts = [pack(cotangent[:, 0], k) for k in range(micro)]
        came, token_parts, grad_parts, feeds = flow.land(came, token_parts, grad_parts, feeds)
    view = flow.kept.pop("view")

    def turn():
        if len(feeds) < nm:
            feeds.append(ring(feeds[-1], 1, nm))

    def turned():
        for n, group in enumerate(groups):
            if f"up{n}" not in flow.order and group[-1] < len(feeds):
                flow.add(f"up{n}", jnp.stack([feeds[k][0] for k in group]), forth)
                flow.add(f"down{n}", jnp.stack([feeds[k][1] for k in group]), back)

    last = [f"{name}{n}" for n in range(len(groups)) for name in ("up", "down")]
    halves = {}

    def core_halves(most):
        for name in last:
            if most and flow.whole(name):
                halves[name] = flow.take_half(name)
                flow.fly(name, swap(halves[name], 1, nd))
                most -= 1

    kv_own, qo_own = flow.take_half("kv"), flow.take_half("qo")
    slot = jnp.stack([(step_here - t) % micro for t in range(micro)])
    within = (slot[:, None] * chunk + jnp.arange(chunk)[None]).reshape(-1)
    position = jnp.stack([(rank ^ j) * rows + within for j in range(ranks)])
    bias = jnp.where(position < TRI + view[0] * VIEW_TOK, 0.0, -1.0).astype(F32)
    flow.fly("kv", swap(kv_own, 1, nd))
    turn()
    x, normed, n_flip = first_norm(came, gains[:1], biases[:1])
    x, normed, n_flip, bias, qo_own, kv_own, feeds = flow.land(
        x, normed, n_flip, bias, qo_own, kv_own, feeds
    )
    turned()
    kv = [kv_own, flow.kept.pop("kv")]

    flow.fly("qo", swap(qo_own, 1, nd))
    turn()
    flow.launch()
    own_kv = project(normed, kv[0], kv[1], 0, 2)
    own_kv, normed, qo_own, feeds = flow.land(own_kv, normed, qo_own, feeds)
    turned()
    qo = [qo_own, flow.kept.pop("qo")]

    def swap_rank(value, bit):
        if bit == 1:
            return swap(value, 1, nd)
        return lax.ppermute(value, "mp", [(i, i ^ (bit >> 1)) for i in range(nm)])

    rank_bits = [1 << b for b in range(ranks.bit_length() - 1)]
    kvs = {0: own_kv}
    for bit in rank_bits:
        for j in list(kvs):
            kvs[j | bit] = swap_rank(kvs[j], bit)
    kvs = [kvs[j] for j in range(ranks)]
    turn()
    flow.launch()
    query = project(normed, qo[0], qo[1], 0, 1)
    kvs, query, bias, grad_parts, feeds = flow.land(kvs, query, bias, grad_parts, feeds)
    turned()

    grad_came, mixed, lses = [], [], []
    at_once = max(nm // 2, 1)
    while len(mixed) < nm or len(grad_came) < micro or not all(
        name in halves or flow.whole(name) for name in last
    ):
        turn()
        flow.launch()
        if len(grad_came) < micro:
            grad_came.append(send(grad_parts, len(grad_came)))
        core_halves(2)
        for k in range(len(mixed), min(len(mixed) + at_once, nm)):
            part, lse = attend(query, kvs, bias, k * per_k, per_k)
            mixed.append(part)
            lses.append(lse)
        mixed, query, halves, grad_parts, grad_came, feeds = flow.land(
            mixed, query, halves, grad_parts, grad_came, feeds
        )
        turned()
    core_halves(len(last))
    middle, normed_two, flip_two = middle_norm(x, mixed, *qo, 1, gains[1:], biases[1:])
    grad, grad_flip = flip(grad_came)
    middle, normed_two, flip_two, halves, grad, grad_flip = flow.land(
        middle, normed_two, flip_two, halves, grad, grad_flip
    )
    weights = []
    for name in last:
        weights += [halves[name], flow.kept.pop(name)]

    result, active, slope = feed(normed_two, middle, sizes, weights)
    out_chunks = result.reshape((micro, chunk, width))
    output = []

    sums = Scatter(nd, nm, flow.bits)
    pairs = [list(range(k, min(k + 2, nm))) for k in range(0, nm, 2)][::-1]
    ways = [back[::-1], forth[::-1]]
    for ks in pairs:
        sums.launch(chip=0)
        pieces = wide_grad(grad_flip, active, ks[0], len(ks), chips)
        pieces, active, grad_flip, out_chunks, grad = sums.land(
            pieces, active, grad_flip, out_chunks, grad
        )
        sums.add("down", ks, *pieces, ways[0])
    sums.launch(core=2)
    output.append(send_chunk(out_chunks, 0))
    hid, gmid, attn, attn_flip, sums_two = feed_back(
        grad, slope, middle, gains[1:], sizes, weights
    )
    hid, gmid, attn, attn_flip, sums_two, flip_two, out_chunks, output = sums.land(
        hid, gmid, attn, attn_flip, sums_two, flip_two, out_chunks, output
    )
    sums.launch(core=0, direct=0, z=0)
    pieces = [wide_grad(flip_two, hid, ks[0], len(ks), chips) for ks in pairs]
    grad_mixed = project(attn, *qo, 1, 1)
    pieces, grad_mixed, query, out_chunks = sums.land(pieces, grad_mixed, query, out_chunks)
    for n, (ks, piece) in enumerate(zip(pairs, pieces)):
        sums.add("up", ks, *piece, ways[n % 2], rings=False)

    dqs, dkvs = {}, {}
    bias_tall = bias[:, :, None]
    closing = list(range(nm))
    dkv_part, dkv_came = {}, {}

    def head_grads():
        if not closing or closing[-1] not in dkv_came:
            return None
        k = closing.pop()
        dkvs[k], keep, give = head_grad(
            n_flip, attn_flip, mixed[k], dqs[k], dkv_part[k], dkv_came[k], chips
        )
        return k, (keep, give)

    def add_heads(ready, outs):
        sums.add("head", [ready[0]], outs[0], outs[1], None)

    def exchange(parts):
        parts = dict(enumerate(parts))
        came = None
        for bit in rank_bits[::-1]:
            if came is not None:
                parts = {j: add_low(part, came[j]) for j, part in parts.items()}
            came = {j ^ bit: swap_rank(parts.pop(j), bit) for j in list(parts) if j & bit}
        return parts[0], came[0]

    parts = None
    for k in list(reversed(range(nm))) + [-1]:
        if k == nm - 1:
            sums.launch(core=2)
        elif k >= 1:
            sums.launch(core=nm - 4, chip=1)
        elif k == 0:
            sums.launch()
        else:
            sums.launch(direct=0, z=0)
        if k >= 0 and len(output) < micro:
            output.append(send_chunk(out_chunks, len(output)))
        ready = head_grads()
        if parts is not None:
            dkv_part[k + 1], dkv_came[k + 1] = exchange(parts)
            parts = None
        if k >= 0:
            dqs[k], *parts = attend_back(
                query, kvs, bias_tall, lses[k], mixed[k], grad_mixed, k * per_k, per_k
            )
        live = (ready and ready[1], dqs, parts, query, dkv_part, dkv_came, dkvs, output, gmid)
        live = sums.land(*live)
        outs, dqs, parts, query, dkv_part, dkv_came, dkvs, output, gmid = live
        if ready:
            add_heads(ready, outs)

    sums.launch()
    first, sums_one = first_back(
        x,
        gmid,
        gains[:1],
        [dqs[k] for k in range(nm)],
        [dkvs.get(k, dkv_part[k]) for k in range(nm)],
        dkv_came[0],
        qo,
        kv,
    )
    first, sums_one, dkv_part, dkv_came = sums.land(first, sums_one, dkv_part, dkv_came)
    first = first.reshape((micro, chunk, width))
    vectors = jnp.take(
        jnp.concatenate([sums_one, sums_two]).reshape(4, nd, width // nd),
        jnp.argsort(index),
        axis=1,
    ).reshape(4, width)
    hops = [lambda value, bit=1 << b: swap(value, bit, nd) for b in range(nd.bit_length() - 1)]
    hops += [
        lambda value, bit=1 << b: lax.ppermute(value, "mp", [(i, i ^ bit) for i in range(nm)])
        for b in range(nm.bit_length() - 1)
    ]
    grad_tokens = []
    while sums.busy() or hops or len(grad_tokens) < micro:
        if len(grad_tokens) < micro:
            grad_tokens.append(send_chunk(first, len(grad_tokens)))
        sums.launch(direct=2)
        if len(grad_tokens) == micro:
            for _ in range(min(3, len(hops))):
                vectors = vectors + hops.pop(0)(vectors)
        ready = head_grads()
        grad_tokens, first, outs, vectors = sums.land(
            grad_tokens, first, ready and ready[1], vectors
        )
        if ready:
            add_heads(ready, outs)
    g_head, g_up, g_down = (sums.done[name] for name in ("head", "up", "down"))
    share = width // (nd * nm)
    vectors = lax.dynamic_slice_in_dim(vectors, (dp * nm + mp) * share, share, 1)
    return (
        unpack(output)[:, None],
        unpack(grad_tokens)[:, None],
        jnp.concatenate([g_head[:1], g_head[2:]])[None],
        g_head[1][None],
        g_up[None],
        g_down[None],
        jnp.stack([vectors[0], vectors[2]])[None],
        vectors[1][None],
        vectors[3][None],
    )


def solution(mesh):
    placed = (
        P(None, "dp", "mp", None),
        P(None, "dp"),
        P(),
        P(),
        P(None, None, "dp", "mp"),
        P(None, "dp", "mp"),
        P(None, "dp", "mp"),
        P(None, "dp", "mp"),
        P(None, "dp", "mp", None),
    )
    return jax.shard_map(
        functools.partial(shards, mesh.shape["dp"], mesh.shape["mp"]),
        mesh=mesh,
        in_specs=placed,
        out_specs=(
            P(None, "dp", "mp", None),
            P(None, "dp", "mp", None),
            P(None, None, "dp", "mp"),
            P(None, "dp", "mp"),
            P(None, "dp", "mp"),
            P(None, "dp", "mp"),
            P(None, None, ("dp", "mp")),
            P(None, ("dp", "mp")),
            P(None, ("dp", "mp")),
        ),
        check_vma=False,
    )
```

```python
import functools

import jax
import jax.numpy as jnp
from jax import lax
from jax.experimental import pallas as pl
from jax.experimental.pallas import tpu as pltpu
from jax.sharding import PartitionSpec as P

HDIM = 64
PAIR = 2 * HDIM
VIEW_TOK = 256
TRI = 768
EPSILON = 1e-05
MASKED = -1000000000.0
F32 = jnp.float32
BF16 = jnp.bfloat16
MIB = 1024 * 1024
ANY = pl.BlockSpec(memory_space=pl.ANY)
WHOLE = pl.BlockSpec(memory_space=pltpu.VMEM)
SHAPE = jax.ShapeDtypeStruct


def params(mib=56):
    return pltpu.CompilerParams(vmem_limit_bytes=mib * MIB)


def cost(flops, nbytes):
    return pl.CostEstimate(flops=int(flops), bytes_accessed=int(nbytes), transcendentals=0)


def dot_nt(a, b):
    return lax.dot_general(a, b, (((1,), (1,)), ((), ())), preferred_element_type=F32)


def dot_nn(a, b):
    return lax.dot_general(a, b, (((1,), (0,)), ((), ())), preferred_element_type=F32)


def dot_tn(a, b):
    return lax.dot_general(a, b, (((0,), (0,)), ((), ())), preferred_element_type=F32)


def row_block(rows):
    return 256 if rows % 256 == 0 else 128


def swap(value, bit, nd):
    return lax.ppermute(value, "dp", [(i, i ^ bit) for i in range(nd)])


def ring(value, step, nm):
    return lax.ppermute(value, "mp", [(i, (i + step) % nm) for i in range(nm)])


class Flow:
    def __init__(self, nd, nm):
        self.nd, self.nm = nd, nm
        self.bits = [1 << b for b in range(1, nd.bit_length() - 1)]
        self.queue = {bit: [] for bit in self.bits}
        self.order, self.pieces, self.flying, self.kept = {}, {}, {}, {}

    def add(self, name, value, order):
        self.order[name] = list(order)
        self.pieces[name] = [(0, value)]
        self.next(name)

    def next(self, name):
        if self.order[name]:
            self.queue[self.order[name][0]].append(name)

    def launch(self, chip=1, names=("",)):
        for bit, tasks in self.queue.items():
            for name in [name for name in tasks if name.startswith(names)][:chip]:
                tasks.remove(name)
                values = [value for _, value in self.pieces[name]]
                value = values[0][None] if len(values) == 1 else jnp.stack(values)
                self.flying["chip", name] = swap(value, bit, self.nd)

    def fly(self, name, value):
        self.flying["kept", name] = value

    def land(self, *extra):
        names, flying, kept = list(self.pieces), list(self.flying), list(self.kept)
        values = lax.optimization_barrier(
            (
                [self.pieces[name] for name in names],
                [self.flying[key] for key in flying],
                [self.kept[key] for key in kept],
                extra,
            )
        )
        for name, pieces in zip(names, values[0]):
            self.pieces[name] = [(j, v) for (j, _), (_, v) in zip(self.pieces[name], pieces)]
        self.kept = dict(zip(kept, values[2]))
        self.flying = {}
        for (kind, name), value in zip(flying, values[1]):
            if kind == "kept":
                self.kept[name] = value
                continue
            bit = self.order[name].pop(0)
            held = self.pieces[name]
            self.pieces[name] = held + [(j | bit, value[n]) for n, (j, _) in enumerate(held)]
            self.next(name)
        extra = values[3]
        return extra[0] if len(extra) == 1 else extra

    def whole(self, name):
        return name in self.pieces and not self.order[name]

    def take_half(self, name):
        pieces = dict(self.pieces.pop(name))
        return jnp.stack([pieces[2 * i] for i in range(self.nd // 2)])


def pack_kernel(index_ref, in_ref, out_ref):
    nd = index_ref.shape[0] - 1
    wide = in_ref.shape[2] // nd
    for p in range(nd):
        there = pl.ds(pl.multiple_of(index_ref[p] * wide, wide), wide)
        out_ref[:, p * wide : (p + 1) * wide] = in_ref[0, :, there]


def pack_features(value, index, which):
    micro, rows, width = value.shape
    nd = index.shape[0]
    if width // nd % 128:
        chunk = lax.dynamic_index_in_dim(value, which, 0, keepdims=False)
        return jnp.take(chunk.reshape(rows, nd, -1), index, axis=1).reshape(rows, width)
    return pl.pallas_call(
        pack_kernel,
        grid_spec=pltpu.PrefetchScalarGridSpec(
            num_scalar_prefetch=1,
            grid=(1,),
            in_specs=[pl.BlockSpec((1, rows, width), lambda i, index_ref: (index_ref[nd], 0, 0))],
            out_specs=pl.BlockSpec((rows, width), lambda i, index_ref: (0, 0)),
        ),
        out_shape=SHAPE((rows, width), value.dtype),
        compiler_params=params(),
        cost_estimate=cost(0, 6 * rows * width),
        name="pack_features",
    )(jnp.append(index, which.astype(jnp.int32)), value)


def unpack_kernel(index_ref, *refs):
    ins, out_ref = refs[:-1], refs[-1]
    nd = index_ref.shape[0] - len(ins)
    wide = out_ref.shape[2] // nd
    for k, in_ref in enumerate(ins):
        for p in range(nd):
            there = pl.ds(pl.multiple_of(index_ref[p] * wide, wide), wide)
            out_ref[index_ref[nd + k], :, there] = in_ref[:, p * wide : (p + 1) * wide]


def unpack_features(chunks, index, places):
    rows, width = chunks[0].shape
    micro, nd = len(chunks), index.shape[0]
    places = [place.astype(jnp.int32) for place in places]
    if width // nd % 128:
        back = jnp.argsort(index)
        stacked = jnp.stack(chunks).reshape(micro, rows, nd, -1)
        stacked = jnp.take(stacked, back, axis=2).reshape(micro, rows, width)
        return jnp.take(stacked, jnp.argsort(jnp.stack(places)), axis=0)
    return pl.pallas_call(
        unpack_kernel,
        in_specs=[pl.BlockSpec(memory_space=pltpu.SMEM)] + [WHOLE] * micro,
        out_specs=WHOLE,
        out_shape=SHAPE((micro, rows, width), chunks[0].dtype),
        compiler_params=params(),
        cost_estimate=cost(0, 4 * micro * rows * width),
        name="unpack_features",
    )(jnp.concatenate([index, jnp.stack(places)]), *chunks)


def standardize(state):
    centre = jnp.mean(state, axis=-1, keepdims=True)
    centred = state - centre
    spread = jnp.mean(centred * centred, axis=-1, keepdims=True)
    inverse = lax.rsqrt(spread + EPSILON)
    return centred * inverse, inverse


def norm_back(grad, state, gain):
    scaled, inverse = standardize(state)
    weighted = grad * gain
    first = jnp.mean(weighted, axis=-1, keepdims=True)
    second = jnp.mean(weighted * scaled, axis=-1, keepdims=True)
    sums = jnp.concatenate(
        [jnp.sum(grad * scaled, axis=0, keepdims=True), jnp.sum(grad, axis=0, keepdims=True)], 0
    )
    return inverse * (weighted - first - scaled * second), sums


def first_norm_kernel(micro, *refs):
    chunks = refs[:micro]
    gain_ref, bias_ref, x_ref, out_ref, flip_ref = refs[micro:]
    rows = chunks[0].shape[0]
    for k, ref in enumerate(chunks):
        here = slice(k * rows, (k + 1) * rows)
        x_ref[here] = ref[...]
        scaled, _ = standardize(ref[...].astype(F32))
        normed = (scaled * gain_ref[...] + bias_ref[...]).astype(BF16)
        out_ref[here] = normed
        flip_ref[:, here] = normed.T


def first_norm(chunks, gain, bias):
    rows, width = chunks[0].shape
    rows = rows * len(chunks)
    return pl.pallas_call(
        functools.partial(first_norm_kernel, len(chunks)),
        in_specs=[WHOLE] * (len(chunks) + 2),
        out_specs=[WHOLE] * 3,
        out_shape=[SHAPE((rows, width), BF16)] * 2 + [SHAPE((width, rows), BF16)],
        compiler_params=params(),
        cost_estimate=cost(0, 10 * rows * width),
        name="first_norm",
    )(*chunks, gain, bias)


def flip_kernel(*refs):
    chunks, out_ref, flip_ref = refs[:-2], refs[-2], refs[-1]
    rows = chunks[0].shape[0]
    for k, ref in enumerate(chunks):
        here = slice(k * rows, (k + 1) * rows)
        out_ref[here] = ref[...]
        flip_ref[:, here] = ref[...].T


def flip(chunks):
    rows, width = chunks[0].shape
    rows = rows * len(chunks)
    return pl.pallas_call(
        flip_kernel,
        in_specs=[WHOLE] * len(chunks),
        out_specs=[WHOLE] * 2,
        out_shape=[SHAPE((rows, width), BF16), SHAPE((width, rows), BF16)],
        compiler_params=params(),
        cost_estimate=cost(0, 6 * rows * width),
        name="flip",
    )(*chunks)


def each_k(refs):
    return [(ref, n) for ref in refs for n in range(ref.shape[1])]


def proj_kernel(parts, in_ref, *refs):
    owns, others, out_ref = refs[:parts], refs[parts : 2 * parts], refs[-1]
    value = in_ref[...]
    half = value.shape[1] // 2
    wide = owns[0].shape[-1]
    for k, ((own, n), (other, _)) in enumerate(zip(each_k(owns), each_k(others))):
        first = own[:, n, 0].reshape(half, wide)
        second = other[:, n, 0].reshape(half, wide)
        total = dot_nn(value[:, :half], first) + dot_nn(value[:, half:], second)
        out_ref[0, :, k * wide : (k + 1) * wide] = total.astype(BF16)


def head_spec(array, count, index_map):
    chips, ks, _, deep, wide = array.shape
    return pl.BlockSpec((chips, ks, count, deep, wide), index_map)


def project(value, weights, start, count):
    rows, width = value.shape
    wide = weights[0][0].shape[-1]
    nm = sum(array.shape[1] for array in weights[0])
    arrays = [*weights[0], *weights[1]]
    return pl.pallas_call(
        functools.partial(proj_kernel, len(weights[0])),
        grid=(count,),
        in_specs=[pl.BlockSpec((rows, width), lambda i: (0, 0))]
        + [head_spec(array, 1, lambda i: (0, 0, start + i, 0, 0)) for array in arrays],
        out_specs=pl.BlockSpec((1, rows, nm * wide), lambda i: (i, 0, 0)),
        out_shape=SHAPE((count, rows, nm * wide), BF16),
        compiler_params=params(),
        cost_estimate=cost(2 * count * rows * width * nm * wide, 2 * count * rows * width),
        name="project",
    )(value, *arrays)


def attend_kernel(parts, q_ref, *refs):
    k_refs, v_refs = refs[:parts], refs[parts : 2 * parts]
    bias_ref, out_ref, lse_ref = refs[2 * parts :]
    rows = q_ref.shape[1]
    low = lax.broadcasted_iota(jnp.int32, (1, PAIR), 1) < HDIM
    query = q_ref[0] * jnp.asarray(HDIM ** (-0.5), BF16)
    mixed = None
    for head in range(2):
        mine = low if head == 0 else jnp.logical_not(low)
        q_mine = jnp.where(mine, query, jnp.zeros_like(query))
        scores = [
            jnp.where(bias_ref[p : p + 1, :] < 0.0, MASKED, dot_nt(q_mine, k_refs[p][0]))
            for p in range(parts)
        ]
        top = functools.reduce(
            jnp.maximum, [jnp.max(part, axis=1, keepdims=True) for part in scores]
        )
        total, part = 0.0, 0.0
        for p in range(parts):
            expo = jnp.exp(scores[p] - top)
            total = total + jnp.sum(expo, axis=1, keepdims=True)
            part = part + dot_nn(expo.astype(BF16), v_refs[p][0])
        part = part / total
        mixed = part if head == 0 else jnp.where(low, mixed, part)
        lse = top + jnp.log(total)
        lse_ref[0, head : head + 1, :] = jnp.transpose(jnp.broadcast_to(lse, (rows, 128)))[0:1, :]
    out_ref[...] = mixed.astype(BF16)


def attend(query, kvs, bias, start, count):
    _, rows, width = query.shape
    parts = len(kvs)
    block = row_block(rows)
    keys = rows * parts
    key_spec = pl.BlockSpec((1, rows, PAIR), lambda h, i: (0, 0, start + h))
    value_spec = pl.BlockSpec((1, rows, PAIR), lambda h, i: (1, 0, start + h))
    return pl.pallas_call(
        functools.partial(attend_kernel, parts),
        grid=(count, rows // block),
        in_specs=[pl.BlockSpec((1, block, PAIR), lambda h, i: (0, i, start + h))]
        + [key_spec] * parts
        + [value_spec] * parts
        + [pl.BlockSpec((parts, rows), lambda h, i: (0, 0))],
        out_specs=[
            pl.BlockSpec((block, PAIR), lambda h, i: (i, h)),
            pl.BlockSpec((1, 2, block), lambda h, i: (h, 0, i)),
        ],
        out_shape=[SHAPE((rows, count * PAIR), BF16), SHAPE((count, 2, rows), F32)],
        compiler_params=params(),
        cost_estimate=cost(16 * rows * keys * count * PAIR, 8 * keys * count * PAIR),
        name="attend",
    )(query, *kvs, *kvs, bias)


def attend_back_kernel(parts, q_ref, *refs):
    k_refs, v_refs = refs[:parts], refs[parts : 2 * parts]
    bias_ref, lse_ref, mixed_ref, grad_ref, dq_ref = refs[2 * parts : 2 * parts + 5]
    dkv_refs = refs[2 * parts + 5 : 3 * parts + 5]
    dk_acc, dv_acc = refs[3 * parts + 5 :]
    step = pl.program_id(1)
    low = lax.broadcasted_iota(jnp.int32, (1, PAIR), 1) < HDIM
    query = q_ref[0] * jnp.asarray(HDIM ** (-0.5), BF16)
    grad = grad_ref[0]
    product = mixed_ref[...].astype(F32) * grad.astype(F32)

    @pl.when(step == 0)
    def _():
        dk_acc[...] = jnp.zeros_like(dk_acc)
        dv_acc[...] = jnp.zeros_like(dv_acc)

    grad_query = None
    for head in range(2):
        mine = low if head == 0 else jnp.logical_not(low)
        q_mine = jnp.where(mine, query, jnp.zeros_like(query))
        g_mine = jnp.where(mine, grad, jnp.zeros_like(grad))
        delta = jnp.sum(jnp.where(mine, product, 0.0), axis=1, keepdims=True)
        delta = jnp.transpose(jnp.broadcast_to(delta, (delta.shape[0], 128)))[0:1, :]
        query_part = 0.0
        for p in range(parts):
            keys, values = k_refs[p][0], v_refs[p][0]
            scores = jnp.where(bias_ref[p] < 0.0, MASKED, dot_nt(keys, q_mine))
            probs = jnp.exp(scores - lse_ref[0, head : head + 1, :])
            upstream = dot_nt(values, g_mine)
            grad_scores = (probs * (upstream - delta)).astype(BF16)
            dv_acc[p] += dot_nn(probs.astype(BF16), g_mine)
            dk_acc[p] += dot_nn(grad_scores, q_mine)
            query_part = query_part + dot_tn(grad_scores, keys)
        grad_query = query_part if head == 0 else jnp.where(low, grad_query, query_part)
    dq_ref[...] = (grad_query * HDIM ** (-0.5)).astype(BF16)

    @pl.when(step == pl.num_programs(1) - 1)
    def _():
        for p in range(parts):
            dkv_refs[p][0] = dk_acc[p].astype(BF16)
            dkv_refs[p][1] = dv_acc[p].astype(BF16)


def attend_back(query, kvs, bias, lse, mixed, grad, start, count):
    _, rows, width = query.shape
    parts = len(kvs)
    block = row_block(rows)
    keys = rows * parts
    key_spec = pl.BlockSpec((1, rows, PAIR), lambda h, i: (0, 0, start + h))
    value_spec = pl.BlockSpec((1, rows, PAIR), lambda h, i: (1, 0, start + h))
    return pl.pallas_call(
        functools.partial(attend_back_kernel, parts),
        grid=(count, rows // block),
        in_specs=[pl.BlockSpec((1, block, PAIR), lambda h, i: (0, i, start + h))]
        + [key_spec] * parts
        + [value_spec] * parts
        + [
            pl.BlockSpec((parts, rows, 1), lambda h, i: (0, 0, 0)),
            pl.BlockSpec((1, 2, block), lambda h, i: (h, 0, i)),
            pl.BlockSpec((block, PAIR), lambda h, i: (i, h)),
            pl.BlockSpec((1, block, PAIR), lambda h, i: (0, i, start + h)),
        ],
        out_specs=[pl.BlockSpec((block, PAIR), lambda h, i: (i, h))]
        + [pl.BlockSpec((2, rows, PAIR), lambda h, i: (0, 0, h))] * parts,
        out_shape=[SHAPE((rows, count * PAIR), BF16)]
        + [SHAPE((2, rows, count * PAIR), BF16)] * parts,
        scratch_shapes=[pltpu.VMEM((parts, rows, PAIR), F32)] * 2,
        compiler_params=params(),
        cost_estimate=cost(40 * rows * keys * count * PAIR, 16 * keys * count * PAIR),
        name="attend_back",
    )(query, *kvs, *kvs, bias, lse, mixed, grad)


def middle_kernel(nm, parts, x_ref, *refs):
    mixed_refs, refs = refs[:nm], refs[nm:]
    weights = refs[:parts], refs[parts : 2 * parts]
    gain_ref, bias_ref, mid_ref, out_ref, flip_ref = refs[2 * parts :]
    half = x_ref.shape[1] // 2
    sides = []
    for side in weights:
        total = 0.0
        for k, (ref, n) in enumerate(each_k(side)):
            total = total + dot_nt(mixed_refs[k][...], ref[:, n, 0].reshape(half, -1))
        sides.append(total)
    middle = x_ref[...].astype(F32) + jnp.concatenate(sides, axis=1)
    mid_ref[...] = middle
    scaled, _ = standardize(middle)
    normed = (scaled * gain_ref[...] + bias_ref[...]).astype(BF16)
    out_ref[...] = normed
    flip_ref[...] = normed.T


def middle_norm(x, mixed, weights, which, gain, bias):
    rows, width = x.shape
    nm, wide = len(mixed), mixed[0].shape[1]
    block = row_block(rows)
    vector = pl.BlockSpec((1, width), lambda i: (0, 0))
    line = pl.BlockSpec((block, width), lambda i: (i, 0))
    arrays = [*weights[0], *weights[1]]
    return pl.pallas_call(
        functools.partial(middle_kernel, nm, len(weights[0])),
        grid=(rows // block,),
        in_specs=[line]
        + [pl.BlockSpec((block, wide), lambda i: (i, 0))] * nm
        + [head_spec(array, 1, lambda i: (0, 0, which, 0, 0)) for array in arrays]
        + [vector, vector],
        out_specs=[line, line, pl.BlockSpec((width, block), lambda i: (0, i))],
        out_shape=[
            SHAPE((rows, width), F32),
            SHAPE((rows, width), BF16),
            SHAPE((width, rows), BF16),
        ],
        compiler_params=params(),
        cost_estimate=cost(2 * rows * width * nm * wide, 14 * x.size),
        name="middle_norm",
    )(x, *mixed, *arrays, gain, bias)


def load_weights(firsts, sizes, index_ref, refs, held, sems):
    step = pl.program_id(0)
    nm = firsts + sum(sizes)
    chips = held.shape[2]
    copies, refs = {k: [] for k in range(nm)}, list(refs)

    def add(k, source, w, side, n, sem):
        copies[k].append(
            pltpu.make_async_copy(source, held.at[w, 2 * k + side, n], sems.at[w, 2 * k + side, sem])
        )

    for k in range(firsts):
        ref = refs.pop(0)
        for w in range(2):
            for side in range(2):
                for n in range(chips):
                    add(k, ref.at[index_ref[side * chips + n], w], w, side, n, n)
    k = firsts
    for size in sizes:
        sides = [refs.pop(0) for _ in range(4)]
        for i in range(size):
            for n, ref in enumerate(sides):
                add(k, ref.at[:, i], n // 2, n % 2, slice(None), 0)
            k += 1

    @pl.when(step == 0)
    def _():
        for k in range(nm):
            for copy in copies[k]:
                copy.start()

    for k in range(nm):

        @pl.when(step == k)
        def _():
            for copy in copies[k]:
                copy.wait()


def feed_kernel(firsts, sizes, index_ref, *refs):
    nm, count = firsts + sum(sizes), firsts + 4 * len(sizes)
    in_ref, mid_ref, out_ref, act_ref, slope_ref, held, acc, sems = refs[count:]
    step = pl.program_id(0)
    load_weights(firsts, sizes, index_ref, refs[:count], held, sems)
    half = in_ref.shape[1] // 2
    up = [held[0, 2 * step + side].reshape(half, -1) for side in range(2)]
    down = [held[1, 2 * step + side].reshape(half, -1) for side in range(2)]

    @pl.when(step == 0)
    def _():
        acc[...] = mid_ref[...]

    hidden = dot_nn(in_ref[:, :half], up[0]) + dot_nn(in_ref[:, half:], up[1])
    below = 0.5 + 0.5 * lax.erf(hidden * (0.5**0.5))
    density = jnp.exp(-0.5 * hidden * hidden) * 0.3989422804014327
    active = (hidden * below).astype(BF16)
    act_ref[0] = active
    slope_ref[0] = (below + hidden * density).astype(BF16)
    acc[:, :half] += dot_nt(active, down[0])
    acc[:, half:] += dot_nt(active, down[1])

    @pl.when(step == nm - 1)
    def _():
        out_ref[...] = acc[...].astype(BF16)


def feed(normed, middle, index, firsts, sizes, weights):
    rows, width = normed.shape
    nm = firsts + sum(sizes)
    nd, (deep, hidden) = index.shape[0], weights[0].shape[2:]
    chips = nd // 2
    line = pl.BlockSpec((rows, width), lambda k: (0, 0))
    wide = pl.BlockSpec((1, rows, hidden), lambda k: (k, 0, 0))
    return pl.pallas_call(
        functools.partial(feed_kernel, firsts, sizes),
        grid=(nm,),
        in_specs=[pl.BlockSpec(memory_space=pltpu.SMEM)]
        + [ANY] * len(weights)
        + [line, line],
        out_specs=[line, wide, wide],
        out_shape=[SHAPE((rows, width), BF16)] + [SHAPE((nm, rows, hidden), BF16)] * 2,
        scratch_shapes=[
            pltpu.VMEM((2, 2 * nm, chips, deep, hidden), BF16),
            pltpu.VMEM((rows, width), F32),
            pltpu.SemaphoreType.DMA((2, 2 * nm, chips)),
        ],
        compiler_params=params(60),
        cost_estimate=cost(4 * rows * width * nm * hidden, 4 * nm * width * hidden),
        name="feed",
    )(index, *weights, normed, middle)


def feed_back_kernel(firsts, sizes, index_ref, *refs):
    nm, count = firsts + sum(sizes), firsts + 4 * len(sizes)
    g_ref, slope_ref, mid_ref, gain_ref = refs[count : count + 4]
    hid_ref, gmid_ref, attn_ref, flip_ref, sums_ref, held, acc, sems = refs[count + 4 :]
    step = pl.program_id(0)
    load_weights(firsts, sizes, index_ref, refs[:count], held, sems)
    half = g_ref.shape[1] // 2
    up = [held[0, 2 * step + side].reshape(half, -1) for side in range(2)]
    down = [held[1, 2 * step + side].reshape(half, -1) for side in range(2)]
    active = dot_nn(g_ref[:, :half], down[0]) + dot_nn(g_ref[:, half:], down[1])
    hidden = (active * slope_ref[0].astype(F32)).astype(BF16)
    hid_ref[0] = hidden
    first, second = dot_nt(hidden, up[0]), dot_nt(hidden, up[1])

    @pl.when(step == 0)
    def _():
        acc[:, :half] = first
        acc[:, half:] = second

    @pl.when(step > 0)
    def _():
        acc[:, :half] += first
        acc[:, half:] += second

    @pl.when(step == nm - 1)
    def _():
        into, sums = norm_back(acc[...], mid_ref[...], gain_ref[...])
        result = g_ref[...].astype(F32) + into
        gmid_ref[...] = result
        attn = result.astype(BF16)
        attn_ref[...] = attn
        flip_ref[...] = attn.T
        sums_ref[...] = sums


def feed_back(grad, slope, middle, gain, index, firsts, sizes, weights):
    rows, width = grad.shape
    nm = firsts + sum(sizes)
    nd, (deep, hidden) = index.shape[0], weights[0].shape[2:]
    chips = nd // 2
    line = pl.BlockSpec((rows, width), lambda k: (0, 0))
    wide = pl.BlockSpec((1, rows, hidden), lambda k: (k, 0, 0))
    return pl.pallas_call(
        functools.partial(feed_back_kernel, firsts, sizes),
        grid=(nm,),
        in_specs=[pl.BlockSpec(memory_space=pltpu.SMEM)]
        + [ANY] * len(weights)
        + [line, wide, line, pl.BlockSpec((1, width), lambda k: (0, 0))],
        out_specs=[
            wide,
            line,
            line,
            pl.BlockSpec((width, rows), lambda k: (0, 0)),
            pl.BlockSpec((2, width), lambda k: (0, 0)),
        ],
        out_shape=[
            SHAPE((nm, rows, hidden), BF16),
            SHAPE((rows, width), F32),
            SHAPE((rows, width), BF16),
            SHAPE((width, rows), BF16),
            SHAPE((2, width), F32),
        ],
        scratch_shapes=[
            pltpu.VMEM((2, 2 * nm, chips, deep, hidden), BF16),
            pltpu.VMEM((rows, width), F32),
            pltpu.SemaphoreType.DMA((2, 2 * nm, chips)),
        ],
        compiler_params=params(60),
        cost_estimate=cost(4 * rows * width * nm * hidden, 4 * nm * width * hidden),
        name="feed_back",
    )(index, *weights, grad, slope, middle, gain)


def wide_grad_kernel(index_ref, a_ref, b_ref, out_ref):
    part = dot_nn(a_ref[...], b_ref[0]).astype(BF16)
    nd, deep = out_ref.shape[0], out_ref.shape[2]
    for p in range(nd):
        out_ref[index_ref[p], 0] = part[p * deep : (p + 1) * deep]


def wide_grad(flipped, values, index):
    width, rows = flipped.shape
    nm, _, hidden = values.shape
    nd = index.shape[0]
    block = min(512, hidden)
    return pl.pallas_call(
        wide_grad_kernel,
        grid=(nm, hidden // block),
        in_specs=[
            pl.BlockSpec(memory_space=pltpu.SMEM),
            pl.BlockSpec((width, rows), lambda k, i: (0, 0)),
            pl.BlockSpec((1, rows, block), lambda k, i: (k, 0, i)),
        ],
        out_specs=pl.BlockSpec((nd, 1, width // nd, block), lambda k, i: (0, k, 0, i)),
        out_shape=SHAPE((nd, nm, width // nd, hidden), BF16),
        compiler_params=params(),
        cost_estimate=cost(2 * nm * width * rows * hidden, 4 * nm * width * hidden),
        name="wide_grad",
    )(index, flipped, values)


def head_grad_kernel(
    n_ref, g_ref, mixed_ref, dq_ref, dkv_ref, came_ref, sum_ref, keep_ref, give_ref
):
    half = n_ref.shape[0] // 2
    chips, _, deep, wide = keep_ref.shape
    total = (dkv_ref[...].astype(F32) + came_ref[...].astype(F32)).astype(BF16)
    sum_ref[...] = total
    pairs = ((n_ref, dq_ref[...]), (g_ref, mixed_ref[...]), (n_ref, total[0]), (n_ref, total[1]))
    for i, (left, right) in enumerate(pairs):
        for out, side in ((keep_ref, left[:half]), (give_ref, left[half:])):
            out[:, i] = dot_nn(side, right).astype(BF16).reshape(chips, deep, wide)


def head_grad(n_flip, g_flip, mixed, dq, dkv, came, chips):
    width, rows = n_flip.shape
    wide = dq.shape[1]
    piece = SHAPE((chips, 4, width // 2 // chips, wide), BF16)
    total, keep, give = pl.pallas_call(
        head_grad_kernel,
        in_specs=[WHOLE] * 6,
        out_specs=[WHOLE] * 3,
        out_shape=[SHAPE(dkv.shape, BF16), piece, piece],
        compiler_params=params(),
        cost_estimate=cost(8 * width * rows * wide, 8 * width * wide),
        name="head_grad",
    )(n_flip, g_flip, mixed, dq, dkv, came)
    return total, keep[None], give[None]


def first_back_kernel(nm, parts, x_ref, gmid_ref, gain_ref, *refs):
    dqs, dkvs, came_ref, refs = refs[:nm], refs[nm : 2 * nm], refs[2 * nm], refs[2 * nm + 1 :]
    qo = refs[:parts], refs[parts : 2 * parts]
    kv = refs[2 * parts : 3 * parts], refs[3 * parts : 4 * parts]
    out_ref, sums_ref = refs[4 * parts :]
    last = (dkvs[0][...].astype(F32) + came_ref[...].astype(F32)).astype(BF16)
    step = pl.program_id(0)
    half = x_ref.shape[1] // 2
    sides = []
    for side in range(2):
        total = 0.0
        for k, ((qo_ref, n), (kv_ref, _)) in enumerate(zip(each_k(qo[side]), each_k(kv[side]))):
            total = total + dot_nt(dqs[k][...], qo_ref[:, n, 0].reshape(half, -1))
            for i in range(2):
                dkv = dkvs[k][i] if k else last[i]
                total = total + dot_nt(dkv, kv_ref[:, n, i].reshape(half, -1))
        sides.append(total)
    into, sums = norm_back(jnp.concatenate(sides, axis=1), x_ref[...].astype(F32), gain_ref[...])
    out_ref[...] = (gmid_ref[...] + into).astype(BF16)

    @pl.when(step == 0)
    def _():
        sums_ref[...] = sums

    @pl.when(step > 0)
    def _():
        sums_ref[...] += sums


def first_back(x, gmid, gain, dqs, dkvs, came, qo, kv):
    rows, width = x.shape
    nm, wide = len(dqs), dqs[0].shape[1]
    block = row_block(rows)
    line = pl.BlockSpec((block, width), lambda i: (i, 0))
    still = lambda i: (0, 0, 0, 0, 0)
    qo_arrays, kv_arrays = [*qo[0], *qo[1]], [*kv[0], *kv[1]]
    return pl.pallas_call(
        functools.partial(first_back_kernel, nm, len(qo[0])),
        grid=(rows // block,),
        in_specs=[line, line, pl.BlockSpec((1, width), lambda i: (0, 0))]
        + [pl.BlockSpec((block, wide), lambda i: (i, 0))] * nm
        + [pl.BlockSpec((2, block, wide), lambda i: (0, i, 0))] * (nm + 1)
        + [head_spec(array, 1, still) for array in qo_arrays]
        + [head_spec(array, 2, still) for array in kv_arrays],
        out_specs=[line, pl.BlockSpec((2, width), lambda i: (0, 0))],
        out_shape=[SHAPE((rows, width), BF16), SHAPE((2, width), F32)],
        compiler_params=params(),
        cost_estimate=cost(6 * rows * width * nm * wide, 12 * x.size),
        name="first_back",
    )(x, gmid, gain, *dqs, *dkvs, came, *qo_arrays, *kv_arrays)


def add_low(a, b):
    return (a.astype(F32) + b.astype(F32)).astype(BF16)


def add_parts_kernel(keep_ref, came_ref, *outs):
    for n, out in enumerate(outs):
        out[...] = add_low(keep_ref[:, n + 1], came_ref[:, n + 1])


def add_parts(keep, came):
    count = keep.shape[1] - 1
    piece = SHAPE(keep.shape[:1] + keep.shape[2:], keep.dtype)
    return pl.pallas_call(
        add_parts_kernel,
        in_specs=[WHOLE] * 2,
        out_specs=[WHOLE] * count,
        out_shape=[piece] * count,
        compiler_params=params(),
        cost_estimate=cost(0, 6 * keep.size),
        name="add_parts",
    )(keep, came)


class Scatter:
    def __init__(self, nd, nm, bits):
        self.nd, self.nm = nd, nm
        self.queue = {1: [], **{bit: [] for bit in bits}, "direct": [], "z": []}
        self.order, self.kept, self.waits, self.flying = {}, {}, {}, {}
        self.ends, self.came, self.done, self.rings, self.joined = {}, {}, {}, {}, {}

    def add(self, name, ks, keep, give, order, rings=True):
        self.order[name, tuple(ks)], self.rings[name] = order, rings
        self.push(1, (name, tuple(ks), -1), list(range(0, self.nd, 2)), keep, give)

    def add_line(self, name, value, rings):
        self.rings[name] = rings
        for k in range(self.nm):
            self.ends[name, k] = (value[k],)
        self.advance(name, self.nm - 1)

    def push(self, link, key, places, keep, give):
        self.kept[key], self.waits[key] = (places, keep), give
        self.queue[link].append(key)

    def launch(self, core=1, chip=1, direct=1, z=1):
        for link, tasks in self.queue.items():
            for _ in range({1: core, "direct": direct, "z": z}.get(link, chip)):
                if not tasks:
                    break
                key = tasks.pop(0)
                value = self.waits.pop(key)
                if link == "z" and isinstance(value, list):
                    value = [ring(part, -n - 1, self.nm) for n, part in enumerate(value)]
                elif link == "z":
                    value = ring(value, -1, self.nm)
                elif link == "direct":
                    more = [tasks.pop(0) for _ in range(min(direct - 1, len(tasks)))]
                    self.joined[key] = more
                    values = [value] + [self.waits.pop(other) for other in more]
                    value = [jnp.concatenate(parts) for parts in zip(*values)]
                    value = [swap(part, 2 * n + 2, self.nd) for n, part in enumerate(value)]
                    self.flying[key] = value
                    break
                else:
                    value = swap(value, link, self.nd)
                self.flying[key] = value

    def busy(self):
        return bool(self.flying) or any(self.queue.values())

    def land(self, *extra):
        waits, flying = list(self.waits), list(self.flying)
        values = lax.optimization_barrier(
            ([self.waits[key] for key in waits], [self.flying[key] for key in flying], extra)
        )
        self.waits = dict(zip(waits, values[0]))
        came = dict(zip(flying, values[1]))
        self.flying = {}
        for key, value in came.items():
            for other in [key] + self.joined.pop(key, []):
                mine = len(other[1]) if isinstance(value, list) and other[2] != "z" else None
                self.arrive(other, value if mine is None else [part[:mine] for part in value])
                value = value if mine is None else [part[mine:] for part in value]
        extra = values[2]
        return extra[0] if len(extra) == 1 else extra

    def arrive(self, key, value):
        name, ks, stage = key
        if stage == "z" and not self.rings[name]:
            parts = [*self.ends.pop((name, 0)), *value]
            self.done[name] = sum(part.astype(F32) for part in parts)
            return
        if stage == "z":
            self.came[name, ks - 1] = value
            self.advance(name, ks - 1)
            return
        order = self.order[name, ks]
        places, keep = self.kept.pop(key)
        if order is None and stage == -1:
            parts = list(add_parts(keep, value))
            own = (keep[:, 0], value[:, 0])
            self.push("direct", (name, ks, 0), own, None, parts)
            return
        if order is None:
            for n, k in enumerate(ks):
                self.ends[name, k] = tuple(part[n] for part in [*places, *value])
                self.advance(name, k)
            return
        if stage + 1 == len(order):
            for n, k in enumerate(ks):
                self.ends[name, k] = (keep[n, 0], value[n, 0])
            for k in reversed(ks):
                self.advance(name, k)
            return
        bit = order[stage + 1]
        stays = [n for n, j in enumerate(places) if not j & bit]
        goes = [n for n, j in enumerate(places) if j & bit]

        def take(array, which):
            return jnp.stack([array[:, n] for n in which], axis=1)

        self.push(
            bit,
            (name, ks, stage + 1),
            [places[n] for n in stays],
            add_low(take(keep, stays), take(value, stays)),
            add_low(take(keep, goes), take(value, goes)),
        )

    def advance(self, name, k):
        if not self.rings[name]:
            if all((name, k) in self.ends for k in range(self.nm)):
                key = (name, 0, "z")
                self.waits[key] = [
                    sum(part.astype(F32) for part in self.ends.pop((name, k))).astype(BF16)
                    for k in range(1, self.nm)
                ]
                self.queue["z"].append(key)
            return
        if (name, k) not in self.ends or (k < self.nm - 1 and (name, k) not in self.came):
            return
        total = sum(part.astype(F32) for part in self.ends.pop((name, k)))
        if k < self.nm - 1:
            total = total + self.came.pop((name, k)).astype(F32)
        if k:
            key = (name, k, "z")
            self.waits[key] = total.astype(BF16)
            self.queue["z"].append(key)
        else:
            self.done[name] = total


def shards(nd, nm, tokens, views, norm_gains, norm_biases, w_proj, w_out, w_up, w_down, cotangent):
    micro, _, chunk, width = tokens.shape
    ranks = nm // micro
    half = max(ranks // 2, 1)
    rows = micro * chunk
    chips = nd // 2
    wide = w_out.shape[2]
    per_k = wide // PAIR
    hidden = w_up.shape[2]
    dp, mp = lax.axis_index("dp"), lax.axis_index("mp")
    group = mp // half
    step_here = group // 2
    rank = (dp & 1) + 2 * (mp % half)
    order_of = [2 * (p % chips) + p // chips for p in range(nd)]
    offsets = jnp.asarray(order_of, jnp.int32)
    index = dp.astype(jnp.int32) ^ offsets

    def routes(k):
        pairs = []
        for d in range(nd):
            for z in range(nm):
                m = (k + z) % micro
                r = z // micro
                to_d = (d & ~1) | (r & 1)
                to_z = (2 * m + (d & 1)) * half + r // 2
                pairs.append((d * nm + z, to_d * nm + to_z))
        return pairs

    there = ((dp & ~1) | ((mp // micro) & 1)).astype(jnp.int32) ^ offsets

    def pack(value, k):
        return pack_features(value, there, (k + mp) % micro)

    def send(packed, k):
        return lax.ppermute(packed[k], ("dp", "mp"), routes(k))

    def send_chunk(chunks, k):
        return lax.ppermute(chunks[k], ("dp", "mp"), [(b, a) for a, b in routes(k)])

    def unpack(came):
        return unpack_features(came, there, [(k + mp) % micro for k in range(micro)])

    def by_place(vector):
        return jnp.take(vector.reshape(-1, nd, width // nd), index, axis=1).reshape(-1, width)

    flow = Flow(nd, nm)
    forth, back = flow.bits, flow.bits[::-1]
    firsts = min(2, nm)
    groups = [list(range(k, min(k + 2, nm))) for k in range(firsts, nm, 2)]
    sizes = tuple(len(group) for group in groups)
    head = [jnp.concatenate([w_proj[0, :1], w_out, w_proj[0, 1:]])]
    feeds = [jnp.concatenate([w_up, w_down])]
    gather = functools.partial(lax.all_gather, axis_name="dp")
    cut = max(nm // 2, 1)
    head_groups = [list(range(0, cut)), list(range(cut, nm))] if nm > 1 else [[0]]

    def headed():
        for n, group in enumerate(head_groups):
            if f"qo{n}" not in flow.order and group[-1] < len(head):
                flow.add(f"qo{n}", jnp.stack([head[k][:2] for k in group]), forth)
                flow.add(f"kv{n}", jnp.stack([head[k][2:] for k in group]), back)

    halves = {}

    def core_halves(most, names):
        for name in names:
            if most and flow.whole(name):
                halves[name] = flow.take_half(name)
                flow.fly(name, swap(halves[name], 1, nd))
                most -= 1

    for step in range(nm - 1):
        head.append(ring(head[-1], 1, nm))
        flow.launch()
        if step == 0:
            view = lax.dynamic_index_in_dim(views[:, 0], mp % micro, 0, keepdims=True)
            view = lax.ppermute(view, ("dp", "mp"), routes(0))
            gains, biases = by_place(norm_gains[0]), by_place(norm_biases[0])
            head, tokens, view, gains, biases, there = flow.land(
                head, tokens, view, gains, biases, there
            )
            token_parts = []
        elif len(token_parts) < micro:
            token_parts.append(pack(tokens[:, 0], len(token_parts)))
            head, tokens, token_parts, cotangent, there = flow.land(
                head, tokens, token_parts, cotangent, there
            )
        else:
            head = flow.land(head)
        headed()
    head, feeds = flow.land(head, feeds)
    weights = [gather(feeds[0])]
    came = []
    head_names = [f"{name}{n}" for n in range(len(head_groups)) for name in ("kv", "qo")]
    while len(came) < micro or not all(n in halves or flow.whole(n) for n in head_names):
        if len(came) < micro:
            came.append(send(token_parts, len(came)))
        flow.launch(chip=2)
        if len(came) == micro:
            core_halves(2, head_names)
        if len(came) == 1:
            grad_parts = [pack(cotangent[:, 0], k) for k in range(micro)]
        came, token_parts, grad_parts, feeds, halves = flow.land(
            came, token_parts, grad_parts, feeds, halves
        )

    def turn():
        if len(feeds) < nm:
            feeds.append(ring(feeds[-1], 1, nm))

    def turned():
        if len(weights) < firsts and len(weights) < len(feeds):
            weights.append(gather(feeds[len(weights)]))
        for n, group in enumerate(groups):
            if f"up{n}" not in flow.order and group[-1] < len(feeds):
                flow.add(f"up{n}", jnp.stack([feeds[k][0] for k in group]), forth)
                flow.add(f"down{n}", jnp.stack([feeds[k][1] for k in group]), back)

    last = [f"{name}{n}" for n in range(len(groups)) for name in ("up", "down")]
    slot = jnp.stack([(step_here - t) % micro for t in range(micro)])
    within = (slot[:, None] * chunk + jnp.arange(chunk)[None]).reshape(-1)
    position = jnp.stack([(rank ^ j) * rows + within for j in range(ranks)])
    bias = jnp.where(position < TRI + view[0] * VIEW_TOK, 0.0, -1.0).astype(F32)
    core_halves(len(head_names), head_names)
    turn()
    x, normed, n_flip = first_norm(came, gains[:1], biases[:1])
    x, normed, n_flip, bias, halves, feeds = flow.land(x, normed, n_flip, bias, halves, feeds)
    turned()

    def both(name):
        names = [f"{name}{n}" for n in range(len(head_groups))]
        return [halves.pop(n) for n in names], [flow.kept.pop(n) for n in names]

    qo, kv = both("qo"), both("kv")

    turn()
    flow.launch()
    own_kv = project(normed, kv, 0, 2)
    own_kv, normed, qo, feeds = flow.land(own_kv, normed, qo, feeds)
    turned()

    def swap_rank(value, bit):
        if bit == 1:
            return swap(value, 1, nd)
        return lax.ppermute(value, "mp", [(i, i ^ (bit >> 1)) for i in range(nm)])

    rank_bits = [1 << b for b in range(ranks.bit_length() - 1)]
    kvs = {0: own_kv}
    for bit in rank_bits:
        for j in list(kvs):
            kvs[j | bit] = swap_rank(kvs[j], bit)
    kvs = [kvs[j] for j in range(ranks)]
    turn()
    flow.launch()
    query = project(normed, qo, 0, 1)
    kvs, query, bias, grad_parts, feeds = flow.land(kvs, query, bias, grad_parts, feeds)
    turned()

    grad_came, mixed, lses = [], [], []
    at_once = max(nm // 2, 1)
    while len(mixed) < nm or len(grad_came) < micro or not all(
        name in halves or flow.whole(name) for name in last
    ):
        turn()
        flow.launch()
        if len(grad_came) < micro:
            grad_came.append(send(grad_parts, len(grad_came)))
        core_halves(2, last)
        for k in range(len(mixed), min(len(mixed) + at_once, nm)):
            part, lse = attend(query, kvs, bias, k * per_k, per_k)
            mixed.append(part)
            lses.append(lse)
        mixed, query, halves, grad_parts, grad_came, feeds = flow.land(
            mixed, query, halves, grad_parts, grad_came, feeds
        )
        turned()
    core_halves(len(last), last)
    middle, normed_two, flip_two = middle_norm(x, mixed, qo, 1, gains[1:], biases[1:])
    grad, grad_flip = flip(grad_came)
    middle, normed_two, flip_two, halves, grad, grad_flip = flow.land(
        middle, normed_two, flip_two, halves, grad, grad_flip
    )
    for name in last:
        weights += [halves[name], flow.kept.pop(name)]

    result, active, slope = feed(normed_two, middle, index, firsts, sizes, weights)
    out_chunks = result.reshape((micro, chunk, width))
    output = []

    sums = Scatter(nd, nm, flow.bits)
    output = [send_chunk(out_chunks, 0)]
    over_dp = functools.partial(lax.psum_scatter, axis_name="dp", scatter_dimension=0, tiled=True)
    grads_down = over_dp(wide_grad(grad_flip, active, index))
    hid, gmid, attn, attn_flip, sums_two = feed_back(
        grad, slope, middle, gains[1:], index, firsts, sizes, weights
    )
    hid, gmid, attn, attn_flip, sums_two, flip_two, output, out_chunks = sums.land(
        hid, gmid, attn, attn_flip, sums_two, flip_two, output, out_chunks
    )
    grads_up = over_dp(wide_grad(flip_two, hid, index))
    grad_mixed = project(attn, qo, 1, 1)

    dqs, dkvs = {}, {}
    bias_tall = bias[:, :, None]
    closing = list(range(nm))
    dkv_part, dkv_came = {}, {}

    def head_grads():
        if not closing or closing[-1] not in dkv_came:
            return None
        k = closing.pop()
        dkvs[k], keep, give = head_grad(
            n_flip, attn_flip, mixed[k], dqs[k], dkv_part[k], dkv_came[k], chips
        )
        return k, (keep, give)

    def add_heads(ready, outs):
        sums.add("head", [ready[0]], outs[0], outs[1], None)

    def exchange(parts):
        parts = dict(enumerate(parts))
        came = None
        for bit in rank_bits[::-1]:
            if came is not None:
                parts = {j: add_low(part, came[j]) for j, part in parts.items()}
            came = {j ^ bit: swap_rank(parts.pop(j), bit) for j in list(parts) if j & bit}
        return parts[0], came[0]

    parts = None
    for k in list(reversed(range(nm))) + [-1]:
        if k == 0:
            sums.add_line("down", grads_down[0], rings=False)
        if k < 0:
            sums.add_line("up", grads_up[0], rings=True)
        sums.launch(direct=1 if k >= 0 else 0)
        while k >= 0 and len(output) < min(micro, nm - k + 1):
            output.append(send_chunk(out_chunks, len(output)))
        ready = head_grads()
        if parts is not None:
            dkv_part[k + 1], dkv_came[k + 1] = exchange(parts)
            parts = None
        if k >= 0:
            dqs[k], *parts = attend_back(
                query, kvs, bias_tall, lses[k], mixed[k], grad_mixed, k * per_k, per_k
            )
        live = (ready and ready[1], dqs, parts, query, dkv_part, dkv_came, dkvs, gmid)
        live = sums.land(*live, output)
        outs, dqs, parts, query, dkv_part, dkv_came, dkvs, gmid, output = live
        if ready:
            add_heads(ready, outs)

    sums.launch()
    first, sums_one = first_back(
        x,
        gmid,
        gains[:1],
        [dqs[k] for k in range(nm)],
        [dkvs.get(k, dkv_part[k]) for k in range(nm)],
        dkv_came[0],
        qo,
        kv,
    )
    first, sums_one, dkv_part, dkv_came, output = sums.land(
        first, sums_one, dkv_part, dkv_came, output
    )
    first = first.reshape((micro, chunk, width))
    vectors = jnp.take(
        jnp.concatenate([sums_one, sums_two]).reshape(4, nd, width // nd),
        jnp.argsort(index),
        axis=1,
    ).reshape(4, width)
    hops = [lambda value, bit=1 << b: swap(value, bit, nd) for b in range(nd.bit_length() - 1)]
    hops += [
        lambda value, bit=1 << b: lax.ppermute(value, "mp", [(i, i ^ bit) for i in range(nm)])
        for b in range(nm.bit_length() - 1)
    ]
    grad_tokens = []
    while sums.busy() or hops or len(grad_tokens) < micro:
        z = 1 if not grad_tokens else 2
        if len(grad_tokens) < micro:
            grad_tokens.append(send_chunk(first, len(grad_tokens)))
        sums.launch(direct=2, z=z)
        if len(grad_tokens) == micro:
            for _ in range(min(3, len(hops))):
                vectors = vectors + hops.pop(0)(vectors)
        ready = head_grads()
        grad_tokens, first, outs, vectors, output = sums.land(
            grad_tokens, first, ready and ready[1], vectors, output
        )
        if ready:
            add_heads(ready, outs)
    g_head, g_up, g_down = (sums.done[name] for name in ("head", "up", "down"))
    share = width // (nd * nm)
    vectors = lax.dynamic_slice_in_dim(vectors, (dp * nm + mp) * share, share, 1)
    return (
        unpack(output)[:, None],
        unpack(grad_tokens)[:, None],
        jnp.concatenate([g_head[:1], g_head[2:]])[None],
        g_head[1][None],
        g_up[None],
        g_down[None],
        jnp.stack([vectors[0], vectors[2]])[None],
        vectors[1][None],
        vectors[3][None],
    )


def solution(mesh):
    placed = (
        P(None, "dp", "mp", None),
        P(None, "dp"),
        P(),
        P(),
        P(None, None, "dp", "mp"),
        P(None, "dp", "mp"),
        P(None, "dp", "mp"),
        P(None, "dp", "mp"),
        P(None, "dp", "mp", None),
    )
    return jax.shard_map(
        functools.partial(shards, mesh.shape["dp"], mesh.shape["mp"]),
        mesh=mesh,
        in_specs=placed,
        out_specs=(
            P(None, "dp", "mp", None),
            P(None, "dp", "mp", None),
            P(None, None, "dp", "mp"),
            P(None, "dp", "mp"),
            P(None, "dp", "mp"),
            P(None, "dp", "mp"),
            P(None, None, ("dp", "mp")),
            P(None, ("dp", "mp")),
            P(None, ("dp", "mp")),
        ),
        check_vma=False,
    )
```

```python
import functools

import jax
import jax.numpy as jnp
from jax import lax
from jax.experimental import pallas as pl
from jax.experimental.pallas import tpu as pltpu
from jax.sharding import PartitionSpec as P

HDIM = 64
PAIR = 2 * HDIM
VIEW_TOK = 256
TRI = 768
EPSILON = 1e-05
MASKED = -1000000000.0
F32 = jnp.float32
BF16 = jnp.bfloat16
MIB = 1024 * 1024
ANY = pl.BlockSpec(memory_space=pl.ANY)
WHOLE = pl.BlockSpec(memory_space=pltpu.VMEM)
SHAPE = jax.ShapeDtypeStruct


def params(mib=56):
    return pltpu.CompilerParams(vmem_limit_bytes=mib * MIB)


def cost(flops, nbytes):
    return pl.CostEstimate(flops=int(flops), bytes_accessed=int(nbytes), transcendentals=0)


def dot_nt(a, b):
    return lax.dot_general(a, b, (((1,), (1,)), ((), ())), preferred_element_type=F32)


def dot_nn(a, b):
    return lax.dot_general(a, b, (((1,), (0,)), ((), ())), preferred_element_type=F32)


def dot_tn(a, b):
    return lax.dot_general(a, b, (((0,), (0,)), ((), ())), preferred_element_type=F32)


def row_block(rows):
    return 256 if rows % 256 == 0 else 128


def swap(value, bit, nd):
    return lax.ppermute(value, "dp", [(i, i ^ bit) for i in range(nd)])


def ring(value, step, nm):
    return lax.ppermute(value, "mp", [(i, (i + step) % nm) for i in range(nm)])


class Flow:
    def __init__(self, nd, nm):
        self.nd, self.nm = nd, nm
        self.bits = [1 << b for b in range(1, nd.bit_length() - 1)]
        self.queue = {bit: [] for bit in self.bits}
        self.order, self.pieces, self.flying, self.kept = {}, {}, {}, {}

    def add(self, name, value, order):
        self.order[name] = list(order)
        self.pieces[name] = [(0, value)]
        self.next(name)

    def next(self, name):
        if self.order[name]:
            self.queue[self.order[name][0]].append(name)

    def launch(self, chip=1, names=("",)):
        for bit, tasks in self.queue.items():
            for name in [name for name in tasks if name.startswith(names)][:chip]:
                tasks.remove(name)
                values = [value for _, value in self.pieces[name]]
                value = values[0][None] if len(values) == 1 else jnp.stack(values)
                self.flying["chip", name] = swap(value, bit, self.nd)

    def fly(self, name, value):
        self.flying["kept", name] = value

    def land(self, *extra):
        names, flying, kept = list(self.pieces), list(self.flying), list(self.kept)
        values = lax.optimization_barrier(
            (
                [self.pieces[name] for name in names],
                [self.flying[key] for key in flying],
                [self.kept[key] for key in kept],
                extra,
            )
        )
        for name, pieces in zip(names, values[0]):
            self.pieces[name] = [(j, v) for (j, _), (_, v) in zip(self.pieces[name], pieces)]
        self.kept = dict(zip(kept, values[2]))
        self.flying = {}
        for (kind, name), value in zip(flying, values[1]):
            if kind == "kept":
                self.kept[name] = value
                continue
            bit = self.order[name].pop(0)
            held = self.pieces[name]
            self.pieces[name] = held + [(j | bit, value[n]) for n, (j, _) in enumerate(held)]
            self.next(name)
        extra = values[3]
        return extra[0] if len(extra) == 1 else extra

    def whole(self, name):
        return name in self.pieces and not self.order[name]

    def take_half(self, name):
        pieces = dict(self.pieces.pop(name))
        return jnp.stack([pieces[2 * i] for i in range(self.nd // 2)])


def pack_kernel(index_ref, in_ref, out_ref):
    nd = index_ref.shape[0] - 1
    wide = in_ref.shape[2] // nd
    for p in range(nd):
        there = pl.ds(pl.multiple_of(index_ref[p] * wide, wide), wide)
        out_ref[:, p * wide : (p + 1) * wide] = in_ref[0, :, there]


def pack_features(value, index, which):
    micro, rows, width = value.shape
    nd = index.shape[0]
    if width // nd % 128:
        chunk = lax.dynamic_index_in_dim(value, which, 0, keepdims=False)
        return jnp.take(chunk.reshape(rows, nd, -1), index, axis=1).reshape(rows, width)
    return pl.pallas_call(
        pack_kernel,
        grid_spec=pltpu.PrefetchScalarGridSpec(
            num_scalar_prefetch=1,
            grid=(1,),
            in_specs=[pl.BlockSpec((1, rows, width), lambda i, index_ref: (index_ref[nd], 0, 0))],
            out_specs=pl.BlockSpec((rows, width), lambda i, index_ref: (0, 0)),
        ),
        out_shape=SHAPE((rows, width), value.dtype),
        compiler_params=params(),
        cost_estimate=cost(0, 6 * rows * width),
        name="pack_features",
    )(jnp.append(index, which.astype(jnp.int32)), value)


def unpack_kernel(index_ref, *refs):
    ins, out_ref = refs[:-1], refs[-1]
    nd = index_ref.shape[0] - len(ins)
    wide = out_ref.shape[2] // nd
    for k, in_ref in enumerate(ins):
        for p in range(nd):
            there = pl.ds(pl.multiple_of(index_ref[p] * wide, wide), wide)
            out_ref[index_ref[nd + k], :, there] = in_ref[:, p * wide : (p + 1) * wide]


def unpack_features(chunks, index, places):
    rows, width = chunks[0].shape
    micro, nd = len(chunks), index.shape[0]
    places = [place.astype(jnp.int32) for place in places]
    if width // nd % 128:
        back = jnp.argsort(index)
        stacked = jnp.stack(chunks).reshape(micro, rows, nd, -1)
        stacked = jnp.take(stacked, back, axis=2).reshape(micro, rows, width)
        return jnp.take(stacked, jnp.argsort(jnp.stack(places)), axis=0)
    return pl.pallas_call(
        unpack_kernel,
        in_specs=[pl.BlockSpec(memory_space=pltpu.SMEM)] + [WHOLE] * micro,
        out_specs=WHOLE,
        out_shape=SHAPE((micro, rows, width), chunks[0].dtype),
        compiler_params=params(),
        cost_estimate=cost(0, 4 * micro * rows * width),
        name="unpack_features",
    )(jnp.concatenate([index, jnp.stack(places)]), *chunks)


def standardize(state):
    centre = jnp.mean(state, axis=-1, keepdims=True)
    centred = state - centre
    spread = jnp.mean(centred * centred, axis=-1, keepdims=True)
    inverse = lax.rsqrt(spread + EPSILON)
    return centred * inverse, inverse


def norm_back(grad, state, gain):
    scaled, inverse = standardize(state)
    weighted = grad * gain
    first = jnp.mean(weighted, axis=-1, keepdims=True)
    second = jnp.mean(weighted * scaled, axis=-1, keepdims=True)
    sums = jnp.concatenate(
        [jnp.sum(grad * scaled, axis=0, keepdims=True), jnp.sum(grad, axis=0, keepdims=True)], 0
    )
    return inverse * (weighted - first - scaled * second), sums


def first_norm_kernel(micro, *refs):
    chunks = refs[:micro]
    gain_ref, bias_ref, x_ref, out_ref, flip_ref = refs[micro:]
    rows = chunks[0].shape[0]
    for k, ref in enumerate(chunks):
        here = slice(k * rows, (k + 1) * rows)
        x_ref[here] = ref[...]
        scaled, _ = standardize(ref[...].astype(F32))
        normed = (scaled * gain_ref[...] + bias_ref[...]).astype(BF16)
        out_ref[here] = normed
        flip_ref[:, here] = normed.T


def first_norm(chunks, gain, bias):
    rows, width = chunks[0].shape
    rows = rows * len(chunks)
    return pl.pallas_call(
        functools.partial(first_norm_kernel, len(chunks)),
        in_specs=[WHOLE] * (len(chunks) + 2),
        out_specs=[WHOLE] * 3,
        out_shape=[SHAPE((rows, width), BF16)] * 2 + [SHAPE((width, rows), BF16)],
        compiler_params=params(),
        cost_estimate=cost(0, 10 * rows * width),
        name="first_norm",
    )(*chunks, gain, bias)


def flip_kernel(*refs):
    chunks, out_ref, flip_ref = refs[:-2], refs[-2], refs[-1]
    rows = chunks[0].shape[0]
    for k, ref in enumerate(chunks):
        here = slice(k * rows, (k + 1) * rows)
        out_ref[here] = ref[...]
        flip_ref[:, here] = ref[...].T


def flip(chunks):
    rows, width = chunks[0].shape
    rows = rows * len(chunks)
    return pl.pallas_call(
        flip_kernel,
        in_specs=[WHOLE] * len(chunks),
        out_specs=[WHOLE] * 2,
        out_shape=[SHAPE((rows, width), BF16), SHAPE((width, rows), BF16)],
        compiler_params=params(),
        cost_estimate=cost(0, 6 * rows * width),
        name="flip",
    )(*chunks)


def each_k(refs):
    return [(ref, n) for ref in refs for n in range(ref.shape[1])]


def proj_kernel(parts, in_ref, *refs):
    owns, others, out_ref = refs[:parts], refs[parts : 2 * parts], refs[-1]
    value = in_ref[...]
    half = value.shape[1] // 2
    wide = owns[0].shape[-1]
    for k, ((own, n), (other, _)) in enumerate(zip(each_k(owns), each_k(others))):
        first = own[:, n, 0].reshape(half, wide)
        second = other[:, n, 0].reshape(half, wide)
        total = dot_nn(value[:, :half], first) + dot_nn(value[:, half:], second)
        out_ref[0, :, k * wide : (k + 1) * wide] = total.astype(BF16)


def head_spec(array, count, index_map):
    chips, ks, _, deep, wide = array.shape
    return pl.BlockSpec((chips, ks, count, deep, wide), index_map)


def project(value, weights, start, count):
    rows, width = value.shape
    wide = weights[0][0].shape[-1]
    nm = sum(array.shape[1] for array in weights[0])
    arrays = [*weights[0], *weights[1]]
    return pl.pallas_call(
        functools.partial(proj_kernel, len(weights[0])),
        grid=(count,),
        in_specs=[pl.BlockSpec((rows, width), lambda i: (0, 0))]
        + [head_spec(array, 1, lambda i: (0, 0, start + i, 0, 0)) for array in arrays],
        out_specs=pl.BlockSpec((1, rows, nm * wide), lambda i: (i, 0, 0)),
        out_shape=SHAPE((count, rows, nm * wide), BF16),
        compiler_params=params(),
        cost_estimate=cost(2 * count * rows * width * nm * wide, 2 * count * rows * width),
        name="project",
    )(value, *arrays)


def attend_kernel(parts, q_ref, *refs):
    k_refs, v_refs = refs[:parts], refs[parts : 2 * parts]
    bias_ref, out_ref, lse_ref = refs[2 * parts :]
    rows = q_ref.shape[1]
    low = lax.broadcasted_iota(jnp.int32, (1, PAIR), 1) < HDIM
    query = q_ref[0] * jnp.asarray(HDIM ** (-0.5), BF16)
    mixed = None
    for head in range(2):
        mine = low if head == 0 else jnp.logical_not(low)
        q_mine = jnp.where(mine, query, jnp.zeros_like(query))
        scores = [
            jnp.where(bias_ref[p : p + 1, :] < 0.0, MASKED, dot_nt(q_mine, k_refs[p][0]))
            for p in range(parts)
        ]
        top = functools.reduce(
            jnp.maximum, [jnp.max(part, axis=1, keepdims=True) for part in scores]
        )
        total, part = 0.0, 0.0
        for p in range(parts):
            expo = jnp.exp(scores[p] - top)
            total = total + jnp.sum(expo, axis=1, keepdims=True)
            part = part + dot_nn(expo.astype(BF16), v_refs[p][0])
        part = part / total
        mixed = part if head == 0 else jnp.where(low, mixed, part)
        lse = top + jnp.log(total)
        lse_ref[0, head : head + 1, :] = jnp.transpose(jnp.broadcast_to(lse, (rows, 128)))[0:1, :]
    out_ref[...] = mixed.astype(BF16)


def attend(query, kvs, bias, start, count):
    _, rows, width = query.shape
    parts = len(kvs)
    block = row_block(rows)
    keys = rows * parts
    key_spec = pl.BlockSpec((1, rows, PAIR), lambda h, i: (0, 0, start + h))
    value_spec = pl.BlockSpec((1, rows, PAIR), lambda h, i: (1, 0, start + h))
    return pl.pallas_call(
        functools.partial(attend_kernel, parts),
        grid=(count, rows // block),
        in_specs=[pl.BlockSpec((1, block, PAIR), lambda h, i: (0, i, start + h))]
        + [key_spec] * parts
        + [value_spec] * parts
        + [pl.BlockSpec((parts, rows), lambda h, i: (0, 0))],
        out_specs=[
            pl.BlockSpec((block, PAIR), lambda h, i: (i, h)),
            pl.BlockSpec((1, 2, block), lambda h, i: (h, 0, i)),
        ],
        out_shape=[SHAPE((rows, count * PAIR), BF16), SHAPE((count, 2, rows), F32)],
        compiler_params=params(),
        cost_estimate=cost(16 * rows * keys * count * PAIR, 8 * keys * count * PAIR),
        name="attend",
    )(query, *kvs, *kvs, bias)


def attend_back_kernel(parts, q_ref, *refs):
    k_refs, v_refs = refs[:parts], refs[parts : 2 * parts]
    bias_ref, lse_ref, mixed_ref, grad_ref, dq_ref = refs[2 * parts : 2 * parts + 5]
    dkv_refs = refs[2 * parts + 5 : 3 * parts + 5]
    dk_acc, dv_acc = refs[3 * parts + 5 :]
    step = pl.program_id(1)
    low = lax.broadcasted_iota(jnp.int32, (1, PAIR), 1) < HDIM
    query = q_ref[0] * jnp.asarray(HDIM ** (-0.5), BF16)
    grad = grad_ref[0]
    product = mixed_ref[...].astype(F32) * grad.astype(F32)

    @pl.when(step == 0)
    def _():
        dk_acc[...] = jnp.zeros_like(dk_acc)
        dv_acc[...] = jnp.zeros_like(dv_acc)

    grad_query = None
    for head in range(2):
        mine = low if head == 0 else jnp.logical_not(low)
        q_mine = jnp.where(mine, query, jnp.zeros_like(query))
        g_mine = jnp.where(mine, grad, jnp.zeros_like(grad))
        delta = jnp.sum(jnp.where(mine, product, 0.0), axis=1, keepdims=True)
        delta = jnp.transpose(jnp.broadcast_to(delta, (delta.shape[0], 128)))[0:1, :]
        query_part = 0.0
        for p in range(parts):
            keys, values = k_refs[p][0], v_refs[p][0]
            scores = jnp.where(bias_ref[p] < 0.0, MASKED, dot_nt(keys, q_mine))
            probs = jnp.exp(scores - lse_ref[0, head : head + 1, :])
            upstream = dot_nt(values, g_mine)
            grad_scores = (probs * (upstream - delta)).astype(BF16)
            dv_acc[p] += dot_nn(probs.astype(BF16), g_mine)
            dk_acc[p] += dot_nn(grad_scores, q_mine)
            query_part = query_part + dot_tn(grad_scores, keys)
        grad_query = query_part if head == 0 else jnp.where(low, grad_query, query_part)
    dq_ref[...] = (grad_query * HDIM ** (-0.5)).astype(BF16)

    @pl.when(step == pl.num_programs(1) - 1)
    def _():
        for p in range(parts):
            dkv_refs[p][0] = dk_acc[p].astype(BF16)
            dkv_refs[p][1] = dv_acc[p].astype(BF16)


def attend_back(query, kvs, bias, lse, mixed, grad, start, count):
    _, rows, width = query.shape
    parts = len(kvs)
    block = row_block(rows)
    keys = rows * parts
    key_spec = pl.BlockSpec((1, rows, PAIR), lambda h, i: (0, 0, start + h))
    value_spec = pl.BlockSpec((1, rows, PAIR), lambda h, i: (1, 0, start + h))
    return pl.pallas_call(
        functools.partial(attend_back_kernel, parts),
        grid=(count, rows // block),
        in_specs=[pl.BlockSpec((1, block, PAIR), lambda h, i: (0, i, start + h))]
        + [key_spec] * parts
        + [value_spec] * parts
        + [
            pl.BlockSpec((parts, rows, 1), lambda h, i: (0, 0, 0)),
            pl.BlockSpec((1, 2, block), lambda h, i: (h, 0, i)),
            pl.BlockSpec((block, PAIR), lambda h, i: (i, h)),
            pl.BlockSpec((1, block, PAIR), lambda h, i: (0, i, start + h)),
        ],
        out_specs=[pl.BlockSpec((block, PAIR), lambda h, i: (i, h))]
        + [pl.BlockSpec((2, rows, PAIR), lambda h, i: (0, 0, h))] * parts,
        out_shape=[SHAPE((rows, count * PAIR), BF16)]
        + [SHAPE((2, rows, count * PAIR), BF16)] * parts,
        scratch_shapes=[pltpu.VMEM((parts, rows, PAIR), F32)] * 2,
        compiler_params=params(),
        cost_estimate=cost(40 * rows * keys * count * PAIR, 16 * keys * count * PAIR),
        name="attend_back",
    )(query, *kvs, *kvs, bias, lse, mixed, grad)


def middle_kernel(nm, parts, x_ref, *refs):
    mixed_refs, refs = refs[:nm], refs[nm:]
    weights = refs[:parts], refs[parts : 2 * parts]
    gain_ref, bias_ref, mid_ref, out_ref, flip_ref = refs[2 * parts :]
    half = x_ref.shape[1] // 2
    sides = []
    for side in weights:
        total = 0.0
        for k, (ref, n) in enumerate(each_k(side)):
            total = total + dot_nt(mixed_refs[k][...], ref[:, n, 0].reshape(half, -1))
        sides.append(total)
    middle = x_ref[...].astype(F32) + jnp.concatenate(sides, axis=1)
    mid_ref[...] = middle
    scaled, _ = standardize(middle)
    normed = (scaled * gain_ref[...] + bias_ref[...]).astype(BF16)
    out_ref[...] = normed
    flip_ref[...] = normed.T


def middle_norm(x, mixed, weights, which, gain, bias):
    rows, width = x.shape
    nm, wide = len(mixed), mixed[0].shape[1]
    block = row_block(rows)
    vector = pl.BlockSpec((1, width), lambda i: (0, 0))
    line = pl.BlockSpec((block, width), lambda i: (i, 0))
    arrays = [*weights[0], *weights[1]]
    return pl.pallas_call(
        functools.partial(middle_kernel, nm, len(weights[0])),
        grid=(rows // block,),
        in_specs=[line]
        + [pl.BlockSpec((block, wide), lambda i: (i, 0))] * nm
        + [head_spec(array, 1, lambda i: (0, 0, which, 0, 0)) for array in arrays]
        + [vector, vector],
        out_specs=[line, line, pl.BlockSpec((width, block), lambda i: (0, i))],
        out_shape=[
            SHAPE((rows, width), F32),
            SHAPE((rows, width), BF16),
            SHAPE((width, rows), BF16),
        ],
        compiler_params=params(),
        cost_estimate=cost(2 * rows * width * nm * wide, 14 * x.size),
        name="middle_norm",
    )(x, *mixed, *arrays, gain, bias)


def load_weights(firsts, sizes, index_ref, refs, held, sems):
    step = pl.program_id(0)
    nm = firsts + sum(sizes)
    chips = held.shape[2]
    copies, refs = {k: [] for k in range(nm)}, list(refs)

    def add(k, source, w, side, n, sem):
        copies[k].append(
            pltpu.make_async_copy(source, held.at[w, 2 * k + side, n], sems.at[w, 2 * k + side, sem])
        )

    ref = refs.pop(0)
    for k in range(firsts):
        for w in range(2):
            for side in range(2):
                for n in range(chips):
                    add(k, ref.at[index_ref[side * chips + n], k, w], w, side, n, n)
    k = firsts
    for size in sizes:
        sides = [refs.pop(0) for _ in range(4)]
        for i in range(size):
            for n, ref in enumerate(sides):
                add(k, ref.at[:, i], n // 2, n % 2, slice(None), 0)
            k += 1

    @pl.when(step == 0)
    def _():
        for k in range(nm):
            for copy in copies[k]:
                copy.start()

    for k in range(nm):

        @pl.when(step == k)
        def _():
            for copy in copies[k]:
                copy.wait()


def feed_kernel(firsts, sizes, index_ref, *refs):
    nm, count = firsts + sum(sizes), 1 + 4 * len(sizes)
    in_ref, mid_ref, out_ref, act_ref, slope_ref, held, acc, sems = refs[count:]
    step = pl.program_id(0)
    load_weights(firsts, sizes, index_ref, refs[:count], held, sems)
    half = in_ref.shape[1] // 2
    up = [held[0, 2 * step + side].reshape(half, -1) for side in range(2)]
    down = [held[1, 2 * step + side].reshape(half, -1) for side in range(2)]

    @pl.when(step == 0)
    def _():
        acc[...] = mid_ref[...]

    hidden = dot_nn(in_ref[:, :half], up[0]) + dot_nn(in_ref[:, half:], up[1])
    below = 0.5 + 0.5 * lax.erf(hidden * (0.5**0.5))
    density = jnp.exp(-0.5 * hidden * hidden) * 0.3989422804014327
    active = (hidden * below).astype(BF16)
    act_ref[0] = active
    slope_ref[0] = (below + hidden * density).astype(BF16)
    acc[:, :half] += dot_nt(active, down[0])
    acc[:, half:] += dot_nt(active, down[1])

    @pl.when(step == nm - 1)
    def _():
        out_ref[...] = acc[...].astype(BF16)


def feed(normed, middle, index, firsts, sizes, weights):
    rows, width = normed.shape
    nm = firsts + sum(sizes)
    nd, (deep, hidden) = index.shape[0], weights[0].shape[3:]
    chips = nd // 2
    line = pl.BlockSpec((rows, width), lambda k: (0, 0))
    wide = pl.BlockSpec((1, rows, hidden), lambda k: (k, 0, 0))
    return pl.pallas_call(
        functools.partial(feed_kernel, firsts, sizes),
        grid=(nm,),
        in_specs=[pl.BlockSpec(memory_space=pltpu.SMEM)]
        + [ANY] * len(weights)
        + [line, line],
        out_specs=[line, wide, wide],
        out_shape=[SHAPE((rows, width), BF16)] + [SHAPE((nm, rows, hidden), BF16)] * 2,
        scratch_shapes=[
            pltpu.VMEM((2, 2 * nm, chips, deep, hidden), BF16),
            pltpu.VMEM((rows, width), F32),
            pltpu.SemaphoreType.DMA((2, 2 * nm, chips)),
        ],
        compiler_params=params(60),
        cost_estimate=cost(4 * rows * width * nm * hidden, 4 * nm * width * hidden),
        name="feed",
    )(index, *weights, normed, middle)


def feed_back_kernel(firsts, sizes, index_ref, *refs):
    nm, count = firsts + sum(sizes), 1 + 4 * len(sizes)
    g_ref, slope_ref, mid_ref, gain_ref = refs[count : count + 4]
    hid_ref, gmid_ref, attn_ref, flip_ref, sums_ref, held, acc, sems = refs[count + 4 :]
    step = pl.program_id(0)
    load_weights(firsts, sizes, index_ref, refs[:count], held, sems)
    half = g_ref.shape[1] // 2
    up = [held[0, 2 * step + side].reshape(half, -1) for side in range(2)]
    down = [held[1, 2 * step + side].reshape(half, -1) for side in range(2)]
    active = dot_nn(g_ref[:, :half], down[0]) + dot_nn(g_ref[:, half:], down[1])
    hidden = (active * slope_ref[0].astype(F32)).astype(BF16)
    hid_ref[0] = hidden
    first, second = dot_nt(hidden, up[0]), dot_nt(hidden, up[1])

    @pl.when(step == 0)
    def _():
        acc[:, :half] = first
        acc[:, half:] = second

    @pl.when(step > 0)
    def _():
        acc[:, :half] += first
        acc[:, half:] += second

    @pl.when(step == nm - 1)
    def _():
        into, sums = norm_back(acc[...], mid_ref[...], gain_ref[...])
        result = g_ref[...].astype(F32) + into
        gmid_ref[...] = result
        attn = result.astype(BF16)
        attn_ref[...] = attn
        flip_ref[...] = attn.T
        sums_ref[...] = sums


def feed_back(grad, slope, middle, gain, index, firsts, sizes, weights):
    rows, width = grad.shape
    nm = firsts + sum(sizes)
    nd, (deep, hidden) = index.shape[0], weights[0].shape[3:]
    chips = nd // 2
    line = pl.BlockSpec((rows, width), lambda k: (0, 0))
    wide = pl.BlockSpec((1, rows, hidden), lambda k: (k, 0, 0))
    return pl.pallas_call(
        functools.partial(feed_back_kernel, firsts, sizes),
        grid=(nm,),
        in_specs=[pl.BlockSpec(memory_space=pltpu.SMEM)]
        + [ANY] * len(weights)
        + [line, wide, line, pl.BlockSpec((1, width), lambda k: (0, 0))],
        out_specs=[
            wide,
            line,
            line,
            pl.BlockSpec((width, rows), lambda k: (0, 0)),
            pl.BlockSpec((2, width), lambda k: (0, 0)),
        ],
        out_shape=[
            SHAPE((nm, rows, hidden), BF16),
            SHAPE((rows, width), F32),
            SHAPE((rows, width), BF16),
            SHAPE((width, rows), BF16),
            SHAPE((2, width), F32),
        ],
        scratch_shapes=[
            pltpu.VMEM((2, 2 * nm, chips, deep, hidden), BF16),
            pltpu.VMEM((rows, width), F32),
            pltpu.SemaphoreType.DMA((2, 2 * nm, chips)),
        ],
        compiler_params=params(60),
        cost_estimate=cost(4 * rows * width * nm * hidden, 4 * nm * width * hidden),
        name="feed_back",
    )(index, *weights, grad, slope, middle, gain)


def wide_grad_kernel(index_ref, a_ref, b_ref, out_ref):
    part = dot_nn(a_ref[...], b_ref[0]).astype(BF16)
    nd, deep = out_ref.shape[0], out_ref.shape[2]
    for p in range(nd):
        out_ref[index_ref[p], 0] = part[p * deep : (p + 1) * deep]


def wide_grad(flipped, values, index):
    width, rows = flipped.shape
    nm, _, hidden = values.shape
    nd = index.shape[0]
    block = min(512, hidden)
    return pl.pallas_call(
        wide_grad_kernel,
        grid=(nm, hidden // block),
        in_specs=[
            pl.BlockSpec(memory_space=pltpu.SMEM),
            pl.BlockSpec((width, rows), lambda k, i: (0, 0)),
            pl.BlockSpec((1, rows, block), lambda k, i: (k, 0, i)),
        ],
        out_specs=pl.BlockSpec((nd, 1, width // nd, block), lambda k, i: (0, k, 0, i)),
        out_shape=SHAPE((nd, nm, width // nd, hidden), BF16),
        compiler_params=params(),
        cost_estimate=cost(2 * nm * width * rows * hidden, 4 * nm * width * hidden),
        name="wide_grad",
    )(index, flipped, values)


def head_grad_kernel(
    n_ref, g_ref, mixed_ref, dq_ref, dkv_ref, came_ref, sum_ref, keep_ref, give_ref
):
    half = n_ref.shape[0] // 2
    chips, _, deep, wide = keep_ref.shape
    total = (dkv_ref[...].astype(F32) + came_ref[...].astype(F32)).astype(BF16)
    sum_ref[...] = total
    pairs = ((n_ref, dq_ref[...]), (g_ref, mixed_ref[...]), (n_ref, total[0]), (n_ref, total[1]))
    for i, (left, right) in enumerate(pairs):
        for out, side in ((keep_ref, left[:half]), (give_ref, left[half:])):
            out[:, i] = dot_nn(side, right).astype(BF16).reshape(chips, deep, wide)


def head_grad(n_flip, g_flip, mixed, dq, dkv, came, chips):
    width, rows = n_flip.shape
    wide = dq.shape[1]
    piece = SHAPE((chips, 4, width // 2 // chips, wide), BF16)
    total, keep, give = pl.pallas_call(
        head_grad_kernel,
        in_specs=[WHOLE] * 6,
        out_specs=[WHOLE] * 3,
        out_shape=[SHAPE(dkv.shape, BF16), piece, piece],
        compiler_params=params(),
        cost_estimate=cost(8 * width * rows * wide, 8 * width * wide),
        name="head_grad",
    )(n_flip, g_flip, mixed, dq, dkv, came)
    return total, keep[None], give[None]


def first_back_kernel(nm, parts, x_ref, gmid_ref, gain_ref, *refs):
    dqs, dkvs, came_ref, refs = refs[:nm], refs[nm : 2 * nm], refs[2 * nm], refs[2 * nm + 1 :]
    qo = refs[:parts], refs[parts : 2 * parts]
    kv = refs[2 * parts : 3 * parts], refs[3 * parts : 4 * parts]
    out_ref, sums_ref = refs[4 * parts :]
    last = (dkvs[0][...].astype(F32) + came_ref[...].astype(F32)).astype(BF16)
    step = pl.program_id(0)
    half = x_ref.shape[1] // 2
    sides = []
    for side in range(2):
        total = 0.0
        for k, ((qo_ref, n), (kv_ref, _)) in enumerate(zip(each_k(qo[side]), each_k(kv[side]))):
            total = total + dot_nt(dqs[k][...], qo_ref[:, n, 0].reshape(half, -1))
            for i in range(2):
                dkv = dkvs[k][i] if k else last[i]
                total = total + dot_nt(dkv, kv_ref[:, n, i].reshape(half, -1))
        sides.append(total)
    into, sums = norm_back(jnp.concatenate(sides, axis=1), x_ref[...].astype(F32), gain_ref[...])
    out_ref[...] = (gmid_ref[...] + into).astype(BF16)

    @pl.when(step == 0)
    def _():
        sums_ref[...] = sums

    @pl.when(step > 0)
    def _():
        sums_ref[...] += sums


def first_back(x, gmid, gain, dqs, dkvs, came, qo, kv):
    rows, width = x.shape
    nm, wide = len(dqs), dqs[0].shape[1]
    block = row_block(rows)
    line = pl.BlockSpec((block, width), lambda i: (i, 0))
    still = lambda i: (0, 0, 0, 0, 0)
    qo_arrays, kv_arrays = [*qo[0], *qo[1]], [*kv[0], *kv[1]]
    return pl.pallas_call(
        functools.partial(first_back_kernel, nm, len(qo[0])),
        grid=(rows // block,),
        in_specs=[line, line, pl.BlockSpec((1, width), lambda i: (0, 0))]
        + [pl.BlockSpec((block, wide), lambda i: (i, 0))] * nm
        + [pl.BlockSpec((2, block, wide), lambda i: (0, i, 0))] * (nm + 1)
        + [head_spec(array, 1, still) for array in qo_arrays]
        + [head_spec(array, 2, still) for array in kv_arrays],
        out_specs=[line, pl.BlockSpec((2, width), lambda i: (0, 0))],
        out_shape=[SHAPE((rows, width), BF16), SHAPE((2, width), F32)],
        compiler_params=params(),
        cost_estimate=cost(6 * rows * width * nm * wide, 12 * x.size),
        name="first_back",
    )(x, gmid, gain, *dqs, *dkvs, came, *qo_arrays, *kv_arrays)


def add_low(a, b):
    return (a.astype(F32) + b.astype(F32)).astype(BF16)


def add_parts_kernel(keep_ref, came_ref, *outs):
    for n, out in enumerate(outs):
        out[...] = add_low(keep_ref[:, n + 1], came_ref[:, n + 1])


def add_parts(keep, came):
    count = keep.shape[1] - 1
    piece = SHAPE(keep.shape[:1] + keep.shape[2:], keep.dtype)
    return pl.pallas_call(
        add_parts_kernel,
        in_specs=[WHOLE] * 2,
        out_specs=[WHOLE] * count,
        out_shape=[piece] * count,
        compiler_params=params(),
        cost_estimate=cost(0, 6 * keep.size),
        name="add_parts",
    )(keep, came)


class Scatter:
    def __init__(self, nd, nm, bits):
        self.nd, self.nm = nd, nm
        self.queue = {1: [], **{bit: [] for bit in bits}, "direct": [], "z": []}
        self.order, self.kept, self.waits, self.flying = {}, {}, {}, {}
        self.ends, self.came, self.done, self.rings = {}, {}, {}, {}

    def add(self, name, ks, keep, give, order, rings=True):
        self.order[name, tuple(ks)], self.rings[name] = order, rings
        self.push(1, (name, tuple(ks), -1), list(range(0, self.nd, 2)), keep, give)

    def add_line(self, name, value, rings):
        self.rings[name] = rings
        if rings:
            for k in range(self.nm):
                self.ends[name, k] = (value[k],)
            self.advance(name, self.nm - 1)
            return
        self.ends[name] = [value[0]]
        for k in sorted(range(1, self.nm), key=lambda k: min(k, self.nm - k)):
            self.waits[name, k, "z"] = value[k]
            self.queue["z"].append((name, k, "z"))

    def push(self, link, key, places, keep, give):
        self.kept[key], self.waits[key] = (places, keep), give
        self.queue[link].append(key)

    def launch(self, core=1, chip=1, direct=1, z=1):
        for link, tasks in self.queue.items():
            for _ in range({1: core, "direct": direct, "z": z}.get(link, chip)):
                if not tasks:
                    break
                key = tasks.pop(0)
                value = self.waits.pop(key)
                if link == "z" and not self.rings[key[0]]:
                    value = ring(value, -key[1], self.nm)
                elif link == "z":
                    value = ring(value, -1, self.nm)
                elif link == "direct":
                    value = [
                        swap(part, 2 * n + 2, self.nd) for n, part in enumerate(add_parts(*value))
                    ]
                else:
                    value = swap(value, link, self.nd)
                self.flying[key] = value

    def busy(self):
        return bool(self.flying) or any(self.queue.values())

    def land(self, *extra):
        waits, flying = list(self.waits), list(self.flying)
        values = lax.optimization_barrier(
            ([self.waits[key] for key in waits], [self.flying[key] for key in flying], extra)
        )
        self.waits = dict(zip(waits, values[0]))
        came = dict(zip(flying, values[1]))
        self.flying = {}
        for key, value in came.items():
            self.arrive(key, value)
        extra = values[2]
        return extra[0] if len(extra) == 1 else extra

    def arrive(self, key, value):
        name, ks, stage = key
        if stage == "z" and not self.rings[name]:
            self.ends[name].append(value)
            if len(self.ends[name]) == self.nm:
                self.done[name] = sum(part.astype(F32) for part in self.ends.pop(name))
            return
        if stage == "z":
            self.came[name, ks - 1] = value
            self.advance(name, ks - 1)
            return
        order = self.order[name, ks]
        places, keep = self.kept.pop(key)
        if order is None and stage == -1:
            own = (keep[:, 0], value[:, 0])
            self.push("direct", (name, ks, 0), own, None, (keep, value))
            return
        if order is None:
            for n, k in enumerate(ks):
                self.ends[name, k] = tuple(part[n] for part in [*places, *value])
                self.advance(name, k)
            return
        if stage + 1 == len(order):
            for n, k in enumerate(ks):
                self.ends[name, k] = (keep[n, 0], value[n, 0])
            for k in reversed(ks):
                self.advance(name, k)
            return
        bit = order[stage + 1]
        stays = [n for n, j in enumerate(places) if not j & bit]
        goes = [n for n, j in enumerate(places) if j & bit]

        def take(array, which):
            return jnp.stack([array[:, n] for n in which], axis=1)

        self.push(
            bit,
            (name, ks, stage + 1),
            [places[n] for n in stays],
            add_low(take(keep, stays), take(value, stays)),
            add_low(take(keep, goes), take(value, goes)),
        )

    def advance(self, name, k):
        if (name, k) not in self.ends or (k < self.nm - 1 and (name, k) not in self.came):
            return
        total = sum(part.astype(F32) for part in self.ends.pop((name, k)))
        if k < self.nm - 1:
            total = total + self.came.pop((name, k)).astype(F32)
        if k:
            key = (name, k, "z")
            self.waits[key] = total.astype(BF16)
            self.queue["z"].append(key)
        else:
            self.done[name] = total


def shards(nd, nm, tokens, views, norm_gains, norm_biases, w_proj, w_out, w_up, w_down, cotangent):
    micro, _, chunk, width = tokens.shape
    ranks = nm // micro
    half = max(ranks // 2, 1)
    rows = micro * chunk
    chips = nd // 2
    wide = w_out.shape[2]
    per_k = wide // PAIR
    hidden = w_up.shape[2]
    dp, mp = lax.axis_index("dp"), lax.axis_index("mp")
    group = mp // half
    step_here = group // 2
    rank = (dp & 1) + 2 * (mp % half)
    order_of = [2 * (p % chips) + p // chips for p in range(nd)]
    offsets = jnp.asarray(order_of, jnp.int32)
    index = dp.astype(jnp.int32) ^ offsets

    def routes(k):
        pairs = []
        for d in range(nd):
            for z in range(nm):
                m = (k + z) % micro
                r = z // micro
                to_d = (d & ~1) | (r & 1)
                to_z = (2 * m + (d & 1)) * half + r // 2
                pairs.append((d * nm + z, to_d * nm + to_z))
        return pairs

    there = ((dp & ~1) | ((mp // micro) & 1)).astype(jnp.int32) ^ offsets

    def pack(value, k):
        return pack_features(value, there, (k + mp) % micro)

    def send(packed, k):
        return lax.ppermute(packed[k], ("dp", "mp"), routes(k))

    def send_chunk(chunks, k):
        return lax.ppermute(chunks[k], ("dp", "mp"), [(b, a) for a, b in routes(k)])

    def unpack(came):
        return unpack_features(came, there, [(k + mp) % micro for k in range(micro)])

    def by_place(vector):
        return jnp.take(vector.reshape(-1, nd, width // nd), index, axis=1).reshape(-1, width)

    flow = Flow(nd, nm)
    forth, back = flow.bits, flow.bits[::-1]
    firsts = min(2, nm)
    groups = [list(range(k, min(k + 2, nm))) for k in range(firsts, nm, 2)]
    sizes = tuple(len(group) for group in groups)
    head = [jnp.concatenate([w_proj[0, :1], w_out, w_proj[0, 1:]])]
    feeds = [jnp.concatenate([w_up, w_down])]
    gather = functools.partial(lax.all_gather, axis_name="dp")
    head_groups = [[0], list(range(1, nm))]

    def headed(n):
        flow.add(f"qo{n}", jnp.stack([head[k][:2] for k in head_groups[n]]), forth)
        flow.add(f"kv{n}", jnp.stack([head[k][2:] for k in head_groups[n]]), back)

    halves = {}

    def core_halves(most, names):
        for name in names:
            if most and flow.whole(name):
                halves[name] = flow.take_half(name)
                flow.fly(name, swap(halves[name], 1, nd))
                most -= 1

    for k in sorted(range(1, nm), key=lambda k: -min(k, nm - k)):
        flow.fly(("head", k), ring(head[0], k, nm))
    headed(0)
    flow.launch()
    token_parts = [pack(tokens[:, 0], k) for k in range(micro)]
    view = lax.dynamic_index_in_dim(views[:, 0], mp % micro, 0, keepdims=True)
    head, tokens, token_parts, cotangent, there, view, feeds, norm_gains, norm_biases = flow.land(
        head, tokens, token_parts, cotangent, there, view, feeds, norm_gains, norm_biases
    )
    head += [flow.kept.pop(("head", k)) for k in range(1, nm)]
    headed(1)
    weights = []
    came = []
    head_names = [f"{name}{n}" for n in range(len(head_groups)) for name in ("kv", "qo")]
    while len(came) < micro or not all(n in halves or flow.whole(n) for n in head_names):
        if len(came) < micro:
            came.append(send(token_parts, len(came)))
        flow.launch(chip=2)
        if len(came) == micro:
            core_halves(2, head_names)
        if len(came) == 1:
            grad_parts = [pack(cotangent[:, 0], k) for k in range(micro)]
            gains, biases = by_place(norm_gains[0]), by_place(norm_biases[0])
        came, token_parts, grad_parts, feeds, halves, gains, biases, view = flow.land(
            came, token_parts, grad_parts, feeds, halves, gains, biases, view
        )

    def turn():
        if len(feeds) < nm:
            feeds.append(ring(feeds[-1], 1, nm))

    def turned():
        if not weights and len(feeds) >= firsts:
            weights.append(gather(jnp.stack(feeds[:firsts])))
        for n, group in enumerate(groups):
            if f"up{n}" not in flow.order and group[-1] < len(feeds):
                flow.add(f"up{n}", jnp.stack([feeds[k][0] for k in group]), forth)
                flow.add(f"down{n}", jnp.stack([feeds[k][1] for k in group]), back)

    last = [f"{name}{n}" for n in range(len(groups)) for name in ("up", "down")]
    core_halves(len(head_names), head_names)
    turn()
    x, normed, n_flip = first_norm(came, gains[:1], biases[:1])
    x, normed, n_flip, halves, feeds, view = flow.land(x, normed, n_flip, halves, feeds, view)
    turned()

    def both(name):
        names = [f"{name}{n}" for n in range(len(head_groups))]
        return [halves.pop(n) for n in names], [flow.kept.pop(n) for n in names]

    qo, kv = both("qo"), both("kv")

    turn()
    flow.launch()
    views = lax.ppermute(view, ("dp", "mp"), routes(0))
    own_kv = project(normed, kv, 0, 2)
    own_kv, normed, qo, feeds, views = flow.land(own_kv, normed, qo, feeds, views)
    turned()

    def swap_rank(value, bit):
        if bit == 1:
            return swap(value, 1, nd)
        return lax.ppermute(value, "mp", [(i, i ^ (bit >> 1)) for i in range(nm)])

    rank_bits = [1 << b for b in range(ranks.bit_length() - 1)]
    kvs = {0: own_kv}
    for bit in rank_bits:
        for j in list(kvs):
            kvs[j | bit] = swap_rank(kvs[j], bit)
    kvs = [kvs[j] for j in range(ranks)]
    turn()
    flow.launch()
    query = project(normed, qo, 0, 1)
    slot = jnp.stack([(step_here - t) % micro for t in range(micro)])
    within = (slot[:, None] * chunk + jnp.arange(chunk)[None]).reshape(-1)
    position = jnp.stack([(rank ^ j) * rows + within for j in range(ranks)])
    bias = jnp.where(position < TRI + views[0] * VIEW_TOK, 0.0, -1.0).astype(F32)
    kvs, query, bias, grad_parts, feeds = flow.land(kvs, query, bias, grad_parts, feeds)
    turned()

    grad_came, mixed, lses = [], [], []
    at_once = max(nm // 2, 1)
    while len(mixed) < nm or len(grad_came) < micro or not all(
        name in halves or flow.whole(name) for name in last
    ):
        turn()
        flow.launch()
        if len(grad_came) < micro:
            grad_came.append(send(grad_parts, len(grad_came)))
        core_halves(2, last)
        for k in range(len(mixed), min(len(mixed) + at_once, nm)):
            part, lse = attend(query, kvs, bias, k * per_k, per_k)
            mixed.append(part)
            lses.append(lse)
        mixed, query, halves, grad_parts, grad_came, feeds = flow.land(
            mixed, query, halves, grad_parts, grad_came, feeds
        )
        turned()
    core_halves(len(last), last)
    middle, normed_two, flip_two = middle_norm(x, mixed, qo, 1, gains[1:], biases[1:])
    grad, grad_flip = flip(grad_came)
    middle, normed_two, flip_two, halves, grad, grad_flip = flow.land(
        middle, normed_two, flip_two, halves, grad, grad_flip
    )
    for name in last:
        weights += [halves[name], flow.kept.pop(name)]

    result, active, slope = feed(normed_two, middle, index, firsts, sizes, weights)
    out_chunks = result.reshape((micro, chunk, width))
    output = []

    sums = Scatter(nd, nm, flow.bits)
    output = [send_chunk(out_chunks, 0)]
    over_dp = functools.partial(lax.psum_scatter, axis_name="dp", scatter_dimension=0, tiled=True)
    grads_down = over_dp(wide_grad(grad_flip, active, index))
    hid, gmid, attn, attn_flip, sums_two = feed_back(
        grad, slope, middle, gains[1:], index, firsts, sizes, weights
    )
    hid, gmid, attn, attn_flip, sums_two, flip_two, output, out_chunks = sums.land(
        hid, gmid, attn, attn_flip, sums_two, flip_two, output, out_chunks
    )
    grads_up = jnp.take(
        over_dp(wide_grad(flip_two, hid, index))[0], (mp - jnp.arange(nm)) % nm, axis=0
    )
    grads_up = lax.psum_scatter(grads_up, "mp", scatter_dimension=0, tiled=True)
    grad_mixed = project(attn, qo, 1, 1)

    dqs, dkvs = {}, {}
    bias_tall = bias[:, :, None]
    closing = list(range(nm))
    dkv_part, dkv_came = {}, {}

    def head_grads():
        if not closing or closing[-1] not in dkv_came:
            return None
        k = closing.pop()
        dkvs[k], keep, give = head_grad(
            n_flip, attn_flip, mixed[k], dqs[k], dkv_part[k], dkv_came[k], chips
        )
        return k, (keep, give)

    def add_heads(ready, outs):
        sums.add("head", [ready[0]], outs[0], outs[1], None)

    def exchange(parts):
        parts = dict(enumerate(parts))
        came = None
        for bit in rank_bits[::-1]:
            if came is not None:
                parts = {j: add_low(part, came[j]) for j, part in parts.items()}
            came = {j ^ bit: swap_rank(parts.pop(j), bit) for j in list(parts) if j & bit}
        return parts[0], came[0]

    parts = None
    for k in list(reversed(range(nm))) + [-1]:
        if k == 0:
            sums.add_line("down", grads_down[0], rings=False)
        sums.launch(direct=1 if k < 0 else 0, z=nm - 1)
        while k >= 0 and len(output) < min(micro, nm - k + 1):
            output.append(send_chunk(out_chunks, len(output)))
        ready = head_grads()
        if parts is not None:
            dkv_part[k + 1], dkv_came[k + 1] = exchange(parts)
            parts = None
        if k >= 0:
            dqs[k], *parts = attend_back(
                query, kvs, bias_tall, lses[k], mixed[k], grad_mixed, k * per_k, per_k
            )
        live = (ready and ready[1], dqs, parts, query, dkv_part, dkv_came, dkvs, gmid)
        live = sums.land(*live, output)
        outs, dqs, parts, query, dkv_part, dkv_came, dkvs, gmid, output = live
        if ready:
            add_heads(ready, outs)

    sums.launch()
    ready = head_grads()
    first, sums_one = first_back(
        x,
        gmid,
        gains[:1],
        [dqs[k] for k in range(nm)],
        [dkvs[k] if k else dkv_part[k] for k in range(nm)],
        dkv_came[0],
        qo,
        kv,
    )
    first, sums_one, outs, output = sums.land(first, sums_one, ready and ready[1], output)
    if ready:
        add_heads(ready, outs)
    first = first.reshape((micro, chunk, width))
    vectors = jnp.take(
        jnp.concatenate([sums_one, sums_two]).reshape(4, nd, width // nd),
        jnp.argsort(index),
        axis=1,
    ).reshape(4, width)
    hops = [lambda value, bit=1 << b: swap(value, bit, nd) for b in range(nd.bit_length() - 1)]
    grad_tokens = []
    while sums.busy() or len(grad_tokens) < micro:
        if len(grad_tokens) < micro:
            grad_tokens.append(send_chunk(first, len(grad_tokens)))
            if len(grad_tokens) == micro:
                output = unpack(output)
        sums.launch()
        while hops:
            vectors = vectors + hops.pop(0)(vectors)
        grad_tokens, first, vectors, output = sums.land(grad_tokens, first, vectors, output)
    g_head, g_down = sums.done["head"], sums.done["down"]
    vectors = sum([ring(vectors, k, nm) for k in range(1, nm)], vectors)
    share = width // (nd * nm)
    vectors = lax.dynamic_slice_in_dim(vectors, (dp * nm + mp) * share, share, 1)
    return (
        output[:, None],
        unpack(grad_tokens)[:, None],
        jnp.concatenate([g_head[:1], g_head[2:]])[None],
        g_head[1][None],
        grads_up.astype(F32),
        g_down[None],
        jnp.stack([vectors[0], vectors[2]])[None],
        vectors[1][None],
        vectors[3][None],
    )


def solution(mesh):
    placed = (
        P(None, "dp", "mp", None),
        P(None, "dp"),
        P(),
        P(),
        P(None, None, "dp", "mp"),
        P(None, "dp", "mp"),
        P(None, "dp", "mp"),
        P(None, "dp", "mp"),
        P(None, "dp", "mp", None),
    )
    return jax.shard_map(
        functools.partial(shards, mesh.shape["dp"], mesh.shape["mp"]),
        mesh=mesh,
        in_specs=placed,
        out_specs=(
            P(None, "dp", "mp", None),
            P(None, "dp", "mp", None),
            P(None, None, "dp", "mp"),
            P(None, "dp", "mp"),
            P(None, "dp", "mp"),
            P(None, "dp", "mp"),
            P(None, None, ("dp", "mp")),
            P(None, ("dp", "mp")),
            P(None, ("dp", "mp")),
        ),
        check_vma=False,
    )
```

```python
import functools

import jax
import jax.numpy as jnp
from jax import lax
from jax.experimental import pallas as pl
from jax.experimental.pallas import tpu as pltpu
from jax.sharding import PartitionSpec as P

HDIM = 64
PAIR = 2 * HDIM
VIEW_TOK = 256
TRI = 768
EPSILON = 1e-05
MASKED = -1000000000.0
F32 = jnp.float32
BF16 = jnp.bfloat16
MIB = 1024 * 1024
ANY = pl.BlockSpec(memory_space=pl.ANY)
WHOLE = pl.BlockSpec(memory_space=pltpu.VMEM)
SHAPE = jax.ShapeDtypeStruct


def params(mib=56):
    return pltpu.CompilerParams(vmem_limit_bytes=mib * MIB)


def cost(flops, nbytes):
    return pl.CostEstimate(flops=int(flops), bytes_accessed=int(nbytes), transcendentals=0)


def dot_nt(a, b):
    return lax.dot_general(a, b, (((1,), (1,)), ((), ())), preferred_element_type=F32)


def dot_nn(a, b):
    return lax.dot_general(a, b, (((1,), (0,)), ((), ())), preferred_element_type=F32)


def dot_tn(a, b):
    return lax.dot_general(a, b, (((0,), (0,)), ((), ())), preferred_element_type=F32)


def row_block(rows):
    return 256 if rows % 256 == 0 else 128


def swap(value, bit, nd):
    return lax.ppermute(value, "dp", [(i, i ^ bit) for i in range(nd)])


def ring(value, step, nm):
    return lax.ppermute(value, "mp", [(i, (i + step) % nm) for i in range(nm)])


class Flow:
    def __init__(self, nd, nm):
        self.nd, self.nm = nd, nm
        self.bits = [1 << b for b in range(1, nd.bit_length() - 1)]
        self.queue = {bit: [] for bit in self.bits}
        self.order, self.pieces, self.flying, self.kept = {}, {}, {}, {}

    def add(self, name, value, order):
        self.order[name] = list(order)
        self.pieces[name] = [(0, value)]
        self.next(name)

    def next(self, name):
        if self.order[name]:
            self.queue[self.order[name][0]].append(name)

    def launch(self, chip=1, names=("",)):
        for bit, tasks in self.queue.items():
            for name in [name for name in tasks if name.startswith(names)][:chip]:
                tasks.remove(name)
                values = [value for _, value in self.pieces[name]]
                value = values[0][None] if len(values) == 1 else jnp.stack(values)
                self.flying["chip", name] = swap(value, bit, self.nd)

    def fly(self, name, value):
        self.flying["kept", name] = value

    def land(self, *extra):
        names, flying, kept = list(self.pieces), list(self.flying), list(self.kept)
        values = lax.optimization_barrier(
            (
                [self.pieces[name] for name in names],
                [self.flying[key] for key in flying],
                [self.kept[key] for key in kept],
                extra,
            )
        )
        for name, pieces in zip(names, values[0]):
            self.pieces[name] = [(j, v) for (j, _), (_, v) in zip(self.pieces[name], pieces)]
        self.kept = dict(zip(kept, values[2]))
        self.flying = {}
        for (kind, name), value in zip(flying, values[1]):
            if kind == "kept":
                self.kept[name] = value
                continue
            bit = self.order[name].pop(0)
            held = self.pieces[name]
            self.pieces[name] = held + [(j | bit, value[n]) for n, (j, _) in enumerate(held)]
            self.next(name)
        extra = values[3]
        return extra[0] if len(extra) == 1 else extra

    def whole(self, name):
        return name in self.pieces and not self.order[name]

    def take_half(self, name):
        pieces = dict(self.pieces.pop(name))
        return jnp.stack([pieces[2 * i] for i in range(self.nd // 2)])


def pack_kernel(index_ref, in_ref, out_ref):
    nd = index_ref.shape[0] - 1
    wide = in_ref.shape[2] // nd
    for p in range(nd):
        there = pl.ds(pl.multiple_of(index_ref[p] * wide, wide), wide)
        out_ref[:, p * wide : (p + 1) * wide] = in_ref[0, :, there]


def pack_features(value, index, which):
    micro, rows, width = value.shape
    nd = index.shape[0]
    if width // nd % 128:
        chunk = lax.dynamic_index_in_dim(value, which, 0, keepdims=False)
        return jnp.take(chunk.reshape(rows, nd, -1), index, axis=1).reshape(rows, width)
    return pl.pallas_call(
        pack_kernel,
        grid_spec=pltpu.PrefetchScalarGridSpec(
            num_scalar_prefetch=1,
            grid=(1,),
            in_specs=[pl.BlockSpec((1, rows, width), lambda i, index_ref: (index_ref[nd], 0, 0))],
            out_specs=pl.BlockSpec((rows, width), lambda i, index_ref: (0, 0)),
        ),
        out_shape=SHAPE((rows, width), value.dtype),
        compiler_params=params(),
        cost_estimate=cost(0, 6 * rows * width),
        name="pack_features",
    )(jnp.append(index, which.astype(jnp.int32)), value)


def unpack_kernel(index_ref, *refs):
    ins, out_ref = refs[:-1], refs[-1]
    nd = index_ref.shape[0] - len(ins)
    wide = out_ref.shape[2] // nd
    for k, in_ref in enumerate(ins):
        for p in range(nd):
            there = pl.ds(pl.multiple_of(index_ref[p] * wide, wide), wide)
            out_ref[index_ref[nd + k], :, there] = in_ref[:, p * wide : (p + 1) * wide]


def unpack_features(chunks, index, places):
    rows, width = chunks[0].shape
    micro, nd = len(chunks), index.shape[0]
    places = [place.astype(jnp.int32) for place in places]
    if width // nd % 128:
        back = jnp.argsort(index)
        stacked = jnp.stack(chunks).reshape(micro, rows, nd, -1)
        stacked = jnp.take(stacked, back, axis=2).reshape(micro, rows, width)
        return jnp.take(stacked, jnp.argsort(jnp.stack(places)), axis=0)
    return pl.pallas_call(
        unpack_kernel,
        in_specs=[pl.BlockSpec(memory_space=pltpu.SMEM)] + [WHOLE] * micro,
        out_specs=WHOLE,
        out_shape=SHAPE((micro, rows, width), chunks[0].dtype),
        compiler_params=params(),
        cost_estimate=cost(0, 4 * micro * rows * width),
        name="unpack_features",
    )(jnp.concatenate([index, jnp.stack(places)]), *chunks)


def standardize(state):
    centre = jnp.mean(state, axis=-1, keepdims=True)
    centred = state - centre
    spread = jnp.mean(centred * centred, axis=-1, keepdims=True)
    inverse = lax.rsqrt(spread + EPSILON)
    return centred * inverse, inverse


def norm_back(grad, state, gain):
    scaled, inverse = standardize(state)
    weighted = grad * gain
    first = jnp.mean(weighted, axis=-1, keepdims=True)
    second = jnp.mean(weighted * scaled, axis=-1, keepdims=True)
    sums = jnp.concatenate(
        [jnp.sum(grad * scaled, axis=0, keepdims=True), jnp.sum(grad, axis=0, keepdims=True)], 0
    )
    return inverse * (weighted - first - scaled * second), sums


def first_norm_kernel(micro, *refs):
    chunks = refs[:micro]
    gain_ref, bias_ref, x_ref, out_ref = refs[micro:]
    rows = chunks[0].shape[0]
    for k, ref in enumerate(chunks):
        here = slice(k * rows, (k + 1) * rows)
        x_ref[here] = ref[...]
        scaled, _ = standardize(ref[...].astype(F32))
        out_ref[here] = (scaled * gain_ref[...] + bias_ref[...]).astype(BF16)


def first_norm(chunks, gain, bias):
    rows, width = chunks[0].shape
    rows = rows * len(chunks)
    return pl.pallas_call(
        functools.partial(first_norm_kernel, len(chunks)),
        in_specs=[WHOLE] * (len(chunks) + 2),
        out_specs=[WHOLE] * 2,
        out_shape=[SHAPE((rows, width), BF16)] * 2,
        compiler_params=params(),
        cost_estimate=cost(0, 8 * rows * width),
        name="first_norm",
    )(*chunks, gain, bias)


def each_k(refs):
    return [(ref, n) for ref in refs for n in range(ref.shape[1])]


def proj_kernel(parts, in_ref, *refs):
    owns, others, out_ref = refs[:parts], refs[parts : 2 * parts], refs[-1]
    value = in_ref[...]
    half = value.shape[1] // 2
    wide = owns[0].shape[-1]
    for k, ((own, n), (other, _)) in enumerate(zip(each_k(owns), each_k(others))):
        first = own[:, n, 0].reshape(half, wide)
        second = other[:, n, 0].reshape(half, wide)
        total = dot_nn(value[:, :half], first) + dot_nn(value[:, half:], second)
        out_ref[0, :, k * wide : (k + 1) * wide] = total.astype(BF16)


def head_spec(array, count, index_map):
    chips, ks, _, deep, wide = array.shape
    return pl.BlockSpec((chips, ks, count, deep, wide), index_map)


def project(value, weights, start, count):
    rows, width = value.shape
    wide = weights[0][0].shape[-1]
    nm = sum(array.shape[1] for array in weights[0])
    arrays = [*weights[0], *weights[1]]
    return pl.pallas_call(
        functools.partial(proj_kernel, len(weights[0])),
        grid=(count,),
        in_specs=[pl.BlockSpec((rows, width), lambda i: (0, 0))]
        + [head_spec(array, 1, lambda i: (0, 0, start + i, 0, 0)) for array in arrays],
        out_specs=pl.BlockSpec((1, rows, nm * wide), lambda i: (i, 0, 0)),
        out_shape=SHAPE((count, rows, nm * wide), BF16),
        compiler_params=params(),
        cost_estimate=cost(2 * count * rows * width * nm * wide, 2 * count * rows * width),
        name="project",
    )(value, *arrays)


def attend_kernel(parts, q_ref, *refs):
    k_refs, v_refs = refs[:parts], refs[parts : 2 * parts]
    bias_ref, out_ref, lse_ref = refs[2 * parts :]
    rows = q_ref.shape[1]
    low = lax.broadcasted_iota(jnp.int32, (1, PAIR), 1) < HDIM
    query = q_ref[0] * jnp.asarray(HDIM ** (-0.5), BF16)
    mixed = None
    for head in range(2):
        mine = low if head == 0 else jnp.logical_not(low)
        q_mine = jnp.where(mine, query, jnp.zeros_like(query))
        scores = [
            jnp.where(bias_ref[p : p + 1, :] < 0.0, MASKED, dot_nt(q_mine, k_refs[p][0]))
            for p in range(parts)
        ]
        top = functools.reduce(
            jnp.maximum, [jnp.max(part, axis=1, keepdims=True) for part in scores]
        )
        total, part = 0.0, 0.0
        for p in range(parts):
            expo = jnp.exp(scores[p] - top)
            total = total + jnp.sum(expo, axis=1, keepdims=True)
            part = part + dot_nn(expo.astype(BF16), v_refs[p][0])
        part = part / total
        mixed = part if head == 0 else jnp.where(low, mixed, part)
        lse = top + jnp.log(total)
        lse_ref[0, head : head + 1, :] = jnp.transpose(jnp.broadcast_to(lse, (rows, 128)))[0:1, :]
    out_ref[...] = mixed.astype(BF16)


def attend(query, kvs, bias, start, count):
    _, rows, width = query.shape
    parts = len(kvs)
    block = row_block(rows)
    keys = rows * parts
    key_spec = pl.BlockSpec((1, rows, PAIR), lambda h, i: (0, 0, start + h))
    value_spec = pl.BlockSpec((1, rows, PAIR), lambda h, i: (1, 0, start + h))
    return pl.pallas_call(
        functools.partial(attend_kernel, parts),
        grid=(count, rows // block),
        in_specs=[pl.BlockSpec((1, block, PAIR), lambda h, i: (0, i, start + h))]
        + [key_spec] * parts
        + [value_spec] * parts
        + [pl.BlockSpec((parts, rows), lambda h, i: (0, 0))],
        out_specs=[
            pl.BlockSpec((block, PAIR), lambda h, i: (i, h)),
            pl.BlockSpec((1, 2, block), lambda h, i: (h, 0, i)),
        ],
        out_shape=[SHAPE((rows, count * PAIR), BF16), SHAPE((count, 2, rows), F32)],
        compiler_params=params(),
        cost_estimate=cost(16 * rows * keys * count * PAIR, 8 * keys * count * PAIR),
        name="attend",
    )(query, *kvs, *kvs, bias)


def attend_back_kernel(parts, q_ref, *refs):
    k_refs, v_refs = refs[:parts], refs[parts : 2 * parts]
    bias_ref, lse_ref, mixed_ref, grad_ref, dq_ref = refs[2 * parts : 2 * parts + 5]
    dkv_refs = refs[2 * parts + 5 : 3 * parts + 5]
    dk_acc, dv_acc = refs[3 * parts + 5 :]
    step = pl.program_id(1)
    low = lax.broadcasted_iota(jnp.int32, (1, PAIR), 1) < HDIM
    query = q_ref[0] * jnp.asarray(HDIM ** (-0.5), BF16)
    grad = grad_ref[0]
    product = mixed_ref[...].astype(F32) * grad.astype(F32)

    @pl.when(step == 0)
    def _():
        dk_acc[...] = jnp.zeros_like(dk_acc)
        dv_acc[...] = jnp.zeros_like(dv_acc)

    grad_query = None
    for head in range(2):
        mine = low if head == 0 else jnp.logical_not(low)
        q_mine = jnp.where(mine, query, jnp.zeros_like(query))
        g_mine = jnp.where(mine, grad, jnp.zeros_like(grad))
        delta = jnp.sum(jnp.where(mine, product, 0.0), axis=1, keepdims=True)
        delta = jnp.transpose(jnp.broadcast_to(delta, (delta.shape[0], 128)))[0:1, :]
        query_part = 0.0
        for p in range(parts):
            keys, values = k_refs[p][0], v_refs[p][0]
            scores = jnp.where(bias_ref[p] < 0.0, MASKED, dot_nt(keys, q_mine))
            probs = jnp.exp(scores - lse_ref[0, head : head + 1, :])
            upstream = dot_nt(values, g_mine)
            grad_scores = (probs * (upstream - delta)).astype(BF16)
            dv_acc[p] += dot_nn(probs.astype(BF16), g_mine)
            dk_acc[p] += dot_nn(grad_scores, q_mine)
            query_part = query_part + dot_tn(grad_scores, keys)
        grad_query = query_part if head == 0 else jnp.where(low, grad_query, query_part)
    dq_ref[...] = (grad_query * HDIM ** (-0.5)).astype(BF16)

    @pl.when(step == pl.num_programs(1) - 1)
    def _():
        for p in range(parts):
            dkv_refs[p][0] = dk_acc[p].astype(BF16)
            dkv_refs[p][1] = dv_acc[p].astype(BF16)


def attend_back(query, kvs, bias, lse, mixed, grad, start, count):
    _, rows, width = query.shape
    parts = len(kvs)
    block = row_block(rows)
    keys = rows * parts
    key_spec = pl.BlockSpec((1, rows, PAIR), lambda h, i: (0, 0, start + h))
    value_spec = pl.BlockSpec((1, rows, PAIR), lambda h, i: (1, 0, start + h))
    return pl.pallas_call(
        functools.partial(attend_back_kernel, parts),
        grid=(count, rows // block),
        in_specs=[pl.BlockSpec((1, block, PAIR), lambda h, i: (0, i, start + h))]
        + [key_spec] * parts
        + [value_spec] * parts
        + [
            pl.BlockSpec((parts, rows, 1), lambda h, i: (0, 0, 0)),
            pl.BlockSpec((1, 2, block), lambda h, i: (h, 0, i)),
            pl.BlockSpec((block, PAIR), lambda h, i: (i, h)),
            pl.BlockSpec((1, block, PAIR), lambda h, i: (0, i, start + h)),
        ],
        out_specs=[pl.BlockSpec((block, PAIR), lambda h, i: (i, h))]
        + [pl.BlockSpec((2, rows, PAIR), lambda h, i: (0, 0, h))] * parts,
        out_shape=[SHAPE((rows, count * PAIR), BF16)]
        + [SHAPE((2, rows, count * PAIR), BF16)] * parts,
        scratch_shapes=[pltpu.VMEM((parts, rows, PAIR), F32)] * 2,
        compiler_params=params(),
        cost_estimate=cost(40 * rows * keys * count * PAIR, 16 * keys * count * PAIR),
        name="attend_back",
    )(query, *kvs, *kvs, bias, lse, mixed, grad)


def middle_kernel(nm, parts, x_ref, *refs):
    mixed_refs, refs = refs[:nm], refs[nm:]
    weights = refs[:parts], refs[parts : 2 * parts]
    gain_ref, bias_ref, mid_ref, out_ref = refs[2 * parts :]
    half = x_ref.shape[1] // 2
    sides = []
    for side in weights:
        total = 0.0
        for k, (ref, n) in enumerate(each_k(side)):
            total = total + dot_nt(mixed_refs[k][...], ref[:, n, 0].reshape(half, -1))
        sides.append(total)
    middle = x_ref[...].astype(F32) + jnp.concatenate(sides, axis=1)
    mid_ref[...] = middle
    scaled, _ = standardize(middle)
    out_ref[...] = (scaled * gain_ref[...] + bias_ref[...]).astype(BF16)


def middle_norm(x, mixed, weights, which, gain, bias):
    rows, width = x.shape
    nm, wide = len(mixed), mixed[0].shape[1]
    block = row_block(rows)
    vector = pl.BlockSpec((1, width), lambda i: (0, 0))
    line = pl.BlockSpec((block, width), lambda i: (i, 0))
    arrays = [*weights[0], *weights[1]]
    return pl.pallas_call(
        functools.partial(middle_kernel, nm, len(weights[0])),
        grid=(rows // block,),
        in_specs=[line]
        + [pl.BlockSpec((block, wide), lambda i: (i, 0))] * nm
        + [head_spec(array, 1, lambda i: (0, 0, which, 0, 0)) for array in arrays]
        + [vector, vector],
        out_specs=[line, line],
        out_shape=[SHAPE((rows, width), F32), SHAPE((rows, width), BF16)],
        compiler_params=params(),
        cost_estimate=cost(2 * rows * width * nm * wide, 14 * x.size),
        name="middle_norm",
    )(x, *mixed, *arrays, gain, bias)


def load_weights(firsts, sizes, index_ref, refs, held, sems):
    step = pl.program_id(0)
    nm = firsts + sum(sizes)
    chips = held.shape[2]
    copies, refs = {k: [] for k in range(nm)}, list(refs)

    def add(k, source, w, side, n, sem):
        copies[k].append(
            pltpu.make_async_copy(source, held.at[w, 2 * k + side, n], sems.at[w, 2 * k + side, sem])
        )

    ref = refs.pop(0)
    for k in range(firsts):
        for w in range(2):
            for side in range(2):
                for n in range(chips):
                    add(k, ref.at[index_ref[side * chips + n], k, w], w, side, n, n)
    k = firsts
    for size in sizes:
        sides = [refs.pop(0) for _ in range(4)]
        for i in range(size):
            for n, ref in enumerate(sides):
                add(k, ref.at[:, i], n // 2, n % 2, slice(None), 0)
            k += 1

    @pl.when(step == 0)
    def _():
        for k in range(nm):
            for copy in copies[k]:
                copy.start()

    for k in range(nm):

        @pl.when(step == k)
        def _():
            for copy in copies[k]:
                copy.wait()


def feed_kernel(firsts, sizes, index_ref, *refs):
    nm, count = firsts + sum(sizes), 1 + 4 * len(sizes)
    in_ref, mid_ref, out_ref, act_ref, slope_ref, held, acc, sems = refs[count:]
    step = pl.program_id(0)
    load_weights(firsts, sizes, index_ref, refs[:count], held, sems)
    half = in_ref.shape[1] // 2
    up = [held[0, 2 * step + side].reshape(half, -1) for side in range(2)]
    down = [held[1, 2 * step + side].reshape(half, -1) for side in range(2)]

    @pl.when(step == 0)
    def _():
        acc[...] = mid_ref[...]

    hidden = dot_nn(in_ref[:, :half], up[0]) + dot_nn(in_ref[:, half:], up[1])
    below = 0.5 + 0.5 * lax.erf(hidden * (0.5**0.5))
    density = jnp.exp(-0.5 * hidden * hidden) * 0.3989422804014327
    active = (hidden * below).astype(BF16)
    act_ref[0] = active
    slope_ref[0] = (below + hidden * density).astype(BF16)
    acc[:, :half] += dot_nt(active, down[0])
    acc[:, half:] += dot_nt(active, down[1])

    @pl.when(step == nm - 1)
    def _():
        out_ref[...] = acc[...].astype(BF16)


def feed(normed, middle, index, firsts, sizes, weights):
    rows, width = normed.shape
    nm = firsts + sum(sizes)
    nd, (deep, hidden) = index.shape[0], weights[0].shape[3:]
    chips = nd // 2
    line = pl.BlockSpec((rows, width), lambda k: (0, 0))
    wide = pl.BlockSpec((1, rows, hidden), lambda k: (k, 0, 0))
    return pl.pallas_call(
        functools.partial(feed_kernel, firsts, sizes),
        grid=(nm,),
        in_specs=[pl.BlockSpec(memory_space=pltpu.SMEM)]
        + [ANY] * len(weights)
        + [line, line],
        out_specs=[line, wide, wide],
        out_shape=[SHAPE((rows, width), BF16)] + [SHAPE((nm, rows, hidden), BF16)] * 2,
        scratch_shapes=[
            pltpu.VMEM((2, 2 * nm, chips, deep, hidden), BF16),
            pltpu.VMEM((rows, width), F32),
            pltpu.SemaphoreType.DMA((2, 2 * nm, chips)),
        ],
        compiler_params=params(60),
        cost_estimate=cost(4 * rows * width * nm * hidden, 4 * nm * width * hidden),
        name="feed",
    )(index, *weights, normed, middle)


def feed_back_kernel(firsts, sizes, index_ref, *refs):
    nm, count = firsts + sum(sizes), 1 + 4 * len(sizes)
    g_ref, slope_ref, mid_ref, gain_ref = refs[count : count + 4]
    hid_ref, gmid_ref, attn_ref, sums_ref, held, acc, sems = refs[count + 4 :]
    step = pl.program_id(0)
    load_weights(firsts, sizes, index_ref, refs[:count], held, sems)
    half = g_ref.shape[1] // 2
    up = [held[0, 2 * step + side].reshape(half, -1) for side in range(2)]
    down = [held[1, 2 * step + side].reshape(half, -1) for side in range(2)]
    active = dot_nn(g_ref[:, :half], down[0]) + dot_nn(g_ref[:, half:], down[1])
    hidden = (active * slope_ref[0].astype(F32)).astype(BF16)
    hid_ref[0] = hidden
    first, second = dot_nt(hidden, up[0]), dot_nt(hidden, up[1])

    @pl.when(step == 0)
    def _():
        acc[:, :half] = first
        acc[:, half:] = second

    @pl.when(step > 0)
    def _():
        acc[:, :half] += first
        acc[:, half:] += second

    @pl.when(step == nm - 1)
    def _():
        into, sums = norm_back(acc[...], mid_ref[...], gain_ref[...])
        result = g_ref[...].astype(F32) + into
        gmid_ref[...] = result
        attn_ref[...] = result.astype(BF16)
        sums_ref[...] = sums


def feed_back(grad, slope, middle, gain, index, firsts, sizes, weights):
    rows, width = grad.shape
    nm = firsts + sum(sizes)
    nd, (deep, hidden) = index.shape[0], weights[0].shape[3:]
    chips = nd // 2
    line = pl.BlockSpec((rows, width), lambda k: (0, 0))
    wide = pl.BlockSpec((1, rows, hidden), lambda k: (k, 0, 0))
    return pl.pallas_call(
        functools.partial(feed_back_kernel, firsts, sizes),
        grid=(nm,),
        in_specs=[pl.BlockSpec(memory_space=pltpu.SMEM)]
        + [ANY] * len(weights)
        + [line, wide, line, pl.BlockSpec((1, width), lambda k: (0, 0))],
        out_specs=[
            wide,
            line,
            line,
            pl.BlockSpec((2, width), lambda k: (0, 0)),
        ],
        out_shape=[
            SHAPE((nm, rows, hidden), BF16),
            SHAPE((rows, width), F32),
            SHAPE((rows, width), BF16),
            SHAPE((2, width), F32),
        ],
        scratch_shapes=[
            pltpu.VMEM((2, 2 * nm, chips, deep, hidden), BF16),
            pltpu.VMEM((rows, width), F32),
            pltpu.SemaphoreType.DMA((2, 2 * nm, chips)),
        ],
        compiler_params=params(60),
        cost_estimate=cost(4 * rows * width * nm * hidden, 4 * nm * width * hidden),
        name="feed_back",
    )(index, *weights, grad, slope, middle, gain)


def wide_grad_kernel(place_ref, a_ref, b_ref, out_ref):
    part = dot_tn(a_ref[...], b_ref[0]).astype(BF16)
    nd, deep = out_ref.shape[0], out_ref.shape[2]
    for p in range(nd):
        out_ref[place_ref[p], 0] = part[p * deep : (p + 1) * deep]


def wide_grad(rows_in, values, place, absolute):
    rows, width = rows_in.shape
    nm, _, hidden = values.shape
    nd = place.shape[0] - 1
    block = min(512, hidden)

    def out_map(k, i, place_ref):
        return (0, lax.rem(place_ref[nd] + nm - k, nm) if absolute else k, 0, i)

    return pl.pallas_call(
        wide_grad_kernel,
        grid_spec=pltpu.PrefetchScalarGridSpec(
            num_scalar_prefetch=1,
            grid=(nm, hidden // block),
            in_specs=[
                pl.BlockSpec((rows, width), lambda k, i, place_ref: (0, 0)),
                pl.BlockSpec((1, rows, block), lambda k, i, place_ref: (k, 0, i)),
            ],
            out_specs=pl.BlockSpec((nd, 1, width // nd, block), out_map),
        ),
        out_shape=SHAPE((nd, nm, width // nd, hidden), BF16),
        compiler_params=params(),
        cost_estimate=cost(2 * nm * width * rows * hidden, 4 * nm * width * hidden),
        name="wide_grad",
    )(place, rows_in, values)


def head_grad_kernel(
    n_ref, g_ref, mixed_ref, dq_ref, dkv_ref, came_ref, sum_ref, keep_ref, give_ref
):
    chips, _, deep, wide = keep_ref.shape
    half = chips * deep
    total = (dkv_ref[...].astype(F32) + came_ref[...].astype(F32)).astype(BF16)
    sum_ref[...] = total
    three = dot_tn(n_ref[...], jnp.concatenate([dq_ref[...], total[0], total[1]], axis=1))
    one = dot_tn(g_ref[...], mixed_ref[...])
    parts = (three[:, :wide], one, three[:, wide : 2 * wide], three[:, 2 * wide :])
    for i, part in enumerate(parts):
        part = part.astype(BF16)
        keep_ref[:, i] = part[:half].reshape(chips, deep, wide)
        give_ref[:, i] = part[half:].reshape(chips, deep, wide)


def head_grad(normed, attn, mixed, dq, dkv, came, chips):
    rows, width = normed.shape
    wide = dq.shape[1]
    piece = SHAPE((chips, 4, width // 2 // chips, wide), BF16)
    total, keep, give = pl.pallas_call(
        head_grad_kernel,
        in_specs=[WHOLE] * 6,
        out_specs=[WHOLE] * 3,
        out_shape=[SHAPE(dkv.shape, BF16), piece, piece],
        compiler_params=params(),
        cost_estimate=cost(8 * width * rows * wide, 8 * width * wide),
        name="head_grad",
    )(normed, attn, mixed, dq, dkv, came)
    return total, keep[None], give[None]


def first_back_kernel(nm, parts, x_ref, gmid_ref, gain_ref, *refs):
    dqs, dkvs, came_ref, refs = refs[:nm], refs[nm : 2 * nm], refs[2 * nm], refs[2 * nm + 1 :]
    qo = refs[:parts], refs[parts : 2 * parts]
    kv = refs[2 * parts : 3 * parts], refs[3 * parts : 4 * parts]
    out_ref, sums_ref = refs[4 * parts :]
    last = (dkvs[0][...].astype(F32) + came_ref[...].astype(F32)).astype(BF16)
    half = x_ref.shape[1] // 2
    sides = []
    for side in range(2):
        total = 0.0
        for k, ((qo_ref, n), (kv_ref, _)) in enumerate(zip(each_k(qo[side]), each_k(kv[side]))):
            total = total + dot_nt(dqs[k][...], qo_ref[:, n, 0].reshape(half, -1))
            for i in range(2):
                dkv = dkvs[k][i] if k else last[i]
                total = total + dot_nt(dkv, kv_ref[:, n, i].reshape(half, -1))
        sides.append(total)
    into, sums = norm_back(jnp.concatenate(sides, axis=1), x_ref[...].astype(F32), gain_ref[...])
    out_ref[...] = (gmid_ref[...] + into).astype(BF16)
    sums_ref[...] = sums


def first_back(x, gmid, gain, dqs, dkvs, came, qo, kv, part, block):
    width = x.shape[1]
    nm, wide = len(dqs), dqs[0].shape[1]
    line = pl.BlockSpec((block, width), lambda i: (part, 0))
    still = lambda i: (0, 0, 0, 0, 0)
    qo_arrays, kv_arrays = [*qo[0], *qo[1]], [*kv[0], *kv[1]]
    return pl.pallas_call(
        functools.partial(first_back_kernel, nm, len(qo[0])),
        grid=(1,),
        in_specs=[line, line, pl.BlockSpec((1, width), lambda i: (0, 0))]
        + [pl.BlockSpec((block, wide), lambda i: (part, 0))] * nm
        + [pl.BlockSpec((2, block, wide), lambda i: (0, part, 0))] * (nm + 1)
        + [head_spec(array, 1, still) for array in qo_arrays]
        + [head_spec(array, 2, still) for array in kv_arrays],
        out_specs=[
            pl.BlockSpec((block, width), lambda i: (0, 0)),
            pl.BlockSpec((2, width), lambda i: (0, 0)),
        ],
        out_shape=[SHAPE((block, width), BF16), SHAPE((2, width), F32)],
        compiler_params=params(),
        cost_estimate=cost(6 * block * width * nm * wide, 12 * block * width),
        name="first_back",
    )(x, gmid, gain, *dqs, *dkvs, came, *qo_arrays, *kv_arrays)


def add_low(a, b):
    return (a.astype(F32) + b.astype(F32)).astype(BF16)


def add_parts_kernel(pairs, *refs):
    outs, row = refs[2 * pairs :], 0
    for i in range(pairs):
        keep_ref, came_ref = refs[2 * i : 2 * i + 2]
        size = keep_ref.shape[0]
        for n, out in enumerate(outs):
            out[row : row + size] = add_low(keep_ref[:, n + 1], came_ref[:, n + 1])
        row += size


def add_parts(pairs):
    keep = pairs[0][0]
    rows = sum(pair[0].shape[0] for pair in pairs)
    piece = SHAPE((rows,) + keep.shape[2:], keep.dtype)
    return pl.pallas_call(
        functools.partial(add_parts_kernel, len(pairs)),
        in_specs=[WHOLE] * (2 * len(pairs)),
        out_specs=[WHOLE] * (keep.shape[1] - 1),
        out_shape=[piece] * (keep.shape[1] - 1),
        compiler_params=params(),
        cost_estimate=cost(0, 6 * len(pairs) * keep.size),
        name="add_parts",
    )(*[array for pair in pairs for array in pair])


class Scatter:
    def __init__(self, nd, nm, bits):
        self.nd, self.nm = nd, nm
        self.queue = {1: [], **{bit: [] for bit in bits}, "direct": [], "z": []}
        self.order, self.kept, self.waits, self.flying = {}, {}, {}, {}
        self.ends, self.came, self.done, self.rings, self.joined = {}, {}, {}, {}, {}

    def add(self, name, ks, keep, give, order, rings=True):
        self.order[name, tuple(ks)], self.rings[name] = order, rings
        self.push(1, (name, tuple(ks), -1), list(range(0, self.nd, 2)), keep, give)

    def add_line(self, name, value, rings):
        self.rings[name] = rings
        if rings:
            for k in range(self.nm):
                self.ends[name, k] = (value[k],)
            self.advance(name, self.nm - 1)
            return
        self.ends[name] = [value[0]]
        for k in sorted(range(1, self.nm), key=lambda k: min(k, self.nm - k)):
            self.waits[name, k, "z"] = value[k]
            self.queue["z"].append((name, k, "z"))

    def push(self, link, key, places, keep, give):
        self.kept[key], self.waits[key] = (places, keep), give
        self.queue[link].append(key)

    def launch(self, core=1, chip=1, direct=1, z=1):
        for link, tasks in self.queue.items():
            for _ in range({1: core, "direct": direct, "z": z}.get(link, chip)):
                if not tasks:
                    break
                key = tasks.pop(0)
                value = self.waits.pop(key)
                if link == "z" and not self.rings[key[0]]:
                    value = ring(value, -key[1], self.nm)
                elif link == "z":
                    value = ring(value, -1, self.nm)
                elif link == "direct":
                    more = [tasks.pop(0) for _ in range(min(direct - 1, len(tasks)))]
                    self.joined[key] = more
                    value = add_parts([value] + [self.waits.pop(other) for other in more])
                    value = [swap(part, 2 * n + 2, self.nd) for n, part in enumerate(value)]
                    self.flying[key] = value
                    break
                else:
                    value = swap(value, link, self.nd)
                self.flying[key] = value

    def busy(self):
        return bool(self.flying) or any(self.queue.values())

    def land(self, *extra):
        waits, flying = list(self.waits), list(self.flying)
        values = lax.optimization_barrier(
            ([self.waits[key] for key in waits], [self.flying[key] for key in flying], extra)
        )
        self.waits = dict(zip(waits, values[0]))
        came = dict(zip(flying, values[1]))
        self.flying = {}
        for key, value in came.items():
            if key not in self.joined:
                self.arrive(key, value)
                continue
            for other in [key] + self.joined.pop(key):
                self.arrive(other, [part[: len(other[1])] for part in value])
                value = [part[len(other[1]) :] for part in value]
        extra = values[2]
        return extra[0] if len(extra) == 1 else extra

    def arrive(self, key, value):
        name, ks, stage = key
        if stage == "z" and not self.rings[name]:
            self.ends[name].append(value)
            if len(self.ends[name]) == self.nm:
                self.done[name] = sum(part.astype(F32) for part in self.ends.pop(name))
            return
        if stage == "z":
            self.came[name, ks - 1] = value
            self.advance(name, ks - 1)
            return
        order = self.order[name, ks]
        places, keep = self.kept.pop(key)
        if order is None and stage == -1:
            own = (keep[:, 0], value[:, 0])
            self.push("direct", (name, ks, 0), own, None, (keep, value))
            return
        if order is None:
            for n, k in enumerate(ks):
                self.ends[name, k] = tuple(part[n] for part in [*places, *value])
                self.advance(name, k)
            return
        if stage + 1 == len(order):
            for n, k in enumerate(ks):
                self.ends[name, k] = (keep[n, 0], value[n, 0])
            for k in reversed(ks):
                self.advance(name, k)
            return
        bit = order[stage + 1]
        stays = [n for n, j in enumerate(places) if not j & bit]
        goes = [n for n, j in enumerate(places) if j & bit]

        def take(array, which):
            return jnp.stack([array[:, n] for n in which], axis=1)

        self.push(
            bit,
            (name, ks, stage + 1),
            [places[n] for n in stays],
            add_low(take(keep, stays), take(value, stays)),
            add_low(take(keep, goes), take(value, goes)),
        )

    def advance(self, name, k):
        if (name, k) not in self.ends or (k < self.nm - 1 and (name, k) not in self.came):
            return
        total = sum(part.astype(F32) for part in self.ends.pop((name, k)))
        if k < self.nm - 1:
            total = total + self.came.pop((name, k)).astype(F32)
        if k:
            key = (name, k, "z")
            self.waits[key] = total.astype(BF16)
            self.queue["z"].append(key)
        else:
            self.done[name] = total


def shards(nd, nm, tokens, views, norm_gains, norm_biases, w_proj, w_out, w_up, w_down, cotangent):
    micro, _, chunk, width = tokens.shape
    ranks = nm // micro
    half = max(ranks // 2, 1)
    rows = micro * chunk
    chips = nd // 2
    wide = w_out.shape[2]
    per_k = wide // PAIR
    hidden = w_up.shape[2]
    dp, mp = lax.axis_index("dp"), lax.axis_index("mp")
    group = mp // half
    step_here = group // 2
    rank = (dp & 1) + 2 * (mp % half)
    order_of = [2 * (p % chips) + p // chips for p in range(nd)]
    offsets = jnp.asarray(order_of, jnp.int32)
    index = dp.astype(jnp.int32) ^ offsets

    def routes(k):
        pairs = []
        for d in range(nd):
            for z in range(nm):
                m = (k + z) % micro
                r = z // micro
                to_d = (d & ~1) | (r & 1)
                to_z = (2 * m + (d & 1)) * half + r // 2
                pairs.append((d * nm + z, to_d * nm + to_z))
        return pairs

    there = ((dp & ~1) | ((mp // micro) & 1)).astype(jnp.int32) ^ offsets

    def pack(value, k):
        return pack_features(value, there, (k + mp) % micro)

    def send(packed, k):
        return lax.ppermute(packed[k], ("dp", "mp"), routes(k))

    def back_routes(k):
        return [(b, a) for a, b in routes(k)]

    def send_chunk(chunks, k):
        return lax.ppermute(chunks[k], ("dp", "mp"), back_routes(k))

    def unpack(came):
        return unpack_features(came, there, [(k + mp) % micro for k in range(micro)])

    def by_place(vector):
        return jnp.take(vector.reshape(-1, nd, width // nd), index, axis=1).reshape(-1, width)

    flow = Flow(nd, nm)
    forth, back = flow.bits, flow.bits[::-1]
    firsts = min(2, nm)
    groups = [list(range(k, min(k + 2, nm))) for k in range(firsts, nm, 2)]
    sizes = tuple(len(group) for group in groups)
    head = [jnp.concatenate([w_proj[0], w_out])]
    feeds = [jnp.concatenate([w_up, w_down])]
    gather = functools.partial(lax.all_gather, axis_name="dp")
    head_groups = [[0], list(range(1, nm))]

    def headed(n):
        flow.add(f"qo{n}", jnp.stack([head[k][::3] for k in head_groups[n]]), forth)
        flow.add(f"kv{n}", jnp.stack([head[k][1:3] for k in head_groups[n]]), back)

    halves = {}

    def core_halves(most, names):
        for name in names:
            if most and flow.whole(name):
                halves[name] = flow.take_half(name)
                flow.fly(name, swap(halves[name], 1, nd))
                most -= 1

    for k in sorted(range(1, nm), key=lambda k: -min(k, nm - k)):
        flow.fly(("head", k), ring(head[0], k, nm))
    headed(0)
    flow.launch()
    token_parts = [pack(tokens[:, 0], k) for k in range(micro)]
    view = lax.dynamic_index_in_dim(views[:, 0], mp % micro, 0, keepdims=True)
    head, tokens, token_parts, cotangent, there, view, feeds, norm_gains, norm_biases = flow.land(
        head, tokens, token_parts, cotangent, there, view, feeds, norm_gains, norm_biases
    )
    head += [flow.kept.pop(("head", k)) for k in range(1, nm)]
    headed(1)
    weights = []
    came = []
    head_names = [f"{name}{n}" for n in range(len(head_groups)) for name in ("kv", "qo")]
    while len(came) < micro or not all(n in halves or flow.whole(n) for n in head_names):
        if len(came) < micro:
            came.append(send(token_parts, len(came)))
        flow.launch(chip=2)
        if len(came) == micro:
            core_halves(2, head_names)
        if len(came) == 1:
            grad_parts = [pack(cotangent[:, 0], k) for k in range(micro)]
            gains, biases = by_place(norm_gains[0]), by_place(norm_biases[0])
        came, token_parts, grad_parts, feeds, halves, gains, biases, view = flow.land(
            came, token_parts, grad_parts, feeds, halves, gains, biases, view
        )

    def turn():
        if len(feeds) < nm:
            feeds.append(ring(feeds[-1], 1, nm))

    def turned():
        if not weights and len(feeds) >= firsts:
            weights.append(gather(jnp.stack(feeds[:firsts])))
        for n, group in enumerate(groups):
            if f"up{n}" not in flow.order and group[-1] < len(feeds):
                flow.add(f"up{n}", jnp.stack([feeds[k][0] for k in group]), forth)
                flow.add(f"down{n}", jnp.stack([feeds[k][1] for k in group]), back)

    last = [f"{name}{n}" for n in range(len(groups)) for name in ("up", "down")]
    core_halves(len(head_names), head_names)
    turn()
    x, normed = first_norm(came, gains[:1], biases[:1])
    x, normed, halves, feeds, view = flow.land(x, normed, halves, feeds, view)
    turned()

    def both(name):
        names = [f"{name}{n}" for n in range(len(head_groups))]
        return [halves.pop(n) for n in names], [flow.kept.pop(n) for n in names]

    qo, kv = both("qo"), both("kv")

    turn()
    flow.launch()
    views = lax.ppermute(view, ("dp", "mp"), routes(0))
    own_kv = project(normed, kv, 0, 2)
    own_kv, normed, qo, feeds, views = flow.land(own_kv, normed, qo, feeds, views)
    turned()

    def swap_rank(value, bit):
        if bit == 1:
            return swap(value, 1, nd)
        return lax.ppermute(value, "mp", [(i, i ^ (bit >> 1)) for i in range(nm)])

    rank_bits = [1 << b for b in range(ranks.bit_length() - 1)]
    kvs = {0: own_kv}
    for bit in rank_bits:
        for j in list(kvs):
            kvs[j | bit] = swap_rank(kvs[j], bit)
    kvs = [kvs[j] for j in range(ranks)]
    turn()
    flow.launch()
    query = project(normed, qo, 0, 1)
    slot = jnp.stack([(step_here - t) % micro for t in range(micro)])
    within = (slot[:, None] * chunk + jnp.arange(chunk)[None]).reshape(-1)
    position = jnp.stack([(rank ^ j) * rows + within for j in range(ranks)])
    bias = jnp.where(position < TRI + views[0] * VIEW_TOK, 0.0, -1.0).astype(F32)
    kvs, query, bias, grad_parts, feeds = flow.land(kvs, query, bias, grad_parts, feeds)
    turned()

    grad_came, mixed, lses = [], [], []
    at_once = max(nm // 2, 1)
    while len(mixed) < nm or len(grad_came) < micro or not all(
        name in halves or flow.whole(name) for name in last
    ):
        turn()
        flow.launch()
        if len(grad_came) < micro:
            grad_came.append(send(grad_parts, len(grad_came)))
        core_halves(2, last)
        for k in range(len(mixed), min(len(mixed) + at_once, nm)):
            part, lse = attend(query, kvs, bias, k * per_k, per_k)
            mixed.append(part)
            lses.append(lse)
        mixed, query, halves, grad_parts, grad_came, feeds = flow.land(
            mixed, query, halves, grad_parts, grad_came, feeds
        )
        turned()
    core_halves(len(last), last)
    middle, normed_two = middle_norm(x, mixed, qo, 1, gains[1:], biases[1:])
    grad = jnp.concatenate(grad_came)
    middle, normed_two, halves, grad = flow.land(middle, normed_two, halves, grad)
    for name in last:
        weights += [halves[name], flow.kept.pop(name)]

    result, active, slope = feed(normed_two, middle, index, firsts, sizes, weights)
    out_chunks = result.reshape((micro, chunk, width))
    output = []

    sums = Scatter(nd, nm, flow.bits)
    output = [send_chunk(out_chunks, 0)]
    over_dp = functools.partial(lax.psum_scatter, axis_name="dp", scatter_dimension=0, tiled=True)
    place = jnp.append(index, mp.astype(jnp.int32))
    grads_down = over_dp(wide_grad(grad, active, place, False))
    hid, gmid, attn, sums_two = feed_back(
        grad, slope, middle, gains[1:], index, firsts, sizes, weights
    )
    hid, gmid, attn, sums_two, normed_two, output, out_chunks = sums.land(
        hid, gmid, attn, sums_two, normed_two, output, out_chunks
    )
    grads_up = over_dp(wide_grad(normed_two, hid, place, True))[0]
    grads_up = lax.psum_scatter(grads_up, "mp", scatter_dimension=0, tiled=True)
    grad_mixed = project(attn, qo, 1, 1)

    dqs, dkvs = {}, {}
    bias_tall = bias[:, :, None]
    closing = list(range(nm))
    dkv_part, dkv_came = {}, {}

    def head_grads():
        if not closing or closing[-1] not in dkv_came:
            return None
        k = closing.pop()
        dkvs[k], keep, give = head_grad(
            normed, attn, mixed[k], dqs[k], dkv_part[k], dkv_came[k], chips
        )
        return k, (keep, give)

    def add_heads(ready, outs):
        sums.add("head", [ready[0]], outs[0], outs[1], None)

    def exchange(parts):
        parts = dict(enumerate(parts))
        came = None
        for bit in rank_bits[::-1]:
            if came is not None:
                parts = {j: add_low(part, came[j]) for j, part in parts.items()}
            came = {j ^ bit: swap_rank(parts.pop(j), bit) for j in list(parts) if j & bit}
        return parts[0], came[0]

    parts = None
    for k in list(reversed(range(nm))) + [-1]:
        if k == 0:
            sums.add_line("down", grads_down[0], rings=False)
        sums.launch(direct=1 if k < 0 else 0, z=nm - 1)
        while k >= 0 and len(output) < min(micro, nm - k + 1):
            output.append(send_chunk(out_chunks, len(output)))
        ready = head_grads()
        if parts is not None:
            dkv_part[k + 1], dkv_came[k + 1] = exchange(parts)
            parts = None
        if k >= 0:
            dqs[k], *parts = attend_back(
                query, kvs, bias_tall, lses[k], mixed[k], grad_mixed, k * per_k, per_k
            )
        live = (ready and ready[1], dqs, parts, query, dkv_part, dkv_came, dkvs, gmid)
        live = sums.land(*live, output)
        outs, dqs, parts, query, dkv_part, dkv_came, dkvs, gmid, output = live
        if ready:
            add_heads(ready, outs)

    sums.launch()
    ready = head_grads()

    def first_part(part):
        return first_back(
            x,
            gmid,
            gains[:1],
            [dqs[k] for k in range(nm)],
            [dkvs[k] if k else dkv_part[k] for k in range(nm)],
            dkv_came[0],
            qo,
            kv,
            part,
            chunk,
        )

    firsts_back = [first_part(0)]
    firsts_back, outs, output, gmid = sums.land(firsts_back, ready and ready[1], output, gmid)
    if ready:
        add_heads(ready, outs)
    hops = [lambda value, bit=1 << b: swap(value, bit, nd) for b in range(nd.bit_length() - 1)]
    grad_tokens, vectors = [], None
    while sums.busy() or hops or len(grad_tokens) < micro:
        if len(grad_tokens) < micro:
            first = firsts_back[len(grad_tokens)][0]
            grad_tokens.append(lax.ppermute(first, ("dp", "mp"), back_routes(len(grad_tokens))))
            if len(grad_tokens) == micro:
                output = unpack(output)
        sums.launch()
        if len(firsts_back) < micro:
            firsts_back.append(first_part(len(firsts_back)))
        elif hops:
            vectors = jnp.concatenate([sum(part[1] for part in firsts_back), sums_two])
            vectors = jnp.take(
                vectors.reshape(4, nd, width // nd), jnp.argsort(index), axis=1
            ).reshape(4, width)
            for hop in hops:
                vectors = vectors + hop(vectors)
            hops = []
        grad_tokens, firsts_back, vectors, output, gmid = sums.land(
            grad_tokens, firsts_back, vectors, output, gmid
        )
    g_head, g_down = sums.done["head"], sums.done["down"]
    vectors = sum([ring(vectors, k, nm) for k in range(1, nm)], vectors)
    share = width // (nd * nm)
    vectors = lax.dynamic_slice_in_dim(vectors, (dp * nm + mp) * share, share, 1)
    return (
        output[:, None],
        unpack(grad_tokens)[:, None],
        jnp.concatenate([g_head[:1], g_head[2:]])[None],
        g_head[1][None],
        grads_up.astype(F32),
        g_down[None],
        jnp.stack([vectors[0], vectors[2]])[None],
        vectors[1][None],
        vectors[3][None],
    )


def solution(mesh):
    placed = (
        P(None, "dp", "mp", None),
        P(None, "dp"),
        P(),
        P(),
        P(None, None, "dp", "mp"),
        P(None, "dp", "mp"),
        P(None, "dp", "mp"),
        P(None, "dp", "mp"),
        P(None, "dp", "mp", None),
    )
    return jax.shard_map(
        functools.partial(shards, mesh.shape["dp"], mesh.shape["mp"]),
        mesh=mesh,
        in_specs=placed,
        out_specs=(
            P(None, "dp", "mp", None),
            P(None, "dp", "mp", None),
            P(None, None, "dp", "mp"),
            P(None, "dp", "mp"),
            P(None, "dp", "mp"),
            P(None, "dp", "mp"),
            P(None, None, ("dp", "mp")),
            P(None, ("dp", "mp")),
            P(None, ("dp", "mp")),
        ),
        check_vma=False,
    )
```

```python
import functools

import jax
import jax.numpy as jnp
from jax import lax
from jax.experimental import pallas as pl
from jax.experimental.pallas import tpu as pltpu
from jax.sharding import PartitionSpec as P

HDIM = 64
PAIR = 2 * HDIM
VIEW_TOK = 256
TRI = 768
EPSILON = 1e-05
MASKED = -1000000000.0
F32 = jnp.float32
BF16 = jnp.bfloat16
MIB = 1024 * 1024
ANY = pl.BlockSpec(memory_space=pl.ANY)
WHOLE = pl.BlockSpec(memory_space=pltpu.VMEM)
SHAPE = jax.ShapeDtypeStruct


def params(mib=56):
    return pltpu.CompilerParams(vmem_limit_bytes=mib * MIB)


def cost(flops, nbytes):
    return pl.CostEstimate(flops=int(flops), bytes_accessed=int(nbytes), transcendentals=0)


def dot_nt(a, b):
    return lax.dot_general(a, b, (((1,), (1,)), ((), ())), preferred_element_type=F32)


def dot_nn(a, b):
    return lax.dot_general(a, b, (((1,), (0,)), ((), ())), preferred_element_type=F32)


def dot_tn(a, b):
    return lax.dot_general(a, b, (((0,), (0,)), ((), ())), preferred_element_type=F32)


def row_block(rows):
    return 256 if rows % 256 == 0 else 128


def swap(value, bit, nd):
    return lax.ppermute(value, "dp", [(i, i ^ bit) for i in range(nd)])


def ring(value, step, nm):
    return lax.ppermute(value, "mp", [(i, (i + step) % nm) for i in range(nm)])


class Flow:
    def __init__(self, nd, nm):
        self.nd, self.nm = nd, nm
        self.bits = [1 << b for b in range(1, nd.bit_length() - 1)]
        self.queue = {bit: [] for bit in self.bits}
        self.order, self.pieces, self.flying, self.kept = {}, {}, {}, {}

    def add(self, name, value, order):
        self.order[name] = list(order)
        self.pieces[name] = [(0, value)]
        self.next(name)

    def next(self, name):
        if self.order[name]:
            self.queue[self.order[name][0]].append(name)

    def launch(self, chip=1, names=("",)):
        for bit, tasks in self.queue.items():
            for name in [name for name in tasks if name.startswith(names)][:chip]:
                tasks.remove(name)
                values = [value for _, value in self.pieces[name]]
                value = values[0][None] if len(values) == 1 else jnp.stack(values)
                self.flying["chip", name] = swap(value, bit, self.nd)

    def fly(self, name, value):
        self.flying["kept", name] = value

    def land(self, *extra):
        names, flying, kept = list(self.pieces), list(self.flying), list(self.kept)
        values = lax.optimization_barrier(
            (
                [self.pieces[name] for name in names],
                [self.flying[key] for key in flying],
                [self.kept[key] for key in kept],
                extra,
            )
        )
        for name, pieces in zip(names, values[0]):
            self.pieces[name] = [(j, v) for (j, _), (_, v) in zip(self.pieces[name], pieces)]
        self.kept = dict(zip(kept, values[2]))
        self.flying = {}
        for (kind, name), value in zip(flying, values[1]):
            if kind == "kept":
                self.kept[name] = value
                continue
            bit = self.order[name].pop(0)
            held = self.pieces[name]
            self.pieces[name] = held + [(j | bit, value[n]) for n, (j, _) in enumerate(held)]
            self.next(name)
        extra = values[3]
        return extra[0] if len(extra) == 1 else extra

    def whole(self, name):
        return name in self.pieces and not self.order[name]

    def take_half(self, name):
        pieces = dict(self.pieces.pop(name))
        return jnp.stack([pieces[2 * i] for i in range(self.nd // 2)])


def pack_kernel(index_ref, in_ref, out_ref):
    nd = index_ref.shape[0] - 1
    wide = in_ref.shape[2] // nd
    for p in range(nd):
        there = pl.ds(pl.multiple_of(index_ref[p] * wide, wide), wide)
        out_ref[:, p * wide : (p + 1) * wide] = in_ref[0, :, there]


def pack_features(value, index, which):
    micro, rows, width = value.shape
    nd = index.shape[0]
    if width // nd % 128:
        chunk = lax.dynamic_index_in_dim(value, which, 0, keepdims=False)
        return jnp.take(chunk.reshape(rows, nd, -1), index, axis=1).reshape(rows, width)
    return pl.pallas_call(
        pack_kernel,
        grid_spec=pltpu.PrefetchScalarGridSpec(
            num_scalar_prefetch=1,
            grid=(1,),
            in_specs=[pl.BlockSpec((1, rows, width), lambda i, index_ref: (index_ref[nd], 0, 0))],
            out_specs=pl.BlockSpec((rows, width), lambda i, index_ref: (0, 0)),
        ),
        out_shape=SHAPE((rows, width), value.dtype),
        compiler_params=params(),
        cost_estimate=cost(0, 6 * rows * width),
        name="pack_features",
    )(jnp.append(index, which.astype(jnp.int32)), value)


def unpack_kernel(index_ref, *refs):
    ins, out_ref = refs[:-1], refs[-1]
    nd = index_ref.shape[0] - len(ins)
    wide = out_ref.shape[2] // nd
    for k, in_ref in enumerate(ins):
        for p in range(nd):
            there = pl.ds(pl.multiple_of(index_ref[p] * wide, wide), wide)
            out_ref[index_ref[nd + k], :, there] = in_ref[:, p * wide : (p + 1) * wide]


def unpack_features(chunks, index, places):
    rows, width = chunks[0].shape
    micro, nd = len(chunks), index.shape[0]
    places = [place.astype(jnp.int32) for place in places]
    if width // nd % 128:
        back = jnp.argsort(index)
        stacked = jnp.stack(chunks).reshape(micro, rows, nd, -1)
        stacked = jnp.take(stacked, back, axis=2).reshape(micro, rows, width)
        return jnp.take(stacked, jnp.argsort(jnp.stack(places)), axis=0)
    return pl.pallas_call(
        unpack_kernel,
        in_specs=[pl.BlockSpec(memory_space=pltpu.SMEM)] + [WHOLE] * micro,
        out_specs=WHOLE,
        out_shape=SHAPE((micro, rows, width), chunks[0].dtype),
        compiler_params=params(),
        cost_estimate=cost(0, 4 * micro * rows * width),
        name="unpack_features",
    )(jnp.concatenate([index, jnp.stack(places)]), *chunks)


def standardize(state):
    centre = jnp.mean(state, axis=-1, keepdims=True)
    centred = state - centre
    spread = jnp.mean(centred * centred, axis=-1, keepdims=True)
    inverse = lax.rsqrt(spread + EPSILON)
    return centred * inverse, inverse


def norm_back(grad, state, gain):
    scaled, inverse = standardize(state)
    weighted = grad * gain
    first = jnp.mean(weighted, axis=-1, keepdims=True)
    second = jnp.mean(weighted * scaled, axis=-1, keepdims=True)
    sums = jnp.concatenate(
        [jnp.sum(grad * scaled, axis=0, keepdims=True), jnp.sum(grad, axis=0, keepdims=True)], 0
    )
    return inverse * (weighted - first - scaled * second), sums


def first_norm_kernel(micro, *refs):
    chunks = refs[:micro]
    gain_ref, bias_ref, x_ref, out_ref = refs[micro:]
    rows = chunks[0].shape[0]
    for k, ref in enumerate(chunks):
        here = slice(k * rows, (k + 1) * rows)
        x_ref[here] = ref[...]
        scaled, _ = standardize(ref[...].astype(F32))
        out_ref[here] = (scaled * gain_ref[...] + bias_ref[...]).astype(BF16)


def first_norm(chunks, gain, bias):
    rows, width = chunks[0].shape
    rows = rows * len(chunks)
    return pl.pallas_call(
        functools.partial(first_norm_kernel, len(chunks)),
        in_specs=[WHOLE] * (len(chunks) + 2),
        out_specs=[WHOLE] * 2,
        out_shape=[SHAPE((rows, width), BF16)] * 2,
        compiler_params=params(),
        cost_estimate=cost(0, 8 * rows * width),
        name="first_norm",
    )(*chunks, gain, bias)


def each_k(refs):
    return [(ref, n) for ref in refs for n in range(ref.shape[1])]


def proj_kernel(parts, in_ref, *refs):
    owns, others, out_ref = refs[:parts], refs[parts : 2 * parts], refs[-1]
    value = in_ref[...]
    half = value.shape[1] // 2
    wide = owns[0].shape[-1]
    for k, ((own, n), (other, _)) in enumerate(zip(each_k(owns), each_k(others))):
        first = own[:, n, 0].reshape(half, wide)
        second = other[:, n, 0].reshape(half, wide)
        total = dot_nn(value[:, :half], first) + dot_nn(value[:, half:], second)
        out_ref[0, :, k * wide : (k + 1) * wide] = total.astype(BF16)


def head_spec(array, count, index_map):
    chips, ks, _, deep, wide = array.shape
    return pl.BlockSpec((chips, ks, count, deep, wide), index_map)


def project(value, weights, start, count):
    rows, width = value.shape
    wide = weights[0][0].shape[-1]
    nm = sum(array.shape[1] for array in weights[0])
    arrays = [*weights[0], *weights[1]]
    return pl.pallas_call(
        functools.partial(proj_kernel, len(weights[0])),
        grid=(count,),
        in_specs=[pl.BlockSpec((rows, width), lambda i: (0, 0))]
        + [head_spec(array, 1, lambda i: (0, 0, start + i, 0, 0)) for array in arrays],
        out_specs=pl.BlockSpec((1, rows, nm * wide), lambda i: (i, 0, 0)),
        out_shape=SHAPE((count, rows, nm * wide), BF16),
        compiler_params=params(),
        cost_estimate=cost(2 * count * rows * width * nm * wide, 2 * count * rows * width),
        name="project",
    )(value, *arrays)


def attend_kernel(parts, q_ref, *refs):
    k_refs, v_refs = refs[:parts], refs[parts : 2 * parts]
    bias_ref, out_ref, lse_ref = refs[2 * parts :]
    rows = q_ref.shape[1]
    low = lax.broadcasted_iota(jnp.int32, (1, PAIR), 1) < HDIM
    query = q_ref[0] * jnp.asarray(HDIM ** (-0.5), BF16)
    mixed = None
    for head in range(2):
        mine = low if head == 0 else jnp.logical_not(low)
        q_mine = jnp.where(mine, query, jnp.zeros_like(query))
        scores = [
            jnp.where(bias_ref[p : p + 1, :] < 0.0, MASKED, dot_nt(q_mine, k_refs[p][0]))
            for p in range(parts)
        ]
        top = functools.reduce(
            jnp.maximum, [jnp.max(part, axis=1, keepdims=True) for part in scores]
        )
        total, part = 0.0, 0.0
        for p in range(parts):
            expo = jnp.exp(scores[p] - top)
            total = total + jnp.sum(expo, axis=1, keepdims=True)
            part = part + dot_nn(expo.astype(BF16), v_refs[p][0])
        part = part / total
        mixed = part if head == 0 else jnp.where(low, mixed, part)
        lse = top + jnp.log(total)
        lse_ref[0, head : head + 1, :] = jnp.transpose(jnp.broadcast_to(lse, (rows, 128)))[0:1, :]
    out_ref[...] = mixed.astype(BF16)


def attend(query, kvs, bias, start, count):
    _, rows, width = query.shape
    parts = len(kvs)
    block = row_block(rows)
    keys = rows * parts
    key_spec = pl.BlockSpec((1, rows, PAIR), lambda h, i: (0, 0, start + h))
    value_spec = pl.BlockSpec((1, rows, PAIR), lambda h, i: (1, 0, start + h))
    return pl.pallas_call(
        functools.partial(attend_kernel, parts),
        grid=(count, rows // block),
        in_specs=[pl.BlockSpec((1, block, PAIR), lambda h, i: (0, i, start + h))]
        + [key_spec] * parts
        + [value_spec] * parts
        + [pl.BlockSpec((parts, rows), lambda h, i: (0, 0))],
        out_specs=[
            pl.BlockSpec((block, PAIR), lambda h, i: (i, h)),
            pl.BlockSpec((1, 2, block), lambda h, i: (h, 0, i)),
        ],
        out_shape=[SHAPE((rows, count * PAIR), BF16), SHAPE((count, 2, rows), F32)],
        compiler_params=params(),
        cost_estimate=cost(16 * rows * keys * count * PAIR, 8 * keys * count * PAIR),
        name="attend",
    )(query, *kvs, *kvs, bias)


def attend_back_kernel(parts, q_ref, *refs):
    k_refs, v_refs = refs[:parts], refs[parts : 2 * parts]
    bias_ref, lse_ref, mixed_ref, grad_ref, dq_ref = refs[2 * parts : 2 * parts + 5]
    dkv_refs = refs[2 * parts + 5 : 3 * parts + 5]
    dk_acc, dv_acc = refs[3 * parts + 5 :]
    step = pl.program_id(1)
    low = lax.broadcasted_iota(jnp.int32, (1, PAIR), 1) < HDIM
    query = q_ref[0] * jnp.asarray(HDIM ** (-0.5), BF16)
    grad = grad_ref[0]
    product = mixed_ref[...].astype(F32) * grad.astype(F32)

    @pl.when(step == 0)
    def _():
        dk_acc[...] = jnp.zeros_like(dk_acc)
        dv_acc[...] = jnp.zeros_like(dv_acc)

    grad_query = None
    for head in range(2):
        mine = low if head == 0 else jnp.logical_not(low)
        q_mine = jnp.where(mine, query, jnp.zeros_like(query))
        g_mine = jnp.where(mine, grad, jnp.zeros_like(grad))
        delta = jnp.sum(jnp.where(mine, product, 0.0), axis=1, keepdims=True)
        delta = jnp.transpose(jnp.broadcast_to(delta, (delta.shape[0], 128)))[0:1, :]
        query_part = 0.0
        for p in range(parts):
            keys, values = k_refs[p][0], v_refs[p][0]
            scores = jnp.where(bias_ref[p] < 0.0, MASKED, dot_nt(keys, q_mine))
            probs = jnp.exp(scores - lse_ref[0, head : head + 1, :])
            upstream = dot_nt(values, g_mine)
            grad_scores = (probs * (upstream - delta)).astype(BF16)
            dv_acc[p] += dot_nn(probs.astype(BF16), g_mine)
            dk_acc[p] += dot_nn(grad_scores, q_mine)
            query_part = query_part + dot_tn(grad_scores, keys)
        grad_query = query_part if head == 0 else jnp.where(low, grad_query, query_part)
    dq_ref[...] = (grad_query * HDIM ** (-0.5)).astype(BF16)

    @pl.when(step == pl.num_programs(1) - 1)
    def _():
        for p in range(parts):
            dkv_refs[p][0] = dk_acc[p].astype(BF16)
            dkv_refs[p][1] = dv_acc[p].astype(BF16)


def attend_back(query, kvs, bias, lse, mixed, grad, start, count):
    _, rows, width = query.shape
    parts = len(kvs)
    block = row_block(rows)
    keys = rows * parts
    key_spec = pl.BlockSpec((1, rows, PAIR), lambda h, i: (0, 0, start + h))
    value_spec = pl.BlockSpec((1, rows, PAIR), lambda h, i: (1, 0, start + h))
    return pl.pallas_call(
        functools.partial(attend_back_kernel, parts),
        grid=(count, rows // block),
        in_specs=[pl.BlockSpec((1, block, PAIR), lambda h, i: (0, i, start + h))]
        + [key_spec] * parts
        + [value_spec] * parts
        + [
            pl.BlockSpec((parts, rows, 1), lambda h, i: (0, 0, 0)),
            pl.BlockSpec((1, 2, block), lambda h, i: (h, 0, i)),
            pl.BlockSpec((block, PAIR), lambda h, i: (i, h)),
            pl.BlockSpec((1, block, PAIR), lambda h, i: (0, i, start + h)),
        ],
        out_specs=[pl.BlockSpec((block, PAIR), lambda h, i: (i, h))]
        + [pl.BlockSpec((2, rows, PAIR), lambda h, i: (0, 0, h))] * parts,
        out_shape=[SHAPE((rows, count * PAIR), BF16)]
        + [SHAPE((2, rows, count * PAIR), BF16)] * parts,
        scratch_shapes=[pltpu.VMEM((parts, rows, PAIR), F32)] * 2,
        compiler_params=params(),
        cost_estimate=cost(40 * rows * keys * count * PAIR, 16 * keys * count * PAIR),
        name="attend_back",
    )(query, *kvs, *kvs, bias, lse, mixed, grad)


def middle_kernel(nm, parts, x_ref, *refs):
    mixed_refs, refs = refs[:nm], refs[nm:]
    weights = refs[:parts], refs[parts : 2 * parts]
    gain_ref, bias_ref, mid_ref, out_ref = refs[2 * parts :]
    half = x_ref.shape[1] // 2
    sides = []
    for side in weights:
        total = 0.0
        for k, (ref, n) in enumerate(each_k(side)):
            total = total + dot_nt(mixed_refs[k][...], ref[:, n, 0].reshape(half, -1))
        sides.append(total)
    middle = x_ref[...].astype(F32) + jnp.concatenate(sides, axis=1)
    mid_ref[...] = middle
    scaled, _ = standardize(middle)
    out_ref[...] = (scaled * gain_ref[...] + bias_ref[...]).astype(BF16)


def middle_norm(x, mixed, weights, which, gain, bias):
    rows, width = x.shape
    nm, wide = len(mixed), mixed[0].shape[1]
    block = row_block(rows)
    vector = pl.BlockSpec((1, width), lambda i: (0, 0))
    line = pl.BlockSpec((block, width), lambda i: (i, 0))
    arrays = [*weights[0], *weights[1]]
    return pl.pallas_call(
        functools.partial(middle_kernel, nm, len(weights[0])),
        grid=(rows // block,),
        in_specs=[line]
        + [pl.BlockSpec((block, wide), lambda i: (i, 0))] * nm
        + [head_spec(array, 1, lambda i: (0, 0, which, 0, 0)) for array in arrays]
        + [vector, vector],
        out_specs=[line, line],
        out_shape=[SHAPE((rows, width), F32), SHAPE((rows, width), BF16)],
        compiler_params=params(),
        cost_estimate=cost(2 * rows * width * nm * wide, 14 * x.size),
        name="middle_norm",
    )(x, *mixed, *arrays, gain, bias)


def load_weights(firsts, sizes, index_ref, refs, held, sems):
    step = pl.program_id(0)
    nm = firsts + sum(sizes)
    chips = held.shape[2]
    copies, refs = {k: [] for k in range(nm)}, list(refs)

    def add(k, source, w, side, n, sem):
        copies[k].append(
            pltpu.make_async_copy(source, held.at[w, 2 * k + side, n], sems.at[w, 2 * k + side, sem])
        )

    ref = refs.pop(0)
    for k in range(firsts):
        for w in range(2):
            for side in range(2):
                for n in range(chips):
                    add(k, ref.at[index_ref[side * chips + n], k, w], w, side, n, n)
    k = firsts
    for size in sizes:
        sides = [refs.pop(0) for _ in range(4)]
        for i in range(size):
            for n, ref in enumerate(sides):
                add(k, ref.at[:, i], n // 2, n % 2, slice(None), 0)
            k += 1

    @pl.when(step == 0)
    def _():
        for k in range(nm):
            for copy in copies[k]:
                copy.start()

    for k in range(nm):

        @pl.when(step == k)
        def _():
            for copy in copies[k]:
                copy.wait()


def feed_kernel(firsts, sizes, index_ref, *refs):
    nm, count = firsts + sum(sizes), 1 + 4 * len(sizes)
    in_ref, mid_ref, out_ref, act_ref, slope_ref, held, acc, sems = refs[count:]
    step = pl.program_id(0)
    load_weights(firsts, sizes, index_ref, refs[:count], held, sems)
    half = in_ref.shape[1] // 2
    up = [held[0, 2 * step + side].reshape(half, -1) for side in range(2)]
    down = [held[1, 2 * step + side].reshape(half, -1) for side in range(2)]

    @pl.when(step == 0)
    def _():
        acc[...] = mid_ref[...]

    hidden = dot_nn(in_ref[:, :half], up[0]) + dot_nn(in_ref[:, half:], up[1])
    below = 0.5 + 0.5 * lax.erf(hidden * (0.5**0.5))
    density = jnp.exp(-0.5 * hidden * hidden) * 0.3989422804014327
    active = (hidden * below).astype(BF16)
    act_ref[0] = active
    slope_ref[0] = (below + hidden * density).astype(BF16)
    acc[:, :half] += dot_nt(active, down[0])
    acc[:, half:] += dot_nt(active, down[1])

    @pl.when(step == nm - 1)
    def _():
        out_ref[...] = acc[...].astype(BF16)


def feed(normed, middle, index, firsts, sizes, weights):
    rows, width = normed.shape
    nm = firsts + sum(sizes)
    nd, (deep, hidden) = index.shape[0], weights[0].shape[3:]
    chips = nd // 2
    line = pl.BlockSpec((rows, width), lambda k: (0, 0))
    wide = pl.BlockSpec((1, rows, hidden), lambda k: (k, 0, 0))
    return pl.pallas_call(
        functools.partial(feed_kernel, firsts, sizes),
        grid=(nm,),
        in_specs=[pl.BlockSpec(memory_space=pltpu.SMEM)]
        + [ANY] * len(weights)
        + [line, line],
        out_specs=[line, wide, wide],
        out_shape=[SHAPE((rows, width), BF16)] + [SHAPE((nm, rows, hidden), BF16)] * 2,
        scratch_shapes=[
            pltpu.VMEM((2, 2 * nm, chips, deep, hidden), BF16),
            pltpu.VMEM((rows, width), F32),
            pltpu.SemaphoreType.DMA((2, 2 * nm, chips)),
        ],
        compiler_params=params(60),
        cost_estimate=cost(4 * rows * width * nm * hidden, 4 * nm * width * hidden),
        name="feed",
    )(index, *weights, normed, middle)


def feed_back_kernel(firsts, sizes, index_ref, *refs):
    nm, count = firsts + sum(sizes), 1 + 4 * len(sizes)
    g_ref, slope_ref, mid_ref, gain_ref = refs[count : count + 4]
    hid_ref, attn_ref, sums_ref, held, acc, sems = refs[count + 4 :]
    step = pl.program_id(0)
    load_weights(firsts, sizes, index_ref, refs[:count], held, sems)
    half = g_ref.shape[1] // 2
    up = [held[0, 2 * step + side].reshape(half, -1) for side in range(2)]
    down = [held[1, 2 * step + side].reshape(half, -1) for side in range(2)]
    active = dot_nn(g_ref[:, :half], down[0]) + dot_nn(g_ref[:, half:], down[1])
    hidden = (active * slope_ref[0].astype(F32)).astype(BF16)
    hid_ref[0] = hidden
    first, second = dot_nt(hidden, up[0]), dot_nt(hidden, up[1])

    @pl.when(step == 0)
    def _():
        acc[:, :half] = first
        acc[:, half:] = second

    @pl.when(step > 0)
    def _():
        acc[:, :half] += first
        acc[:, half:] += second

    @pl.when(step == nm - 1)
    def _():
        into, sums = norm_back(acc[...], mid_ref[...], gain_ref[...])
        attn_ref[...] = (g_ref[...].astype(F32) + into).astype(BF16)
        sums_ref[...] = sums


def feed_back(grad, slope, middle, gain, index, firsts, sizes, weights):
    rows, width = grad.shape
    nm = firsts + sum(sizes)
    nd, (deep, hidden) = index.shape[0], weights[0].shape[3:]
    chips = nd // 2
    line = pl.BlockSpec((rows, width), lambda k: (0, 0))
    wide = pl.BlockSpec((1, rows, hidden), lambda k: (k, 0, 0))
    return pl.pallas_call(
        functools.partial(feed_back_kernel, firsts, sizes),
        grid=(nm,),
        in_specs=[pl.BlockSpec(memory_space=pltpu.SMEM)]
        + [ANY] * len(weights)
        + [line, wide, line, pl.BlockSpec((1, width), lambda k: (0, 0))],
        out_specs=[
            wide,
            line,
            pl.BlockSpec((2, width), lambda k: (0, 0)),
        ],
        out_shape=[
            SHAPE((nm, rows, hidden), BF16),
            SHAPE((rows, width), BF16),
            SHAPE((2, width), F32),
        ],
        scratch_shapes=[
            pltpu.VMEM((2, 2 * nm, chips, deep, hidden), BF16),
            pltpu.VMEM((rows, width), F32),
            pltpu.SemaphoreType.DMA((2, 2 * nm, chips)),
        ],
        compiler_params=params(60),
        cost_estimate=cost(4 * rows * width * nm * hidden, 4 * nm * width * hidden),
        name="feed_back",
    )(index, *weights, grad, slope, middle, gain)


def wide_grad_kernel(place_ref, a_ref, b_ref, out_ref):
    part = dot_tn(a_ref[...], b_ref[0]).astype(BF16)
    nd, deep = out_ref.shape[0], out_ref.shape[2]
    for p in range(nd):
        out_ref[place_ref[p], 0] = part[p * deep : (p + 1) * deep]


def wide_grad(rows_in, values, place, absolute):
    rows, width = rows_in.shape
    nm, _, hidden = values.shape
    nd = place.shape[0] - 1
    block = min(512, hidden)

    def out_map(k, i, place_ref):
        return (0, lax.rem(place_ref[nd] + nm - k, nm) if absolute else k, 0, i)

    return pl.pallas_call(
        wide_grad_kernel,
        grid_spec=pltpu.PrefetchScalarGridSpec(
            num_scalar_prefetch=1,
            grid=(nm, hidden // block),
            in_specs=[
                pl.BlockSpec((rows, width), lambda k, i, place_ref: (0, 0)),
                pl.BlockSpec((1, rows, block), lambda k, i, place_ref: (k, 0, i)),
            ],
            out_specs=pl.BlockSpec((nd, 1, width // nd, block), out_map),
        ),
        out_shape=SHAPE((nd, nm, width // nd, hidden), BF16),
        compiler_params=params(),
        cost_estimate=cost(2 * nm * width * rows * hidden, 4 * nm * width * hidden),
        name="wide_grad",
    )(place, rows_in, values)


def head_grad_kernel(
    n_ref, g_ref, mixed_ref, dq_ref, dkv_ref, came_ref, sum_ref, keep_ref, give_ref
):
    chips, _, deep, wide = keep_ref.shape
    half = chips * deep
    total = (dkv_ref[...].astype(F32) + came_ref[...].astype(F32)).astype(BF16)
    sum_ref[...] = total
    three = dot_tn(n_ref[...], jnp.concatenate([dq_ref[...], total[0], total[1]], axis=1))
    one = dot_tn(g_ref[...], mixed_ref[...])
    parts = (three[:, :wide], one, three[:, wide : 2 * wide], three[:, 2 * wide :])
    for i, part in enumerate(parts):
        part = part.astype(BF16)
        keep_ref[:, i] = part[:half].reshape(chips, deep, wide)
        give_ref[:, i] = part[half:].reshape(chips, deep, wide)


def head_grad(normed, attn, mixed, dq, dkv, came, chips):
    rows, width = normed.shape
    wide = dq.shape[1]
    piece = SHAPE((chips, 4, width // 2 // chips, wide), BF16)
    total, keep, give = pl.pallas_call(
        head_grad_kernel,
        in_specs=[WHOLE] * 6,
        out_specs=[WHOLE] * 3,
        out_shape=[SHAPE(dkv.shape, BF16), piece, piece],
        compiler_params=params(),
        cost_estimate=cost(8 * width * rows * wide, 8 * width * wide),
        name="head_grad",
    )(normed, attn, mixed, dq, dkv, came)
    return total, keep[None], give[None]


def first_back_kernel(nm, parts, x_ref, attn_ref, gain_ref, *refs):
    dqs, dkvs, came_ref, refs = refs[:nm], refs[nm : 2 * nm], refs[2 * nm], refs[2 * nm + 1 :]
    qo = refs[:parts], refs[parts : 2 * parts]
    kv = refs[2 * parts : 3 * parts], refs[3 * parts : 4 * parts]
    out_ref, sums_ref = refs[4 * parts :]
    last = (dkvs[0][...].astype(F32) + came_ref[...].astype(F32)).astype(BF16)
    half = x_ref.shape[1] // 2
    sides = []
    for side in range(2):
        total = 0.0
        for k, ((qo_ref, n), (kv_ref, _)) in enumerate(zip(each_k(qo[side]), each_k(kv[side]))):
            total = total + dot_nt(dqs[k][...], qo_ref[:, n, 0].reshape(half, -1))
            for i in range(2):
                dkv = dkvs[k][i] if k else last[i]
                total = total + dot_nt(dkv, kv_ref[:, n, i].reshape(half, -1))
        sides.append(total)
    into, sums = norm_back(jnp.concatenate(sides, axis=1), x_ref[...].astype(F32), gain_ref[...])
    out_ref[...] = (attn_ref[...].astype(F32) + into).astype(BF16)
    sums_ref[...] = sums


def first_back(x, attn, gain, dqs, dkvs, came, qo, kv, part, block):
    width = x.shape[1]
    nm, wide = len(dqs), dqs[0].shape[1]
    line = pl.BlockSpec((block, width), lambda i: (part, 0))
    still = lambda i: (0, 0, 0, 0, 0)
    qo_arrays, kv_arrays = [*qo[0], *qo[1]], [*kv[0], *kv[1]]
    return pl.pallas_call(
        functools.partial(first_back_kernel, nm, len(qo[0])),
        grid=(1,),
        in_specs=[line, line, pl.BlockSpec((1, width), lambda i: (0, 0))]
        + [pl.BlockSpec((block, wide), lambda i: (part, 0))] * nm
        + [pl.BlockSpec((2, block, wide), lambda i: (0, part, 0))] * (nm + 1)
        + [head_spec(array, 1, still) for array in qo_arrays]
        + [head_spec(array, 2, still) for array in kv_arrays],
        out_specs=[
            pl.BlockSpec((block, width), lambda i: (0, 0)),
            pl.BlockSpec((2, width), lambda i: (0, 0)),
        ],
        out_shape=[SHAPE((block, width), BF16), SHAPE((2, width), F32)],
        compiler_params=params(),
        cost_estimate=cost(6 * block * width * nm * wide, 12 * block * width),
        name="first_back",
    )(x, attn, gain, *dqs, *dkvs, came, *qo_arrays, *kv_arrays)


def add_low(a, b):
    return (a.astype(F32) + b.astype(F32)).astype(BF16)


def add_parts_kernel(pairs, *refs):
    outs, row = refs[2 * pairs :], 0
    for i in range(pairs):
        keep_ref, came_ref = refs[2 * i : 2 * i + 2]
        size = keep_ref.shape[0]
        for n, out in enumerate(outs):
            out[row : row + size] = add_low(keep_ref[:, n + 1], came_ref[:, n + 1])
        row += size


def add_parts(pairs):
    keep = pairs[0][0]
    rows = sum(pair[0].shape[0] for pair in pairs)
    piece = SHAPE((rows,) + keep.shape[2:], keep.dtype)
    return pl.pallas_call(
        functools.partial(add_parts_kernel, len(pairs)),
        in_specs=[WHOLE] * (2 * len(pairs)),
        out_specs=[WHOLE] * (keep.shape[1] - 1),
        out_shape=[piece] * (keep.shape[1] - 1),
        compiler_params=params(),
        cost_estimate=cost(0, 6 * len(pairs) * keep.size),
        name="add_parts",
    )(*[array for pair in pairs for array in pair])


class Scatter:
    def __init__(self, nd, nm, bits):
        self.nd, self.nm = nd, nm
        self.queue = {1: [], **{bit: [] for bit in bits}, "direct": [], "z": []}
        self.order, self.kept, self.waits, self.flying = {}, {}, {}, {}
        self.ends, self.came, self.done, self.rings, self.joined = {}, {}, {}, {}, {}

    def add(self, name, ks, keep, give, order, rings=True):
        self.order[name, tuple(ks)], self.rings[name] = order, rings
        self.push(1, (name, tuple(ks), -1), list(range(0, self.nd, 2)), keep, give)

    def add_line(self, name, value, rings):
        self.rings[name] = rings
        if rings:
            for k in range(self.nm):
                self.ends[name, k] = (value[k],)
            self.advance(name, self.nm - 1)
            return
        self.ends[name] = [value[0]]
        for k in sorted(range(1, self.nm), key=lambda k: min(k, self.nm - k)):
            self.waits[name, k, "z"] = value[k]
            self.queue["z"].append((name, k, "z"))

    def push(self, link, key, places, keep, give):
        self.kept[key], self.waits[key] = (places, keep), give
        self.queue[link].append(key)

    def launch(self, core=1, chip=1, direct=1, z=1):
        for link, tasks in self.queue.items():
            for _ in range({1: core, "direct": direct, "z": z}.get(link, chip)):
                if not tasks:
                    break
                key = tasks.pop(0)
                value = self.waits.pop(key)
                if link == "z" and not self.rings[key[0]]:
                    value = ring(value, -key[1], self.nm)
                elif link == "z":
                    value = ring(value, -1, self.nm)
                elif link == "direct":
                    more = [tasks.pop(0) for _ in range(min(direct - 1, len(tasks)))]
                    self.joined[key] = more
                    value = add_parts([value] + [self.waits.pop(other) for other in more])
                    value = [swap(part, 2 * n + 2, self.nd) for n, part in enumerate(value)]
                    self.flying[key] = value
                    break
                else:
                    value = swap(value, link, self.nd)
                self.flying[key] = value

    def busy(self):
        return bool(self.flying) or any(self.queue.values())

    def land(self, *extra):
        waits, flying = list(self.waits), list(self.flying)
        values = lax.optimization_barrier(
            ([self.waits[key] for key in waits], [self.flying[key] for key in flying], extra)
        )
        self.waits = dict(zip(waits, values[0]))
        came = dict(zip(flying, values[1]))
        self.flying = {}
        for key, value in came.items():
            if key not in self.joined:
                self.arrive(key, value)
                continue
            for other in [key] + self.joined.pop(key):
                self.arrive(other, [part[: len(other[1])] for part in value])
                value = [part[len(other[1]) :] for part in value]
        extra = values[2]
        return extra[0] if len(extra) == 1 else extra

    def arrive(self, key, value):
        name, ks, stage = key
        if stage == "z" and not self.rings[name]:
            self.ends[name].append(value)
            if len(self.ends[name]) == self.nm:
                self.done[name] = sum(part.astype(F32) for part in self.ends.pop(name))
            return
        if stage == "z":
            self.came[name, ks - 1] = value
            self.advance(name, ks - 1)
            return
        order = self.order[name, ks]
        places, keep = self.kept.pop(key)
        if order is None and stage == -1:
            own = (keep[:, 0], value[:, 0])
            self.push("direct", (name, ks, 0), own, None, (keep, value))
            return
        if order is None:
            for n, k in enumerate(ks):
                self.ends[name, k] = tuple(part[n] for part in [*places, *value])
                self.advance(name, k)
            return
        if stage + 1 == len(order):
            for n, k in enumerate(ks):
                self.ends[name, k] = (keep[n, 0], value[n, 0])
            for k in reversed(ks):
                self.advance(name, k)
            return
        bit = order[stage + 1]
        stays = [n for n, j in enumerate(places) if not j & bit]
        goes = [n for n, j in enumerate(places) if j & bit]

        def take(array, which):
            return jnp.stack([array[:, n] for n in which], axis=1)

        self.push(
            bit,
            (name, ks, stage + 1),
            [places[n] for n in stays],
            add_low(take(keep, stays), take(value, stays)),
            add_low(take(keep, goes), take(value, goes)),
        )

    def advance(self, name, k):
        if (name, k) not in self.ends or (k < self.nm - 1 and (name, k) not in self.came):
            return
        total = sum(part.astype(F32) for part in self.ends.pop((name, k)))
        if k < self.nm - 1:
            total = total + self.came.pop((name, k)).astype(F32)
        if k:
            key = (name, k, "z")
            self.waits[key] = total.astype(BF16)
            self.queue["z"].append(key)
        else:
            self.done[name] = total


def shards(nd, nm, tokens, views, norm_gains, norm_biases, w_proj, w_out, w_up, w_down, cotangent):
    micro, _, chunk, width = tokens.shape
    ranks = nm // micro
    half = max(ranks // 2, 1)
    rows = micro * chunk
    chips = nd // 2
    wide = w_out.shape[2]
    per_k = wide // PAIR
    hidden = w_up.shape[2]
    dp, mp = lax.axis_index("dp"), lax.axis_index("mp")
    group = mp // half
    step_here = group // 2
    rank = (dp & 1) + 2 * (mp % half)
    order_of = [2 * (p % chips) + p // chips for p in range(nd)]
    offsets = jnp.asarray(order_of, jnp.int32)
    index = dp.astype(jnp.int32) ^ offsets

    def routes(k):
        pairs = []
        for d in range(nd):
            for z in range(nm):
                m = (k + z) % micro
                r = z // micro
                to_d = (d & ~1) | (r & 1)
                to_z = (2 * m + (d & 1)) * half + r // 2
                pairs.append((d * nm + z, to_d * nm + to_z))
        return pairs

    there = ((dp & ~1) | ((mp // micro) & 1)).astype(jnp.int32) ^ offsets

    def pack(value, k):
        return pack_features(value, there, (k + mp) % micro)

    def send(packed, k):
        return lax.ppermute(packed[k], ("dp", "mp"), routes(k))

    def back_routes(k):
        return [(b, a) for a, b in routes(k)]

    def send_chunk(chunks, k):
        return lax.ppermute(chunks[k], ("dp", "mp"), back_routes(k))

    def unpack(came):
        return unpack_features(came, there, [(k + mp) % micro for k in range(micro)])

    def by_place(vector):
        return jnp.take(vector.reshape(-1, nd, width // nd), index, axis=1).reshape(-1, width)

    flow = Flow(nd, nm)
    forth, back = flow.bits, flow.bits[::-1]
    firsts = min(2, nm)
    groups = [list(range(k, min(k + 2, nm))) for k in range(firsts, nm, 2)]
    sizes = tuple(len(group) for group in groups)
    head = [jnp.concatenate([w_proj[0], w_out])]
    feeds = [jnp.concatenate([w_up, w_down])]
    gather = functools.partial(lax.all_gather, axis_name="dp")
    head_groups = [[0], list(range(1, nm))]

    def headed(n):
        flow.add(f"qo{n}", jnp.stack([head[k][::3] for k in head_groups[n]]), forth)
        flow.add(f"kv{n}", jnp.stack([head[k][1:3] for k in head_groups[n]]), back)

    halves = {}

    def core_halves(most, names):
        for name in names:
            if most and flow.whole(name):
                halves[name] = flow.take_half(name)
                flow.fly(name, swap(halves[name], 1, nd))
                most -= 1

    for k in sorted(range(1, nm), key=lambda k: -min(k, nm - k)):
        flow.fly(("head", k), ring(head[0], k, nm))
    headed(0)
    flow.launch()
    token_parts = [pack(tokens[:, 0], k) for k in range(micro)]
    view = lax.dynamic_index_in_dim(views[:, 0], mp % micro, 0, keepdims=True)
    head, tokens, token_parts, cotangent, there, view, feeds, norm_gains, norm_biases = flow.land(
        head, tokens, token_parts, cotangent, there, view, feeds, norm_gains, norm_biases
    )
    head += [flow.kept.pop(("head", k)) for k in range(1, nm)]
    headed(1)
    weights = []
    came = []
    head_names = [f"{name}{n}" for n in range(len(head_groups)) for name in ("kv", "qo")]
    while len(came) < micro or not all(n in halves or flow.whole(n) for n in head_names):
        if len(came) < micro:
            came.append(send(token_parts, len(came)))
        flow.launch(chip=2)
        if len(came) == micro:
            core_halves(2, head_names)
        if len(came) == 1:
            grad_parts = [pack(cotangent[:, 0], k) for k in range(micro)]
            gains, biases = by_place(norm_gains[0]), by_place(norm_biases[0])
        came, token_parts, grad_parts, feeds, halves, gains, biases, view = flow.land(
            came, token_parts, grad_parts, feeds, halves, gains, biases, view
        )

    def turn():
        if len(feeds) < nm:
            feeds.append(ring(feeds[-1], 1, nm))

    def turned():
        if not weights and len(feeds) >= firsts:
            weights.append(gather(jnp.stack(feeds[:firsts])))
        for n, group in enumerate(groups):
            if f"up{n}" not in flow.order and group[-1] < len(feeds):
                flow.add(f"up{n}", jnp.stack([feeds[k][0] for k in group]), forth)
                flow.add(f"down{n}", jnp.stack([feeds[k][1] for k in group]), back)

    last = [f"{name}{n}" for n in range(len(groups)) for name in ("up", "down")]
    core_halves(len(head_names), head_names)
    turn()
    x, normed = first_norm(came, gains[:1], biases[:1])
    x, normed, halves, feeds, view = flow.land(x, normed, halves, feeds, view)
    turned()

    def both(name):
        names = [f"{name}{n}" for n in range(len(head_groups))]
        return [halves.pop(n) for n in names], [flow.kept.pop(n) for n in names]

    qo, kv = both("qo"), both("kv")

    turn()
    flow.launch()
    views = lax.ppermute(view, ("dp", "mp"), routes(0))
    own_kv = project(normed, kv, 0, 2)
    own_kv, normed, qo, feeds, views = flow.land(own_kv, normed, qo, feeds, views)
    turned()

    def swap_rank(value, bit):
        if bit == 1:
            return swap(value, 1, nd)
        return lax.ppermute(value, "mp", [(i, i ^ (bit >> 1)) for i in range(nm)])

    rank_bits = [1 << b for b in range(ranks.bit_length() - 1)]
    kvs = {0: own_kv}
    for bit in rank_bits:
        for j in list(kvs):
            kvs[j | bit] = swap_rank(kvs[j], bit)
    kvs = [kvs[j] for j in range(ranks)]
    turn()
    flow.launch()
    query = project(normed, qo, 0, 1)
    slot = jnp.stack([(step_here - t) % micro for t in range(micro)])
    within = (slot[:, None] * chunk + jnp.arange(chunk)[None]).reshape(-1)
    position = jnp.stack([(rank ^ j) * rows + within for j in range(ranks)])
    bias = jnp.where(position < TRI + views[0] * VIEW_TOK, 0.0, -1.0).astype(F32)
    kvs, query, bias, grad_parts, feeds = flow.land(kvs, query, bias, grad_parts, feeds)
    turned()

    grad_came, mixed, lses = [], [], []
    at_once = max(nm // 2, 1)
    while len(mixed) < nm or len(grad_came) < micro or not all(
        name in halves or flow.whole(name) for name in last
    ):
        turn()
        flow.launch()
        if len(grad_came) < micro:
            grad_came.append(send(grad_parts, len(grad_came)))
        core_halves(2, last)
        for k in range(len(mixed), min(len(mixed) + at_once, nm)):
            part, lse = attend(query, kvs, bias, k * per_k, per_k)
            mixed.append(part)
            lses.append(lse)
        mixed, query, halves, grad_parts, grad_came, feeds = flow.land(
            mixed, query, halves, grad_parts, grad_came, feeds
        )
        turned()
    core_halves(len(last), last)
    middle, normed_two = middle_norm(x, mixed, qo, 1, gains[1:], biases[1:])
    grad = jnp.concatenate(grad_came)
    middle, normed_two, halves, grad = flow.land(middle, normed_two, halves, grad)
    for name in last:
        weights += [halves[name], flow.kept.pop(name)]

    result, active, slope = feed(normed_two, middle, index, firsts, sizes, weights)
    out_chunks = result.reshape((micro, chunk, width))
    output = []

    sums = Scatter(nd, nm, flow.bits)
    output = [send_chunk(out_chunks, 0)]
    over_dp = functools.partial(lax.psum_scatter, axis_name="dp", scatter_dimension=0, tiled=True)
    place = jnp.append(index, mp.astype(jnp.int32))
    grads_down = over_dp(wide_grad(grad, active, place, False))
    hid, attn, sums_two = feed_back(
        grad, slope, middle, gains[1:], index, firsts, sizes, weights
    )
    hid, attn, sums_two, normed_two, output, out_chunks = sums.land(
        hid, attn, sums_two, normed_two, output, out_chunks
    )
    grads_up = over_dp(wide_grad(normed_two, hid, place, True))[0]
    grads_up = lax.psum_scatter(grads_up, "mp", scatter_dimension=0, tiled=True)
    grad_mixed = project(attn, qo, 1, 1)

    dqs, dkvs = {}, {}
    bias_tall = bias[:, :, None]
    closing = list(range(nm))
    dkv_part, dkv_came = {}, {}

    def head_grads():
        if not closing or closing[-1] not in dkv_came:
            return None
        k = closing.pop()
        dkvs[k], keep, give = head_grad(
            normed, attn, mixed[k], dqs[k], dkv_part[k], dkv_came[k], chips
        )
        return k, (keep, give)

    def add_heads(ready, outs):
        sums.add("head", [ready[0]], outs[0], outs[1], None)

    def exchange(parts):
        parts = dict(enumerate(parts))
        came = None
        for bit in rank_bits[::-1]:
            if came is not None:
                parts = {j: add_low(part, came[j]) for j, part in parts.items()}
            came = {j ^ bit: swap_rank(parts.pop(j), bit) for j in list(parts) if j & bit}
        return parts[0], came[0]

    parts = None
    for k in list(reversed(range(nm))) + [-1]:
        if k == 0:
            sums.add_line("down", grads_down[0], rings=False)
        sums.launch(direct=1 if k < 0 else 0, z=nm - 1)
        while k >= 0 and len(output) < min(micro, nm - k + 1):
            output.append(send_chunk(out_chunks, len(output)))
        ready = head_grads()
        if parts is not None:
            dkv_part[k + 1], dkv_came[k + 1] = exchange(parts)
            parts = None
        if k >= 0:
            dqs[k], *parts = attend_back(
                query, kvs, bias_tall, lses[k], mixed[k], grad_mixed, k * per_k, per_k
            )
        live = (ready and ready[1], dqs, parts, query, dkv_part, dkv_came, dkvs, attn)
        live = sums.land(*live, output)
        outs, dqs, parts, query, dkv_part, dkv_came, dkvs, attn, output = live
        if ready:
            add_heads(ready, outs)

    sums.launch()
    ready = head_grads()

    def first_part(part):
        return first_back(
            x,
            attn,
            gains[:1],
            [dqs[k] for k in range(nm)],
            [dkvs[k] if k else dkv_part[k] for k in range(nm)],
            dkv_came[0],
            qo,
            kv,
            part,
            chunk,
        )

    firsts_back = [first_part(0)]
    firsts_back, outs, output, attn = sums.land(firsts_back, ready and ready[1], output, attn)
    if ready:
        add_heads(ready, outs)
    hops = [lambda value, bit=1 << b: swap(value, bit, nd) for b in range(nd.bit_length() - 1)]
    grad_tokens, vectors = [], None
    while sums.busy() or hops or len(grad_tokens) < micro:
        if len(grad_tokens) < micro:
            first = firsts_back[len(grad_tokens)][0]
            grad_tokens.append(lax.ppermute(first, ("dp", "mp"), back_routes(len(grad_tokens))))
            if len(grad_tokens) == micro:
                output = unpack(output)
        sums.launch()
        if len(firsts_back) < micro:
            firsts_back.append(first_part(len(firsts_back)))
        elif hops:
            vectors = jnp.concatenate([sum(part[1] for part in firsts_back), sums_two])
            vectors = jnp.take(
                vectors.reshape(4, nd, width // nd), jnp.argsort(index), axis=1
            ).reshape(4, width)
            for hop in hops:
                vectors = vectors + hop(vectors)
            hops = []
        grad_tokens, firsts_back, vectors, output, attn = sums.land(
            grad_tokens, firsts_back, vectors, output, attn
        )
    g_head, g_down = sums.done["head"], sums.done["down"]
    vectors = sum([ring(vectors, k, nm) for k in range(1, nm)], vectors)
    share = width // (nd * nm)
    vectors = lax.dynamic_slice_in_dim(vectors, (dp * nm + mp) * share, share, 1)
    return (
        output[:, None],
        unpack(grad_tokens)[:, None],
        jnp.concatenate([g_head[:1], g_head[2:]])[None],
        g_head[1][None],
        grads_up.astype(F32),
        g_down[None],
        jnp.stack([vectors[0], vectors[2]])[None],
        vectors[1][None],
        vectors[3][None],
    )


def solution(mesh):
    placed = (
        P(None, "dp", "mp", None),
        P(None, "dp"),
        P(),
        P(),
        P(None, None, "dp", "mp"),
        P(None, "dp", "mp"),
        P(None, "dp", "mp"),
        P(None, "dp", "mp"),
        P(None, "dp", "mp", None),
    )
    return jax.shard_map(
        functools.partial(shards, mesh.shape["dp"], mesh.shape["mp"]),
        mesh=mesh,
        in_specs=placed,
        out_specs=(
            P(None, "dp", "mp", None),
            P(None, "dp", "mp", None),
            P(None, None, "dp", "mp"),
            P(None, "dp", "mp"),
            P(None, "dp", "mp"),
            P(None, "dp", "mp"),
            P(None, None, ("dp", "mp")),
            P(None, ("dp", "mp")),
            P(None, ("dp", "mp")),
        ),
        check_vma=False,
    )
```

```python
import functools

import jax
import jax.numpy as jnp
from jax import lax
from jax.experimental import pallas as pl
from jax.experimental.pallas import tpu as pltpu
from jax.sharding import PartitionSpec as P

HDIM = 64
PAIR = 2 * HDIM
VIEW_TOK = 256
TRI = 768
EPSILON = 1e-05
MASKED = -1000000000.0
F32 = jnp.float32
BF16 = jnp.bfloat16
MIB = 1024 * 1024
ANY = pl.BlockSpec(memory_space=pl.ANY)
WHOLE = pl.BlockSpec(memory_space=pltpu.VMEM)
SHAPE = jax.ShapeDtypeStruct


def params(mib=56):
    return pltpu.CompilerParams(vmem_limit_bytes=mib * MIB)


def cost(flops, nbytes):
    return pl.CostEstimate(flops=int(flops), bytes_accessed=int(nbytes), transcendentals=0)


def dot_nt(a, b):
    return lax.dot_general(a, b, (((1,), (1,)), ((), ())), preferred_element_type=F32)


def dot_nn(a, b):
    return lax.dot_general(a, b, (((1,), (0,)), ((), ())), preferred_element_type=F32)


def dot_tn(a, b):
    return lax.dot_general(a, b, (((0,), (0,)), ((), ())), preferred_element_type=F32)


def row_block(rows):
    return 256 if rows % 256 == 0 else 128


def swap(value, bit, nd):
    return lax.ppermute(value, "dp", [(i, i ^ bit) for i in range(nd)])


def ring(value, step, nm):
    return lax.ppermute(value, "mp", [(i, (i + step) % nm) for i in range(nm)])


class Flow:
    def __init__(self, nd, nm):
        self.nd, self.nm = nd, nm
        self.bits = [1 << b for b in range(1, nd.bit_length() - 1)]
        self.queue = {bit: [] for bit in self.bits}
        self.order, self.pieces, self.flying, self.kept = {}, {}, {}, {}

    def add(self, name, value, order):
        self.order[name] = list(order)
        self.pieces[name] = [(0, value)]
        self.next(name)

    def next(self, name):
        if self.order[name]:
            self.queue[self.order[name][0]].append(name)

    def launch(self, chip=1, names=("",)):
        for bit, tasks in self.queue.items():
            for name in [name for name in tasks if name.startswith(names)][:chip]:
                tasks.remove(name)
                values = [value for _, value in self.pieces[name]]
                value = values[0][None] if len(values) == 1 else jnp.stack(values)
                self.flying["chip", name] = swap(value, bit, self.nd)

    def fly(self, name, value):
        self.flying["kept", name] = value

    def land(self, *extra):
        names, flying, kept = list(self.pieces), list(self.flying), list(self.kept)
        values = lax.optimization_barrier(
            (
                [self.pieces[name] for name in names],
                [self.flying[key] for key in flying],
                [self.kept[key] for key in kept],
                extra,
            )
        )
        for name, pieces in zip(names, values[0]):
            self.pieces[name] = [(j, v) for (j, _), (_, v) in zip(self.pieces[name], pieces)]
        self.kept = dict(zip(kept, values[2]))
        self.flying = {}
        for (kind, name), value in zip(flying, values[1]):
            if kind == "kept":
                self.kept[name] = value
                continue
            bit = self.order[name].pop(0)
            held = self.pieces[name]
            self.pieces[name] = held + [(j | bit, value[n]) for n, (j, _) in enumerate(held)]
            self.next(name)
        extra = values[3]
        return extra[0] if len(extra) == 1 else extra

    def whole(self, name):
        return name in self.pieces and not self.order[name]

    def take_half(self, name):
        pieces = dict(self.pieces.pop(name))
        return jnp.stack([pieces[2 * i] for i in range(self.nd // 2)])


def pack_kernel(index_ref, in_ref, out_ref):
    nd = index_ref.shape[0] - 1
    wide = in_ref.shape[2] // nd
    for p in range(nd):
        there = pl.ds(pl.multiple_of(index_ref[p] * wide, wide), wide)
        out_ref[:, p * wide : (p + 1) * wide] = in_ref[0, :, there]


def pack_features(value, index, which):
    micro, rows, width = value.shape
    nd = index.shape[0]
    if width // nd % 128:
        chunk = lax.dynamic_index_in_dim(value, which, 0, keepdims=False)
        return jnp.take(chunk.reshape(rows, nd, -1), index, axis=1).reshape(rows, width)
    return pl.pallas_call(
        pack_kernel,
        grid_spec=pltpu.PrefetchScalarGridSpec(
            num_scalar_prefetch=1,
            grid=(1,),
            in_specs=[pl.BlockSpec((1, rows, width), lambda i, index_ref: (index_ref[nd], 0, 0))],
            out_specs=pl.BlockSpec((rows, width), lambda i, index_ref: (0, 0)),
        ),
        out_shape=SHAPE((rows, width), value.dtype),
        compiler_params=params(),
        cost_estimate=cost(0, 6 * rows * width),
        name="pack_features",
    )(jnp.append(index, which.astype(jnp.int32)), value)


def unpack_kernel(index_ref, *refs):
    ins, out_ref = refs[:-1], refs[-1]
    nd = index_ref.shape[0] - len(ins)
    wide = out_ref.shape[2] // nd
    for k, in_ref in enumerate(ins):
        for p in range(nd):
            there = pl.ds(pl.multiple_of(index_ref[p] * wide, wide), wide)
            out_ref[index_ref[nd + k], :, there] = in_ref[:, p * wide : (p + 1) * wide]


def unpack_features(chunks, index, places):
    rows, width = chunks[0].shape
    micro, nd = len(chunks), index.shape[0]
    places = [place.astype(jnp.int32) for place in places]
    if width // nd % 128:
        back = jnp.argsort(index)
        stacked = jnp.stack(chunks).reshape(micro, rows, nd, -1)
        stacked = jnp.take(stacked, back, axis=2).reshape(micro, rows, width)
        return jnp.take(stacked, jnp.argsort(jnp.stack(places)), axis=0)
    return pl.pallas_call(
        unpack_kernel,
        in_specs=[pl.BlockSpec(memory_space=pltpu.SMEM)] + [WHOLE] * micro,
        out_specs=WHOLE,
        out_shape=SHAPE((micro, rows, width), chunks[0].dtype),
        compiler_params=params(),
        cost_estimate=cost(0, 4 * micro * rows * width),
        name="unpack_features",
    )(jnp.concatenate([index, jnp.stack(places)]), *chunks)


def standardize(state):
    centre = jnp.mean(state, axis=-1, keepdims=True)
    centred = state - centre
    spread = jnp.mean(centred * centred, axis=-1, keepdims=True)
    inverse = lax.rsqrt(spread + EPSILON)
    return centred * inverse, inverse


def norm_back(grad, state, gain):
    scaled, inverse = standardize(state)
    weighted = grad * gain
    first = jnp.mean(weighted, axis=-1, keepdims=True)
    second = jnp.mean(weighted * scaled, axis=-1, keepdims=True)
    sums = jnp.concatenate(
        [jnp.sum(grad * scaled, axis=0, keepdims=True), jnp.sum(grad, axis=0, keepdims=True)], 0
    )
    return inverse * (weighted - first - scaled * second), sums


def first_norm_kernel(micro, *refs):
    chunks = refs[:micro]
    gain_ref, bias_ref, x_ref, out_ref = refs[micro:]
    rows = chunks[0].shape[0]
    for k, ref in enumerate(chunks):
        here = slice(k * rows, (k + 1) * rows)
        x_ref[here] = ref[...]
        scaled, _ = standardize(ref[...].astype(F32))
        out_ref[here] = (scaled * gain_ref[...] + bias_ref[...]).astype(BF16)


def first_norm(chunks, gain, bias):
    rows, width = chunks[0].shape
    rows = rows * len(chunks)
    return pl.pallas_call(
        functools.partial(first_norm_kernel, len(chunks)),
        in_specs=[WHOLE] * (len(chunks) + 2),
        out_specs=[WHOLE] * 2,
        out_shape=[SHAPE((rows, width), BF16)] * 2,
        compiler_params=params(),
        cost_estimate=cost(0, 8 * rows * width),
        name="first_norm",
    )(*chunks, gain, bias)


def each_k(refs):
    return [(ref, n) for ref in refs for n in range(ref.shape[1])]


def proj_kernel(parts, in_ref, *refs):
    owns, others, out_ref = refs[:parts], refs[parts : 2 * parts], refs[-1]
    value = in_ref[...]
    half = value.shape[1] // 2
    wide = owns[0].shape[-1]
    for k, ((own, n), (other, _)) in enumerate(zip(each_k(owns), each_k(others))):
        first = own[:, n, 0].reshape(half, wide)
        second = other[:, n, 0].reshape(half, wide)
        total = dot_nn(value[:, :half], first) + dot_nn(value[:, half:], second)
        out_ref[0, :, k * wide : (k + 1) * wide] = total.astype(BF16)


def head_spec(array, count, index_map):
    chips, ks, _, deep, wide = array.shape
    return pl.BlockSpec((chips, ks, count, deep, wide), index_map)


def project(value, weights, start, count):
    rows, width = value.shape
    wide = weights[0][0].shape[-1]
    nm = sum(array.shape[1] for array in weights[0])
    arrays = [*weights[0], *weights[1]]
    return pl.pallas_call(
        functools.partial(proj_kernel, len(weights[0])),
        grid=(count,),
        in_specs=[pl.BlockSpec((rows, width), lambda i: (0, 0))]
        + [head_spec(array, 1, lambda i: (0, 0, start + i, 0, 0)) for array in arrays],
        out_specs=pl.BlockSpec((1, rows, nm * wide), lambda i: (i, 0, 0)),
        out_shape=SHAPE((count, rows, nm * wide), BF16),
        compiler_params=params(),
        cost_estimate=cost(2 * count * rows * width * nm * wide, 2 * count * rows * width),
        name="project",
    )(value, *arrays)


def attend_kernel(parts, q_ref, *refs):
    k_refs, v_refs = refs[:parts], refs[parts : 2 * parts]
    bias_ref, out_ref, lse_ref = refs[2 * parts :]
    rows = q_ref.shape[1]
    low = lax.broadcasted_iota(jnp.int32, (1, PAIR), 1) < HDIM
    query = q_ref[0] * jnp.asarray(HDIM ** (-0.5), BF16)
    mixed = None
    for head in range(2):
        mine = low if head == 0 else jnp.logical_not(low)
        q_mine = jnp.where(mine, query, jnp.zeros_like(query))
        scores = [
            jnp.where(bias_ref[p : p + 1, :] < 0.0, MASKED, dot_nt(q_mine, k_refs[p][0]))
            for p in range(parts)
        ]
        top = functools.reduce(
            jnp.maximum, [jnp.max(part, axis=1, keepdims=True) for part in scores]
        )
        total, part = 0.0, 0.0
        for p in range(parts):
            expo = jnp.exp(scores[p] - top)
            total = total + jnp.sum(expo, axis=1, keepdims=True)
            part = part + dot_nn(expo.astype(BF16), v_refs[p][0])
        part = part / total
        mixed = part if head == 0 else jnp.where(low, mixed, part)
        lse = top + jnp.log(total)
        lse_ref[0, head : head + 1, :] = jnp.transpose(jnp.broadcast_to(lse, (rows, 128)))[0:1, :]
    out_ref[...] = mixed.astype(BF16)


def attend(query, kvs, bias, start, count):
    _, rows, width = query.shape
    parts = len(kvs)
    block = row_block(rows)
    keys = rows * parts
    key_spec = pl.BlockSpec((1, rows, PAIR), lambda h, i: (0, 0, start + h))
    value_spec = pl.BlockSpec((1, rows, PAIR), lambda h, i: (1, 0, start + h))
    return pl.pallas_call(
        functools.partial(attend_kernel, parts),
        grid=(count, rows // block),
        in_specs=[pl.BlockSpec((1, block, PAIR), lambda h, i: (0, i, start + h))]
        + [key_spec] * parts
        + [value_spec] * parts
        + [pl.BlockSpec((parts, rows), lambda h, i: (0, 0))],
        out_specs=[
            pl.BlockSpec((block, PAIR), lambda h, i: (i, h)),
            pl.BlockSpec((1, 2, block), lambda h, i: (h, 0, i)),
        ],
        out_shape=[SHAPE((rows, count * PAIR), BF16), SHAPE((count, 2, rows), F32)],
        compiler_params=params(),
        cost_estimate=cost(16 * rows * keys * count * PAIR, 8 * keys * count * PAIR),
        name="attend",
    )(query, *kvs, *kvs, bias)


def attend_back_kernel(parts, q_ref, *refs):
    k_refs, v_refs = refs[:parts], refs[parts : 2 * parts]
    bias_ref, lse_ref, mixed_ref, grad_ref, dq_ref = refs[2 * parts : 2 * parts + 5]
    dkv_refs = refs[2 * parts + 5 : 3 * parts + 5]
    dk_acc, dv_acc = refs[3 * parts + 5 :]
    step = pl.program_id(1)
    low = lax.broadcasted_iota(jnp.int32, (1, PAIR), 1) < HDIM
    query = q_ref[0] * jnp.asarray(HDIM ** (-0.5), BF16)
    grad = grad_ref[0]
    product = mixed_ref[...].astype(F32) * grad.astype(F32)

    @pl.when(step == 0)
    def _():
        dk_acc[...] = jnp.zeros_like(dk_acc)
        dv_acc[...] = jnp.zeros_like(dv_acc)

    grad_query = None
    for head in range(2):
        mine = low if head == 0 else jnp.logical_not(low)
        q_mine = jnp.where(mine, query, jnp.zeros_like(query))
        g_mine = jnp.where(mine, grad, jnp.zeros_like(grad))
        delta = jnp.sum(jnp.where(mine, product, 0.0), axis=1, keepdims=True)
        delta = jnp.transpose(jnp.broadcast_to(delta, (delta.shape[0], 128)))[0:1, :]
        query_part = 0.0
        for p in range(parts):
            keys, values = k_refs[p][0], v_refs[p][0]
            scores = jnp.where(bias_ref[p] < 0.0, MASKED, dot_nt(keys, q_mine))
            probs = jnp.exp(scores - lse_ref[0, head : head + 1, :])
            upstream = dot_nt(values, g_mine)
            grad_scores = (probs * (upstream - delta)).astype(BF16)
            dv_acc[p] += dot_nn(probs.astype(BF16), g_mine)
            dk_acc[p] += dot_nn(grad_scores, q_mine)
            query_part = query_part + dot_tn(grad_scores, keys)
        grad_query = query_part if head == 0 else jnp.where(low, grad_query, query_part)
    dq_ref[...] = (grad_query * HDIM ** (-0.5)).astype(BF16)

    @pl.when(step == pl.num_programs(1) - 1)
    def _():
        for p in range(parts):
            dkv_refs[p][0] = dk_acc[p].astype(BF16)
            dkv_refs[p][1] = dv_acc[p].astype(BF16)


def attend_back(query, kvs, bias, lse, mixed, grad, start, count):
    _, rows, width = query.shape
    parts = len(kvs)
    block = row_block(rows)
    keys = rows * parts
    key_spec = pl.BlockSpec((1, rows, PAIR), lambda h, i: (0, 0, start + h))
    value_spec = pl.BlockSpec((1, rows, PAIR), lambda h, i: (1, 0, start + h))
    return pl.pallas_call(
        functools.partial(attend_back_kernel, parts),
        grid=(count, rows // block),
        in_specs=[pl.BlockSpec((1, block, PAIR), lambda h, i: (0, i, start + h))]
        + [key_spec] * parts
        + [value_spec] * parts
        + [
            pl.BlockSpec((parts, rows, 1), lambda h, i: (0, 0, 0)),
            pl.BlockSpec((1, 2, block), lambda h, i: (h, 0, i)),
            pl.BlockSpec((block, PAIR), lambda h, i: (i, h)),
            pl.BlockSpec((1, block, PAIR), lambda h, i: (0, i, start + h)),
        ],
        out_specs=[pl.BlockSpec((block, PAIR), lambda h, i: (i, h))]
        + [pl.BlockSpec((2, rows, PAIR), lambda h, i: (0, 0, h))] * parts,
        out_shape=[SHAPE((rows, count * PAIR), BF16)]
        + [SHAPE((2, rows, count * PAIR), BF16)] * parts,
        scratch_shapes=[pltpu.VMEM((parts, rows, PAIR), F32)] * 2,
        compiler_params=params(),
        cost_estimate=cost(40 * rows * keys * count * PAIR, 16 * keys * count * PAIR),
        name="attend_back",
    )(query, *kvs, *kvs, bias, lse, mixed, grad)


def middle_kernel(nm, parts, x_ref, *refs):
    mixed_refs, refs = refs[:nm], refs[nm:]
    weights = refs[:parts], refs[parts : 2 * parts]
    gain_ref, bias_ref, mid_ref, out_ref = refs[2 * parts :]
    half = x_ref.shape[1] // 2
    sides = []
    for side in weights:
        total = 0.0
        for k, (ref, n) in enumerate(each_k(side)):
            total = total + dot_nt(mixed_refs[k][...], ref[:, n, 0].reshape(half, -1))
        sides.append(total)
    middle = x_ref[...].astype(F32) + jnp.concatenate(sides, axis=1)
    mid_ref[...] = middle
    scaled, _ = standardize(middle)
    out_ref[...] = (scaled * gain_ref[...] + bias_ref[...]).astype(BF16)


def middle_norm(x, mixed, weights, which, gain, bias):
    rows, width = x.shape
    nm, wide = len(mixed), mixed[0].shape[1]
    block = row_block(rows)
    vector = pl.BlockSpec((1, width), lambda i: (0, 0))
    line = pl.BlockSpec((block, width), lambda i: (i, 0))
    arrays = [*weights[0], *weights[1]]
    return pl.pallas_call(
        functools.partial(middle_kernel, nm, len(weights[0])),
        grid=(rows // block,),
        in_specs=[line]
        + [pl.BlockSpec((block, wide), lambda i: (i, 0))] * nm
        + [head_spec(array, 1, lambda i: (0, 0, which, 0, 0)) for array in arrays]
        + [vector, vector],
        out_specs=[line, line],
        out_shape=[SHAPE((rows, width), F32), SHAPE((rows, width), BF16)],
        compiler_params=params(),
        cost_estimate=cost(2 * rows * width * nm * wide, 14 * x.size),
        name="middle_norm",
    )(x, *mixed, *arrays, gain, bias)


def load_weights(firsts, sizes, index_ref, refs, held, sems):
    step = pl.program_id(0)
    nm = firsts + sum(sizes)
    chips = held.shape[2]
    copies, refs = {k: [] for k in range(nm)}, list(refs)

    def add(k, source, w, side, n, sem):
        copies[k].append(
            pltpu.make_async_copy(source, held.at[w, 2 * k + side, n], sems.at[w, 2 * k + side, sem])
        )

    ref = refs.pop(0)
    for k in range(firsts):
        for w in range(2):
            for side in range(2):
                for n in range(chips):
                    add(k, ref.at[index_ref[side * chips + n], k, w], w, side, n, n)
    k = firsts
    for size in sizes:
        sides = [refs.pop(0) for _ in range(4)]
        for i in range(size):
            for n, ref in enumerate(sides):
                add(k, ref.at[:, i], n // 2, n % 2, slice(None), 0)
            k += 1

    @pl.when(step == 0)
    def _():
        for k in range(nm):
            for copy in copies[k]:
                copy.start()

    for k in range(nm):

        @pl.when(step == k)
        def _():
            for copy in copies[k]:
                copy.wait()


def feed_kernel(firsts, sizes, index_ref, *refs):
    nm, count = firsts + sum(sizes), 1 + 4 * len(sizes)
    in_ref, mid_ref, out_ref, act_ref, slope_ref, held, acc, sems = refs[count:]
    step = pl.program_id(0)
    load_weights(firsts, sizes, index_ref, refs[:count], held, sems)
    half = in_ref.shape[1] // 2
    up = [held[0, 2 * step + side].reshape(half, -1) for side in range(2)]
    down = [held[1, 2 * step + side].reshape(half, -1) for side in range(2)]

    @pl.when(step == 0)
    def _():
        acc[...] = mid_ref[...]

    hidden = dot_nn(in_ref[:, :half], up[0]) + dot_nn(in_ref[:, half:], up[1])
    below = 0.5 + 0.5 * lax.erf(hidden * (0.5**0.5))
    density = jnp.exp(-0.5 * hidden * hidden) * 0.3989422804014327
    active = (hidden * below).astype(BF16)
    act_ref[0] = active
    slope_ref[0] = (below + hidden * density).astype(BF16)
    acc[:, :half] += dot_nt(active, down[0])
    acc[:, half:] += dot_nt(active, down[1])

    @pl.when(step == nm - 1)
    def _():
        out_ref[...] = acc[...].astype(BF16)


def feed(normed, middle, index, firsts, sizes, weights):
    rows, width = normed.shape
    nm = firsts + sum(sizes)
    nd, (deep, hidden) = index.shape[0], weights[0].shape[3:]
    chips = nd // 2
    line = pl.BlockSpec((rows, width), lambda k: (0, 0))
    wide = pl.BlockSpec((1, rows, hidden), lambda k: (k, 0, 0))
    return pl.pallas_call(
        functools.partial(feed_kernel, firsts, sizes),
        grid=(nm,),
        in_specs=[pl.BlockSpec(memory_space=pltpu.SMEM)]
        + [ANY] * len(weights)
        + [line, line],
        out_specs=[line, wide, wide],
        out_shape=[SHAPE((rows, width), BF16)] + [SHAPE((nm, rows, hidden), BF16)] * 2,
        scratch_shapes=[
            pltpu.VMEM((2, 2 * nm, chips, deep, hidden), BF16),
            pltpu.VMEM((rows, width), F32),
            pltpu.SemaphoreType.DMA((2, 2 * nm, chips)),
        ],
        compiler_params=params(60),
        cost_estimate=cost(4 * rows * width * nm * hidden, 4 * nm * width * hidden),
        name="feed",
    )(index, *weights, normed, middle)


def feed_back_kernel(firsts, sizes, index_ref, *refs):
    nm, count = firsts + sum(sizes), 1 + 4 * len(sizes)
    g_ref, slope_ref, mid_ref, gain_ref = refs[count : count + 4]
    hid_ref, attn_ref, sums_ref, held, acc, sems = refs[count + 4 :]
    step = pl.program_id(0)
    load_weights(firsts, sizes, index_ref, refs[:count], held, sems)
    half = g_ref.shape[1] // 2
    up = [held[0, 2 * step + side].reshape(half, -1) for side in range(2)]
    down = [held[1, 2 * step + side].reshape(half, -1) for side in range(2)]
    active = dot_nn(g_ref[:, :half], down[0]) + dot_nn(g_ref[:, half:], down[1])
    hidden = (active * slope_ref[0].astype(F32)).astype(BF16)
    hid_ref[0] = hidden
    first, second = dot_nt(hidden, up[0]), dot_nt(hidden, up[1])

    @pl.when(step == 0)
    def _():
        acc[:, :half] = first
        acc[:, half:] = second

    @pl.when(step > 0)
    def _():
        acc[:, :half] += first
        acc[:, half:] += second

    @pl.when(step == nm - 1)
    def _():
        into, sums = norm_back(acc[...], mid_ref[...], gain_ref[...])
        attn_ref[...] = (g_ref[...].astype(F32) + into).astype(BF16)
        sums_ref[...] = sums


def feed_back(grad, slope, middle, gain, index, firsts, sizes, weights):
    rows, width = grad.shape
    nm = firsts + sum(sizes)
    nd, (deep, hidden) = index.shape[0], weights[0].shape[3:]
    chips = nd // 2
    line = pl.BlockSpec((rows, width), lambda k: (0, 0))
    wide = pl.BlockSpec((1, rows, hidden), lambda k: (k, 0, 0))
    return pl.pallas_call(
        functools.partial(feed_back_kernel, firsts, sizes),
        grid=(nm,),
        in_specs=[pl.BlockSpec(memory_space=pltpu.SMEM)]
        + [ANY] * len(weights)
        + [line, wide, line, pl.BlockSpec((1, width), lambda k: (0, 0))],
        out_specs=[
            wide,
            line,
            pl.BlockSpec((2, width), lambda k: (0, 0)),
        ],
        out_shape=[
            SHAPE((nm, rows, hidden), BF16),
            SHAPE((rows, width), BF16),
            SHAPE((2, width), F32),
        ],
        scratch_shapes=[
            pltpu.VMEM((2, 2 * nm, chips, deep, hidden), BF16),
            pltpu.VMEM((rows, width), F32),
            pltpu.SemaphoreType.DMA((2, 2 * nm, chips)),
        ],
        compiler_params=params(60),
        cost_estimate=cost(4 * rows * width * nm * hidden, 4 * nm * width * hidden),
        name="feed_back",
    )(index, *weights, grad, slope, middle, gain)


def wide_grad_kernel(place_ref, a_ref, b_ref, out_ref):
    part = dot_tn(a_ref[...], b_ref[0]).astype(BF16)
    nd, deep = out_ref.shape[0], out_ref.shape[2]
    for p in range(nd):
        out_ref[place_ref[p], 0] = part[p * deep : (p + 1) * deep]


def wide_grad(rows_in, values, place, absolute):
    rows, width = rows_in.shape
    nm, _, hidden = values.shape
    nd = place.shape[0] - 1
    block = min(512, hidden)

    def out_map(k, i, place_ref):
        return (0, lax.rem(place_ref[nd] + nm - k, nm) if absolute else k, 0, i)

    return pl.pallas_call(
        wide_grad_kernel,
        grid_spec=pltpu.PrefetchScalarGridSpec(
            num_scalar_prefetch=1,
            grid=(nm, hidden // block),
            in_specs=[
                pl.BlockSpec((rows, width), lambda k, i, place_ref: (0, 0)),
                pl.BlockSpec((1, rows, block), lambda k, i, place_ref: (k, 0, i)),
            ],
            out_specs=pl.BlockSpec((nd, 1, width // nd, block), out_map),
        ),
        out_shape=SHAPE((nd, nm, width // nd, hidden), BF16),
        compiler_params=params(),
        cost_estimate=cost(2 * nm * width * rows * hidden, 4 * nm * width * hidden),
        name="wide_grad",
    )(place, rows_in, values)


def head_grad_kernel(
    n_ref, g_ref, mixed_ref, dq_ref, dkv_ref, came_ref, sum_ref, keep_ref, give_ref
):
    chips, _, deep, wide = keep_ref.shape
    half = chips * deep
    total = (dkv_ref[...].astype(F32) + came_ref[...].astype(F32)).astype(BF16)
    sum_ref[...] = total
    three = dot_tn(n_ref[...], jnp.concatenate([dq_ref[...], total[0], total[1]], axis=1))
    one = dot_tn(g_ref[...], mixed_ref[...])
    parts = (three[:, :wide], one, three[:, wide : 2 * wide], three[:, 2 * wide :])
    for i, part in enumerate(parts):
        part = part.astype(BF16)
        keep_ref[:, i] = part[:half].reshape(chips, deep, wide)
        give_ref[:, i] = part[half:].reshape(chips, deep, wide)


def head_grad(normed, attn, mixed, dq, dkv, came, chips):
    rows, width = normed.shape
    wide = dq.shape[1]
    piece = SHAPE((chips, 4, width // 2 // chips, wide), BF16)
    total, keep, give = pl.pallas_call(
        head_grad_kernel,
        in_specs=[WHOLE] * 6,
        out_specs=[WHOLE] * 3,
        out_shape=[SHAPE(dkv.shape, BF16), piece, piece],
        compiler_params=params(),
        cost_estimate=cost(8 * width * rows * wide, 8 * width * wide),
        name="head_grad",
    )(normed, attn, mixed, dq, dkv, came)
    return total, keep[None], give[None]


def first_back_kernel(nm, parts, x_ref, attn_ref, gain_ref, *refs):
    dqs, dkvs, came_ref, refs = refs[:nm], refs[nm : 2 * nm], refs[2 * nm], refs[2 * nm + 1 :]
    qo = refs[:parts], refs[parts : 2 * parts]
    kv = refs[2 * parts : 3 * parts], refs[3 * parts : 4 * parts]
    out_ref, sums_ref = refs[4 * parts :]
    last = (dkvs[0][...].astype(F32) + came_ref[...].astype(F32)).astype(BF16)
    half = x_ref.shape[1] // 2
    sides = []
    for side in range(2):
        total = 0.0
        for k, ((qo_ref, n), (kv_ref, _)) in enumerate(zip(each_k(qo[side]), each_k(kv[side]))):
            total = total + dot_nt(dqs[k][...], qo_ref[:, n, 0].reshape(half, -1))
            for i in range(2):
                dkv = dkvs[k][i] if k else last[i]
                total = total + dot_nt(dkv, kv_ref[:, n, i].reshape(half, -1))
        sides.append(total)
    into, sums = norm_back(jnp.concatenate(sides, axis=1), x_ref[...].astype(F32), gain_ref[...])
    out_ref[...] = (attn_ref[...].astype(F32) + into).astype(BF16)
    sums_ref[...] = sums


def first_back(x, attn, gain, dqs, dkvs, came, qo, kv, part, block):
    width = x.shape[1]
    nm, wide = len(dqs), dqs[0].shape[1]
    line = pl.BlockSpec((block, width), lambda i: (part, 0))
    still = lambda i: (0, 0, 0, 0, 0)
    qo_arrays, kv_arrays = [*qo[0], *qo[1]], [*kv[0], *kv[1]]
    return pl.pallas_call(
        functools.partial(first_back_kernel, nm, len(qo[0])),
        grid=(1,),
        in_specs=[line, line, pl.BlockSpec((1, width), lambda i: (0, 0))]
        + [pl.BlockSpec((block, wide), lambda i: (part, 0))] * nm
        + [pl.BlockSpec((2, block, wide), lambda i: (0, part, 0))] * (nm + 1)
        + [head_spec(array, 1, still) for array in qo_arrays]
        + [head_spec(array, 2, still) for array in kv_arrays],
        out_specs=[
            pl.BlockSpec((block, width), lambda i: (0, 0)),
            pl.BlockSpec((2, width), lambda i: (0, 0)),
        ],
        out_shape=[SHAPE((block, width), BF16), SHAPE((2, width), F32)],
        compiler_params=params(),
        cost_estimate=cost(6 * block * width * nm * wide, 12 * block * width),
        name="first_back",
    )(x, attn, gain, *dqs, *dkvs, came, *qo_arrays, *kv_arrays)


def add_low(a, b):
    return (a.astype(F32) + b.astype(F32)).astype(BF16)


def add_parts_kernel(pairs, *refs):
    outs, row = refs[2 * pairs :], 0
    for i in range(pairs):
        keep_ref, came_ref = refs[2 * i : 2 * i + 2]
        size = keep_ref.shape[0]
        for n, out in enumerate(outs):
            out[row : row + size] = add_low(keep_ref[:, n + 1], came_ref[:, n + 1])
        row += size


def add_parts(pairs):
    keep = pairs[0][0]
    rows = sum(pair[0].shape[0] for pair in pairs)
    piece = SHAPE((rows,) + keep.shape[2:], keep.dtype)
    return pl.pallas_call(
        functools.partial(add_parts_kernel, len(pairs)),
        in_specs=[WHOLE] * (2 * len(pairs)),
        out_specs=[WHOLE] * (keep.shape[1] - 1),
        out_shape=[piece] * (keep.shape[1] - 1),
        compiler_params=params(),
        cost_estimate=cost(0, 6 * len(pairs) * keep.size),
        name="add_parts",
    )(*[array for pair in pairs for array in pair])


class Scatter:
    def __init__(self, nd, nm, bits):
        self.nd, self.nm = nd, nm
        self.queue = {1: [], **{bit: [] for bit in bits}, "direct": [], "z": []}
        self.order, self.kept, self.waits, self.flying = {}, {}, {}, {}
        self.ends, self.came, self.done, self.rings, self.joined = {}, {}, {}, {}, {}

    def add(self, name, ks, keep, give, order, rings=True):
        self.order[name, tuple(ks)], self.rings[name] = order, rings
        self.push(1, (name, tuple(ks), -1), list(range(0, self.nd, 2)), keep, give)

    def add_line(self, name, value, rings):
        self.rings[name] = rings
        if rings:
            for k in range(self.nm):
                self.ends[name, k] = (value[k],)
            self.advance(name, self.nm - 1)
            return
        self.ends[name] = [value[0]]
        for k in sorted(range(1, self.nm), key=lambda k: min(k, self.nm - k)):
            self.waits[name, k, "z"] = value[k]
            self.queue["z"].append((name, k, "z"))

    def push(self, link, key, places, keep, give):
        self.kept[key], self.waits[key] = (places, keep), give
        self.queue[link].append(key)

    def launch(self, core=1, chip=1, direct=1, z=1):
        for link, tasks in self.queue.items():
            for _ in range({1: core, "direct": direct, "z": z}.get(link, chip)):
                if not tasks:
                    break
                key = tasks.pop(0)
                value = self.waits.pop(key)
                if link == "z" and not self.rings[key[0]]:
                    value = ring(value, -key[1], self.nm)
                elif link == "z":
                    value = ring(value, -1, self.nm)
                elif link == "direct":
                    more = [tasks.pop(0) for _ in range(min(direct - 1, len(tasks)))]
                    self.joined[key] = more
                    value = add_parts([value] + [self.waits.pop(other) for other in more])
                    value = [swap(part, 2 * n + 2, self.nd) for n, part in enumerate(value)]
                    self.flying[key] = value
                    break
                else:
                    value = swap(value, link, self.nd)
                self.flying[key] = value

    def busy(self):
        return bool(self.flying) or any(self.queue.values())

    def land(self, *extra):
        waits, flying = list(self.waits), list(self.flying)
        values = lax.optimization_barrier(
            ([self.waits[key] for key in waits], [self.flying[key] for key in flying], extra)
        )
        self.waits = dict(zip(waits, values[0]))
        came = dict(zip(flying, values[1]))
        self.flying = {}
        for key, value in came.items():
            if key not in self.joined:
                self.arrive(key, value)
                continue
            for other in [key] + self.joined.pop(key):
                self.arrive(other, [part[: len(other[1])] for part in value])
                value = [part[len(other[1]) :] for part in value]
        extra = values[2]
        return extra[0] if len(extra) == 1 else extra

    def arrive(self, key, value):
        name, ks, stage = key
        if stage == "z" and not self.rings[name]:
            self.ends[name].append(value)
            if len(self.ends[name]) == self.nm:
                self.done[name] = sum(part.astype(F32) for part in self.ends.pop(name))
            return
        if stage == "z":
            self.came[name, ks - 1] = value
            self.advance(name, ks - 1)
            return
        order = self.order[name, ks]
        places, keep = self.kept.pop(key)
        if order is None and stage == -1:
            own = (keep[:, 0], value[:, 0])
            self.push("direct", (name, ks, 0), own, None, (keep, value))
            return
        if order is None:
            for n, k in enumerate(ks):
                self.ends[name, k] = tuple(part[n] for part in [*places, *value])
                self.advance(name, k)
            return
        if stage + 1 == len(order):
            for n, k in enumerate(ks):
                self.ends[name, k] = (keep[n, 0], value[n, 0])
            for k in reversed(ks):
                self.advance(name, k)
            return
        bit = order[stage + 1]
        stays = [n for n, j in enumerate(places) if not j & bit]
        goes = [n for n, j in enumerate(places) if j & bit]

        def take(array, which):
            return jnp.stack([array[:, n] for n in which], axis=1)

        self.push(
            bit,
            (name, ks, stage + 1),
            [places[n] for n in stays],
            add_low(take(keep, stays), take(value, stays)),
            add_low(take(keep, goes), take(value, goes)),
        )

    def advance(self, name, k):
        if (name, k) not in self.ends or (k < self.nm - 1 and (name, k) not in self.came):
            return
        total = sum(part.astype(F32) for part in self.ends.pop((name, k)))
        if k < self.nm - 1:
            total = total + self.came.pop((name, k)).astype(F32)
        if k:
            key = (name, k, "z")
            self.waits[key] = total.astype(BF16)
            self.queue["z"].append(key)
        else:
            self.done[name] = total


def shards(nd, nm, tokens, views, norm_gains, norm_biases, w_proj, w_out, w_up, w_down, cotangent):
    micro, _, chunk, width = tokens.shape
    ranks = nm // micro
    half = max(ranks // 2, 1)
    rows = micro * chunk
    chips = nd // 2
    wide = w_out.shape[2]
    per_k = wide // PAIR
    hidden = w_up.shape[2]
    dp, mp = lax.axis_index("dp"), lax.axis_index("mp")
    group = mp // half
    step_here = group // 2
    rank = (dp & 1) + 2 * (mp % half)
    order_of = [2 * (p % chips) + p // chips for p in range(nd)]
    offsets = jnp.asarray(order_of, jnp.int32)
    index = dp.astype(jnp.int32) ^ offsets

    def routes(k):
        pairs = []
        for d in range(nd):
            for z in range(nm):
                m = (k + z) % micro
                r = z // micro
                to_d = (d & ~1) | (r & 1)
                to_z = (2 * m + (d & 1)) * half + r // 2
                pairs.append((d * nm + z, to_d * nm + to_z))
        return pairs

    there = ((dp & ~1) | ((mp // micro) & 1)).astype(jnp.int32) ^ offsets

    def pack(value, k):
        return pack_features(value, there, (k + mp) % micro)

    def send(packed, k):
        return lax.ppermute(packed[k], ("dp", "mp"), routes(k))

    def back_routes(k):
        return [(b, a) for a, b in routes(k)]

    def send_chunk(chunks, k):
        return lax.ppermute(chunks[k], ("dp", "mp"), back_routes(k))

    def unpack(came):
        return unpack_features(came, there, [(k + mp) % micro for k in range(micro)])

    def by_place(vector):
        return jnp.take(vector.reshape(-1, nd, width // nd), index, axis=1).reshape(-1, width)

    flow = Flow(nd, nm)
    forth, back = flow.bits, flow.bits[::-1]
    firsts = min(2, nm)
    groups = [list(range(k, min(k + 2, nm))) for k in range(firsts, nm, 2)]
    sizes = tuple(len(group) for group in groups)
    head = [jnp.concatenate([w_proj[0], w_out])]
    feeds = [jnp.concatenate([w_up, w_down])]
    gather = functools.partial(lax.all_gather, axis_name="dp")
    head_groups = [[0], list(range(1, nm))]

    def headed(n):
        flow.add(f"qo{n}", jnp.stack([head[k][::3] for k in head_groups[n]]), forth)
        flow.add(f"kv{n}", jnp.stack([head[k][1:3] for k in head_groups[n]]), back)

    halves = {}

    def core_halves(most, names):
        for name in names:
            if most and flow.whole(name):
                halves[name] = flow.take_half(name)
                flow.fly(name, swap(halves[name], 1, nd))
                most -= 1

    for k in sorted(range(1, nm), key=lambda k: -min(k, nm - k)):
        flow.fly(("head", k), ring(head[0], k, nm))
    headed(0)
    flow.launch()
    token_parts = [pack(tokens[:, 0], k) for k in range(micro)]
    view = lax.dynamic_index_in_dim(views[:, 0], mp % micro, 0, keepdims=True)
    head, tokens, token_parts, cotangent, there, view, feeds, norm_gains, norm_biases = flow.land(
        head, tokens, token_parts, cotangent, there, view, feeds, norm_gains, norm_biases
    )
    head += [flow.kept.pop(("head", k)) for k in range(1, nm)]
    headed(1)
    weights = []
    came = []
    head_names = [f"{name}{n}" for n in range(len(head_groups)) for name in ("kv", "qo")]
    while len(came) < micro or not all(n in halves or flow.whole(n) for n in head_names):
        if len(came) < micro:
            came.append(send(token_parts, len(came)))
        flow.launch(chip=2)
        if len(came) == micro:
            core_halves(2, head_names)
        if len(came) == 1:
            grad_parts = [pack(cotangent[:, 0], k) for k in range(micro)]
            gains, biases = by_place(norm_gains[0]), by_place(norm_biases[0])
        came, token_parts, grad_parts, feeds, halves, gains, biases, view = flow.land(
            came, token_parts, grad_parts, feeds, halves, gains, biases, view
        )

    def turn():
        if len(feeds) < nm:
            feeds.append(ring(feeds[-1], 1, nm))

    def turned():
        if not weights and len(feeds) >= firsts:
            weights.append(gather(jnp.stack(feeds[:firsts])))
        for n, group in enumerate(groups):
            if f"up{n}" not in flow.order and group[-1] < len(feeds):
                flow.add(f"up{n}", jnp.stack([feeds[k][0] for k in group]), forth)
                flow.add(f"down{n}", jnp.stack([feeds[k][1] for k in group]), back)

    last = [f"{name}{n}" for n in range(len(groups)) for name in ("up", "down")]
    core_halves(len(head_names), head_names)
    turn()
    x, normed = first_norm(came, gains[:1], biases[:1])
    x, normed, halves, feeds, view = flow.land(x, normed, halves, feeds, view)
    turned()

    def both(name):
        names = [f"{name}{n}" for n in range(len(head_groups))]
        return [halves.pop(n) for n in names], [flow.kept.pop(n) for n in names]

    qo, kv = both("qo"), both("kv")

    turn()
    flow.launch()
    views = lax.ppermute(view, ("dp", "mp"), routes(0))
    own_kv = project(normed, kv, 0, 2)
    own_kv, normed, qo, feeds, views = flow.land(own_kv, normed, qo, feeds, views)
    turned()

    def swap_rank(value, bit):
        if bit == 1:
            return swap(value, 1, nd)
        return lax.ppermute(value, "mp", [(i, i ^ (bit >> 1)) for i in range(nm)])

    rank_bits = [1 << b for b in range(ranks.bit_length() - 1)]
    kvs = {0: own_kv}
    for bit in rank_bits:
        for j in list(kvs):
            kvs[j | bit] = swap_rank(kvs[j], bit)
    kvs = [kvs[j] for j in range(ranks)]
    turn()
    flow.launch()
    query = project(normed, qo, 0, 1)
    slot = jnp.stack([(step_here - t) % micro for t in range(micro)])
    within = (slot[:, None] * chunk + jnp.arange(chunk)[None]).reshape(-1)
    position = jnp.stack([(rank ^ j) * rows + within for j in range(ranks)])
    bias = jnp.where(position < TRI + views[0] * VIEW_TOK, 0.0, -1.0).astype(F32)
    kvs, query, bias, grad_parts, feeds = flow.land(kvs, query, bias, grad_parts, feeds)
    turned()

    grad_came, mixed, lses = [], [], []
    at_once = max(nm // 2, 1)
    while len(mixed) < nm or len(grad_came) < micro or not all(
        name in halves or flow.whole(name) for name in last
    ):
        turn()
        flow.launch()
        if len(grad_came) < micro:
            grad_came.append(send(grad_parts, len(grad_came)))
        core_halves(2, last)
        for k in range(len(mixed), min(len(mixed) + at_once, nm)):
            part, lse = attend(query, kvs, bias, k * per_k, per_k)
            mixed.append(part)
            lses.append(lse)
        mixed, query, halves, grad_parts, grad_came, feeds = flow.land(
            mixed, query, halves, grad_parts, grad_came, feeds
        )
        turned()
    core_halves(len(last), last)
    middle, normed_two = middle_norm(x, mixed, qo, 1, gains[1:], biases[1:])
    grad = jnp.concatenate(grad_came)
    middle, normed_two, halves, grad = flow.land(middle, normed_two, halves, grad)
    for name in last:
        weights += [halves[name], flow.kept.pop(name)]

    result, active, slope = feed(normed_two, middle, index, firsts, sizes, weights)
    out_chunks = result.reshape((micro, chunk, width))
    output = []

    sums = Scatter(nd, nm, flow.bits)
    output = [send_chunk(out_chunks, 0)]
    over_dp = functools.partial(lax.psum_scatter, axis_name="dp", scatter_dimension=0, tiled=True)
    place = jnp.append(index, mp.astype(jnp.int32))
    grads_down = over_dp(wide_grad(grad, active, place, False))
    hid, attn, sums_two = feed_back(
        grad, slope, middle, gains[1:], index, firsts, sizes, weights
    )
    hid, attn, sums_two, normed_two, output, out_chunks = sums.land(
        hid, attn, sums_two, normed_two, output, out_chunks
    )
    grads_up = over_dp(wide_grad(normed_two, hid, place, True))[0]
    grads_up = lax.psum_scatter(grads_up, "mp", scatter_dimension=0, tiled=True)
    grad_mixed = project(attn, qo, 1, 1)

    dqs, dkvs = {}, {}
    bias_tall = bias[:, :, None]
    closing = list(range(nm))
    dkv_part, dkv_came = {}, {}

    def head_grads():
        if not closing or closing[-1] not in dkv_came:
            return None
        k = closing.pop()
        dkvs[k], keep, give = head_grad(
            normed, attn, mixed[k], dqs[k], dkv_part[k], dkv_came[k], chips
        )
        return k, (keep, give)

    def add_heads(ready, outs):
        sums.add("head", [ready[0]], outs[0], outs[1], None)

    def exchange(parts):
        parts = dict(enumerate(parts))
        came = None
        for bit in rank_bits[::-1]:
            if came is not None:
                parts = {j: add_low(part, came[j]) for j, part in parts.items()}
            came = {j ^ bit: swap_rank(parts.pop(j), bit) for j in list(parts) if j & bit}
        return parts[0], came[0]

    parts = None
    for k in list(reversed(range(nm))) + [-1]:
        if k == 1:
            sums.add_line("down", grads_down[0], rings=False)
        sums.launch(direct=1 if k < 0 else 0, z=nm - 1)
        while k >= 0 and len(output) < min(micro, nm - k + 1):
            output.append(send_chunk(out_chunks, len(output)))
        ready = head_grads()
        if parts is not None:
            dkv_part[k + 1], dkv_came[k + 1] = exchange(parts)
            parts = None
        if k >= 0:
            dqs[k], *parts = attend_back(
                query, kvs, bias_tall, lses[k], mixed[k], grad_mixed, k * per_k, per_k
            )
        live = (ready and ready[1], dqs, parts, query, dkv_part, dkv_came, dkvs, attn)
        live = sums.land(*live, output)
        outs, dqs, parts, query, dkv_part, dkv_came, dkvs, attn, output = live
        if ready:
            add_heads(ready, outs)

    sums.launch()
    ready = head_grads()

    def first_part(part):
        return first_back(
            x,
            attn,
            gains[:1],
            [dqs[k] for k in range(nm)],
            [dkvs[k] if k else dkv_part[k] for k in range(nm)],
            dkv_came[0],
            qo,
            kv,
            part,
            chunk,
        )

    firsts_back = [first_part(0)]
    firsts_back, outs, output, attn = sums.land(firsts_back, ready and ready[1], output, attn)
    if ready:
        add_heads(ready, outs)
    hops = [lambda value, bit=1 << b: swap(value, bit, nd) for b in range(nd.bit_length() - 1)]
    grad_tokens, vectors = [], None
    while sums.busy() or hops or len(grad_tokens) < micro:
        if len(grad_tokens) < micro:
            first = firsts_back[len(grad_tokens)][0]
            grad_tokens.append(lax.ppermute(first, ("dp", "mp"), back_routes(len(grad_tokens))))
            if len(grad_tokens) == micro:
                output = unpack(output)
        sums.launch()
        if len(firsts_back) < micro:
            firsts_back.append(first_part(len(firsts_back)))
        elif hops:
            vectors = jnp.concatenate([sum(part[1] for part in firsts_back), sums_two])
            vectors = jnp.take(
                vectors.reshape(4, nd, width // nd), jnp.argsort(index), axis=1
            ).reshape(4, width)
            for hop in hops:
                vectors = vectors + hop(vectors)
            hops = []
        grad_tokens, firsts_back, vectors, output, attn = sums.land(
            grad_tokens, firsts_back, vectors, output, attn
        )
    g_head, g_down = sums.done["head"], sums.done["down"]
    vectors = sum([ring(vectors, k, nm) for k in range(1, nm)], vectors)
    share = width // (nd * nm)
    vectors = lax.dynamic_slice_in_dim(vectors, (dp * nm + mp) * share, share, 1)
    return (
        output[:, None],
        unpack(grad_tokens)[:, None],
        jnp.concatenate([g_head[:1], g_head[2:]])[None],
        g_head[1][None],
        grads_up.astype(F32),
        g_down[None],
        jnp.stack([vectors[0], vectors[2]])[None],
        vectors[1][None],
        vectors[3][None],
    )


def solution(mesh):
    placed = (
        P(None, "dp", "mp", None),
        P(None, "dp"),
        P(),
        P(),
        P(None, None, "dp", "mp"),
        P(None, "dp", "mp"),
        P(None, "dp", "mp"),
        P(None, "dp", "mp"),
        P(None, "dp", "mp", None),
    )
    return jax.shard_map(
        functools.partial(shards, mesh.shape["dp"], mesh.shape["mp"]),
        mesh=mesh,
        in_specs=placed,
        out_specs=(
            P(None, "dp", "mp", None),
            P(None, "dp", "mp", None),
            P(None, None, "dp", "mp"),
            P(None, "dp", "mp"),
            P(None, "dp", "mp"),
            P(None, "dp", "mp"),
            P(None, None, ("dp", "mp")),
            P(None, ("dp", "mp")),
            P(None, ("dp", "mp")),
        ),
        check_vma=False,
    )
```
